32 devices in a mesh: dp: 16 (over z, y, x), tensor: 2 (over core).
Axes of the slice: x: 2, y: 2, z: 4, core: 2. Of those that a mesh axis runs over, the one named last changes fastest.
Arguments:
- tokens: float32 [16384, 768], P(('dp', 'tensor')), may hold values from -6 to 6
- offsets: int32 [16, 16], P('dp'), may hold values from 0 to 1024, as said below
- w_qkv: bfloat16 [768, 3, 768], P('dp', None, 'tensor'), may hold values from -0.21875 to 0.21875
- w_attn_out: bfloat16 [768, 768], P('tensor', 'dp'), may hold values from -1.75 to 1.75
- w_in: bfloat16 [768, 2, 1152], P('dp', None, 'tensor'), may hold values from -0.21875 to 0.21875
- w_mlp_out: bfloat16 [1152, 768], P('tensor', 'dp'), may hold values from -0.1875 to 0.1875
- gain_attn: bfloat16 [768], P('dp'), may hold values from 0.099609375 to 1.8984375
- gain_mlp: bfloat16 [768], P('dp'), may hold values from 0.099609375 to 1.8984375
- cotangent: float32 [16384, 768], P(('dp', 'tensor')), may hold values from -6 to 6
Outputs:
- outputs: float32 [16384, 768], P(('dp', 'tensor'))
- grad_tokens: float32 [16384, 768], P(('dp', 'tensor'))
- grad_w_qkv: float32 [768, 3, 768], P('dp', None, 'tensor')
- grad_w_attn_out: float32 [768, 768], P('tensor', 'dp')
- grad_w_in: float32 [768, 2, 1152], P('dp', None, 'tensor')
- grad_w_mlp_out: float32 [1152, 768], P('tensor', 'dp')
- grad_gain_attn: float32 [768], P('dp')
- grad_gain_mlp: float32 [768], P('dp')
The draws below stay inside these ranges and needn't reach their ends.
Inputs may be any that keep to these rules, and one draw needn't show every extreme that they name: `offsets`: each row holds the first tokens of 16 sequences of one group of 1024 tokens, rising from 0 and never falling (equal entries are empty sequences); a sequence ends where the next begins, the last at 1024. No sequence has more than 512 tokens; in every row one has exactly 512 and holds the group's tokens 512 - 1 and 512.
All inputs are finite; a program needn't handle non-finite values.
Results may differ from the reference program's by a relative error of at most 0.018.
Values may be sent and summed in bfloat16 or wider, within the bound.
A program may use at most 128 MiB of HBM per device.

```python
import math
import jax
import jax.numpy as jnp
from jax import lax

D = 768
HEADS = 12
HEAD_DIM = 64
FF = 1152
SEQ_SLOTS = 16
GROUP = 1024
SEQ_MAX = 512
GROUPS = 16
TOKENS = 16384


def draw_offsets(key, part):
    key_start, key_left, key_right = jax.random.split(key, 3)
    left_count = (SEQ_SLOTS - 3) // 2
    right_count = SEQ_SLOTS - 3 - left_count
    long_start = jax.random.randint(key_start, (GROUPS, 1), 1, SEQ_MAX).astype(jnp.int32)
    left_cuts = jax.random.randint(key_left, (GROUPS, left_count), 0, 1 << 20).astype(jnp.int32) % (long_start + 1)
    right_raw = jax.random.randint(key_right, (GROUPS, right_count), 0, 1 << 20).astype(jnp.int32)
    right_cuts = long_start + SEQ_MAX + right_raw % (SEQ_MAX - long_start + 1)
    zeros_col = jnp.zeros((GROUPS, 1), jnp.int32)
    return jnp.concatenate([zeros_col, jnp.sort(left_cuts, axis=1), long_start, long_start + SEQ_MAX, jnp.sort(right_cuts, axis=1)], axis=1).astype(jnp.int32)


def raised(entries, own_key, source, target, shards_of, factor):
    owner, partner = [(jnp.arange(entries.shape[dim]) // (entries.shape[dim] // shards_of)).reshape([-1 if axis == dim else 1 for axis in range(entries.ndim)]) for dim in (source, target)]
    chosen = jax.random.permutation(own_key, shards_of)[partner]
    strong = (owner == chosen) | (owner == (partner + shards_of // 2) % shards_of)
    return jnp.where(strong, factor * entries, entries)


def block_levels(own_key, dims, shards, low, largest):
    def one(dim, parts):
        heights = jax.random.uniform(jax.random.fold_in(jax.random.fold_in(own_key, 6), dim), (parts,), jnp.float32, low / len(shards), largest / len(shards))
        return jnp.repeat(jnp.exp(heights), dims[dim] // parts).reshape((-1,) + (1,) * (len(dims) - dim - 1))

    level = one(*shards[0])
    for cut in shards[1:]:
        level = level * one(*cut)
    return level


def noise(rng, extent, scale, bound, pieces=(), kind=jnp.bfloat16):
    entries = scale * jax.random.normal(rng, extent, jnp.float32)
    if pieces:
        entries = entries * block_levels(rng, extent, pieces, -0.22, 0.18)
    return jnp.clip(entries, -bound, bound).astype(kind)


def bell_draw_with(rng, extent, deviation, limit, cuts, heavy, kind=jnp.bfloat16):
    result = deviation * jax.random.normal(rng, extent, jnp.float32)
    if cuts:
        result = result * block_levels(rng, extent, cuts, -0.22, 0.18)
    return jnp.clip(raised(result, jax.random.fold_in(rng, 3), *heavy), -limit, limit).astype(kind)


def setup_inputs(seed: int = 0) -> dict:
    keys = jax.random.split(jax.random.key(seed), 10)
    tokens = bell_draw_with(keys[0], (TOKENS, D), 1.0, 6.0, ((0, 32),), (0, 1, 32, 2.75), jnp.float32)
    offsets = draw_offsets(jax.random.fold_in(keys[9], 71), 0)
    w_qkv = noise(keys[2], (D, 3, D), D ** -0.5, 0.21875, ((0, 16), (2, 2)))
    w_attn_out = noise(keys[3], (D, D), (D // 64) ** -0.5, 1.75, ((0, 2), (1, 16)))
    w_in = noise(keys[4], (D, 2, FF), D ** -0.5, 0.21875, ((0, 16), (2, 2)))
    w_mlp_out = noise(keys[5], (FF, D), FF ** -0.5, 0.1875, ((0, 2), (1, 16)))
    gain_attn = jnp.clip(1.0 + 0.18 * jax.random.normal(keys[6], (D,), jnp.float32), 0.099609375, 1.8984375).astype(jnp.bfloat16)
    gain_mlp = jnp.clip(1.0 + 0.18 * jax.random.normal(keys[7], (D,), jnp.float32), 0.099609375, 1.8984375).astype(jnp.bfloat16)
    cotangent = bell_draw_with(keys[8], (TOKENS, D), 1.0, 6.0, ((0, 32),), (0, 1, 32, 2.75), jnp.float32)
    return dict(tokens=tokens, offsets=offsets, w_qkv=w_qkv, w_attn_out=w_attn_out, w_in=w_in, w_mlp_out=w_mlp_out, gain_attn=gain_attn, gain_mlp=gain_mlp, cotangent=cotangent)


EPSILON = 1e-05
ROPE_BASE = 160000.0
NEGATIVE = -1e+30

@jax.custom_vjp
def low(v):
    return lax.optimization_barrier(v.astype(jnp.bfloat16)).astype(jnp.float32)

@jax.custom_vjp
def low_back(v):
    return v

def low_keep(v):
    return (low(v), None)

def low_pass(kept, grad):
    return (grad,)

def back_keep(v):
    return (v, None)

def back_low(kept, grad):
    return (low(grad),)
low.defvjp(low_keep, low_pass)
low_back.defvjp(back_keep, back_low)

def seq_starts(offset_row, count_rows):
    position = jnp.arange(count_rows, dtype=jnp.int32)
    before = offset_row[None, :] <= position[:, None]
    return lax.optimization_barrier(jnp.max(jnp.where(before, offset_row[None, :], 0), axis=1)).astype(jnp.int32)

def rope_tables(starts):
    count_rows = starts.shape[0]
    position = jnp.arange(count_rows, dtype=jnp.int32) - starts
    half_dim = HEAD_DIM // 2
    inverse = jnp.power(jnp.float32(ROPE_BASE), -2.0 * jnp.arange(half_dim, dtype=jnp.float32) / HEAD_DIM)
    angles = position.astype(jnp.float32)[:, None] * inverse[None, :]
    return (jnp.cos(angles), jnp.sin(angles))

def rotate(head_rows, cosine_tab, sine_tab):
    half_dim = HEAD_DIM // 2
    first_half = head_rows[..., :half_dim]
    second = head_rows[..., half_dim:]
    cosine_b = cosine_tab[:, None, :]
    sine_b = sine_tab[:, None, :]
    return jnp.concatenate([first_half * cosine_b - second * sine_b, second * cosine_b + first_half * sine_b], axis=-1)

def layer_norm(inputs_v, gain_v):
    centre = inputs_v - lax.optimization_barrier(jnp.mean(inputs_v, axis=-1, keepdims=True))
    spread = lax.optimization_barrier(jnp.mean(centre * centre, axis=-1, keepdims=True))
    return centre * lax.rsqrt(spread + EPSILON) * gain_v

def group_forward(tokens_grp, offset_row, w_qkv, w_attn_out, w_in, w_mlp_out, gain_attn, gain_mlp):
    highest = lax.Precision.HIGHEST
    count_rows = tokens_grp.shape[0]
    scale_factor = 1.0 / math.sqrt(HEAD_DIM)
    starts = seq_starts(offset_row, count_rows)
    cosine_tab, sine_tab = rope_tables(starts)
    normed = low(layer_norm(tokens_grp, gain_attn))
    projected = low_back(jnp.einsum('td,dsk->tsk', normed, w_qkv, precision=highest))
    split_heads = projected.reshape(count_rows, 3, HEADS, HEAD_DIM)
    queries = low(rotate(split_heads[:, 0], cosine_tab, sine_tab))
    key_rows = low(rotate(split_heads[:, 1], cosine_tab, sine_tab))
    values = low(split_heads[:, 2])
    scores = low_back(jnp.einsum('qhe,khe->hqk', queries, key_rows, precision=highest) * scale_factor)
    same_seq = starts[:, None] == starts[None, :]
    weights_low = low(jax.nn.softmax(jnp.where(same_seq[None], scores, NEGATIVE), axis=-1))
    mixed_out = jnp.einsum('hqk,khe->qhe', weights_low, values, precision=highest)
    context = low_back(low(mixed_out.reshape(count_rows, HEADS * HEAD_DIM)))
    attended = low_back(jnp.dot(context, w_attn_out, precision=highest))
    hidden = tokens_grp + attended
    normed_mlp = low(layer_norm(hidden, gain_mlp))
    gate_up = low_back(jnp.einsum('td,dsf->tsf', normed_mlp, w_in, precision=highest))
    product = low(jax.nn.gelu(gate_up[:, 0], approximate=False) * gate_up[:, 1])
    branch = low_back(jnp.dot(product, w_mlp_out, precision=highest))
    return hidden + branch

def reference(tokens, offsets, w_qkv, w_attn_out, w_in, w_mlp_out, gain_attn, gain_mlp, cotangent):
    params = (w_qkv.astype(jnp.float32), w_attn_out.astype(jnp.float32), w_in.astype(jnp.float32), w_mlp_out.astype(jnp.float32), gain_attn.astype(jnp.float32), gain_mlp.astype(jnp.float32))
    grouped = tokens.reshape(GROUPS, GROUP, D)

    def forward(grouped_in, params_in):

        def one_group(group_pair):
            return group_forward(group_pair[0], group_pair[1], *params_in)
        return lax.map(jax.checkpoint(one_group), (grouped_in, offsets))
    outputs, pullback = jax.vjp(forward, grouped, params)
    grad_tokens, grad_params = pullback(cotangent.reshape(GROUPS, GROUP, D))
    return (outputs.reshape(TOKENS, D), grad_tokens.reshape(TOKENS, D), grad_params[0], grad_params[1], grad_params[2], grad_params[3], grad_params[4], grad_params[5])
```

```python
import functools
import math
import types

import jax
import jax.numpy as jnp
from jax import lax
from jax.experimental import pallas as pl
from jax.experimental.pallas import tpu as pltpu
from jax.sharding import PartitionSpec as P

HEAD_DIM = 64


EPSILON = 1e-05
ROPE_BASE = 160000.0
NEGATIVE = -1e30
LANES = 128
QUERY_BLOCK = 256
SCALE = 1.0 / math.sqrt(HEAD_DIM)
VMEM_LIMIT = 48 * 1024 * 1024


def seq_starts(offset_row, position):
    before = offset_row[None, :] <= position[:, None]
    return jnp.max(jnp.where(before, offset_row[None, :], 0), axis=1)


def rope_tables(position):
    half_dim = HEAD_DIM // 2
    inverse = jnp.power(
        jnp.float32(ROPE_BASE), -2.0 * jnp.arange(half_dim, dtype=jnp.float32) / HEAD_DIM
    )
    angles = position.astype(jnp.float32)[:, None] * inverse[None, :]
    copies = LANES // half_dim
    cosine = jnp.cos(angles)
    sine = jnp.sin(angles)
    return (
        jnp.concatenate([cosine] * copies, axis=1),
        jnp.concatenate([-sine, sine] * (copies // 2), axis=1),
    )


def levels_of(count):
    out = []
    stride = 1
    while stride < count:
        size = min(4, count // stride)
        out.append((stride, size))
        stride *= size
    return out


def swap_pairs(count, mask):
    return [(place, place ^ mask) for place in range(count)]


def send_step(held, stride, size):
    count = lax.axis_size("dp")
    return [held] + [
        lax.ppermute(held, "dp", swap_pairs(count, step * stride)) for step in range(1, size)
    ]


def place_step(taken, stride, size):
    mine = (lax.axis_index("dp") // stride) % size
    outer, height, width = taken[0].shape
    spread = jnp.zeros((outer, size, height, width), taken[0].dtype)
    for step in range(size):
        spread = lax.dynamic_update_slice(spread, taken[step][:, None], (0, mine ^ step, 0, 0))
    return spread.reshape(outer * size, height, width)


def after(later, *earlier):
    return lax.optimization_barrier((later, *earlier))[0]


def gather_both(first, second):
    one, two = first[None], second[None]
    taken = None
    for level in reversed(levels_of(lax.axis_size("dp"))):
        if taken is not None:
            two = place_step(taken, *last)
        one = place_step(send_step(one, *level), *level)
        taken = send_step(after(two, one), *level)
        last = level
    return one.reshape(-1, one.shape[2]), (taken, last)


def gather_rest(pending, *earlier):
    taken, level = pending
    taken = lax.optimization_barrier((taken, *earlier))[0]
    full = place_step(taken, *level)
    return full.reshape(-1, full.shape[2])


def sum_blocks(terms, *earlier):
    count = lax.axis_size("dp")
    me = lax.axis_index("dp")
    height = terms.shape[0] // count
    width = terms.shape[1]
    held = terms
    for stride, size in levels_of(count):
        mine = (me // stride) % size
        parts = held.reshape(-1, size, height, width)
        pick = lambda place: lax.dynamic_index_in_dim(parts, place, 1, keepdims=False)
        got = [
            lax.ppermute(pick(mine ^ step), "dp", swap_pairs(count, step * stride))
            for step in range(1, size)
        ]
        if earlier:
            got = lax.optimization_barrier((got, *earlier))[0]
            earlier = ()
        total = pick(mine).astype(jnp.float32)
        for other in got:
            total = total + other.astype(jnp.float32)
        held = total.astype(jnp.bfloat16)
    return total.reshape(height, width)


def other_half(local_rows):
    return lax.ppermute(local_rows, "tensor", [(0, 1), (1, 0)])


def spread_rows(local_rows):
    return jnp.concatenate([local_rows, other_half(local_rows)], axis=0)


def collect_own(partial_sums, rows_here):
    sent = other_half(partial_sums[rows_here:].astype(jnp.bfloat16))
    return partial_sums[:rows_here] + sent.astype(jnp.float32)


def collect_all(partial_sums, rows_here):
    got = other_half(partial_sums.astype(jnp.bfloat16))
    swapped = jnp.concatenate([got[rows_here:], got[:rows_here]], axis=0)
    return partial_sums + swapped.astype(jnp.float32)


def norm_parts(inputs_v):
    centre = inputs_v - jnp.mean(inputs_v, axis=-1, keepdims=True)
    spread = jnp.mean(centre * centre, axis=-1, keepdims=True)
    scale_v = lax.rsqrt(spread + EPSILON)
    return centre * scale_v, scale_v


def norm_backward(incoming, gain_v, unit, scale_v):
    scaled = incoming * gain_v
    mean_one = jnp.mean(scaled, axis=-1, keepdims=True)
    mean_two = jnp.mean(scaled * unit, axis=-1, keepdims=True)
    return scale_v * (scaled - mean_one - unit * mean_two)


def two_terms(column):
    high = column.astype(jnp.bfloat16)
    rest = (column - lax.reduce_precision(column, 8, 7)).astype(jnp.bfloat16)
    return jnp.stack([high, rest], axis=1)


def padded(pieces):
    width = sum(piece.shape[1] for piece in pieces)
    short = -width % 128
    height = pieces[0].shape[0]
    if short:
        pieces = pieces + [jnp.zeros((height, short), jnp.bfloat16)]
    return jnp.concatenate(pieces, axis=1)


def dot_nn(left, right):
    return jnp.dot(left, right, preferred_element_type=jnp.float32)


def dot_nt(left, right):
    return lax.dot_general(
        left, right, (((1,), (1,)), ((), ())), preferred_element_type=jnp.float32
    )


def dot_tn(left, right):
    return lax.dot_general(
        left, right, (((0,), (0,)), ((), ())), preferred_element_type=jnp.float32
    )


def turn(rows, cosine, sine_signed, lane):
    half_dim = HEAD_DIM // 2
    ahead = pltpu.roll(rows, rows.shape[1] - half_dim, axis=1)
    behind = pltpu.roll(rows, half_dim, axis=1)
    swapped = jnp.where(lane % HEAD_DIM < half_dim, ahead, behind)
    return rows * cosine + swapped * sine_signed


def forward_kernel(
    normed_ref, wq_ref, wk_ref, wv_ref, cos_ref, sin_ref, srow_ref, scol_ref,
    q_ref, k_ref, v_ref, ctx_ref, lse_ref, vt_ref,
):
    rows = normed_ref.shape[0]
    block = min(QUERY_BLOCK, rows)
    normed = normed_ref[...]
    cosine = cos_ref[...]
    sine = sin_ref[...]
    lane = lax.broadcasted_iota(jnp.int32, (rows, LANES), 1)
    dot = functools.partial(jnp.dot, preferred_element_type=jnp.float32)
    q_ref[...] = turn(dot(normed, wq_ref[...]), cosine, sine, lane).astype(jnp.bfloat16)
    k_ref[...] = turn(dot(normed, wk_ref[...]), cosine, sine, lane).astype(jnp.bfloat16)
    values = dot(normed, wv_ref[...])
    v_ref[...] = values.astype(jnp.bfloat16)
    vt_ref[...] = values.T.astype(jnp.bfloat16)

    @pl.loop(0, rows // block)
    def _(step):
        at = pl.ds(pl.multiple_of(step * block, block), block)
        same = scol_ref[...] == srow_ref[:, at]
        parts = []
        for head in range(LANES // HEAD_DIM):
            cols = slice(head * HEAD_DIM, (head + 1) * HEAD_DIM)
            scores = dot_nt(k_ref[:, cols], q_ref[at, cols]) * SCALE
            scores = jnp.where(same, scores, NEGATIVE)
            top = jnp.max(scores, axis=0, keepdims=True)
            terms = jnp.exp(scores - top)
            total = jnp.sum(terms, axis=0, keepdims=True)
            weights = (terms * (1.0 / total)).astype(jnp.bfloat16)
            parts.append(dot(vt_ref[cols, :], weights))
            lse_ref[0, head : head + 1, at] = top + jnp.log(total)
        ctx_ref[at, :] = jnp.concatenate(parts, axis=0).T.astype(jnp.bfloat16)


def backward_kernel(
    grad_ref, wo_ref, q_ref, k_ref, v_ref, cos_ref, sin_ref, srow_ref, scol_ref, lse_ref,
    dq_ref, dk_ref, dv_ref, g_ref, kt_ref, acc_q, acc_k, acc_v,
):
    rows = grad_ref.shape[0]
    block = min(QUERY_BLOCK, rows)
    dot = functools.partial(jnp.dot, preferred_element_type=jnp.float32)
    g_ref[...] = dot(grad_ref[...], wo_ref[...]).astype(jnp.bfloat16)
    kt_ref[...] = k_ref[...].astype(jnp.float32).T.astype(jnp.bfloat16)
    acc_k[...] = jnp.zeros_like(acc_k)
    acc_v[...] = jnp.zeros_like(acc_v)

    @pl.loop(0, rows // block)
    def _(step):
        at = pl.ds(pl.multiple_of(step * block, block), block)
        same = scol_ref[...] == srow_ref[:, at]
        parts = []
        for head in range(LANES // HEAD_DIM):
            cols = slice(head * HEAD_DIM, (head + 1) * HEAD_DIM)
            query = q_ref[at, cols]
            grad = g_ref[at, cols]
            scores = dot_nt(k_ref[:, cols], query) * SCALE
            probs = jnp.exp(jnp.where(same, scores - lse_ref[0, head : head + 1, at], NEGATIVE))
            acc_v[:, cols] += dot(probs.astype(jnp.bfloat16), grad)
            grad_probs = dot_nt(v_ref[:, cols], grad)
            weighted = probs * grad_probs
            drop = jnp.sum(weighted, axis=0, keepdims=True)
            grad_scores = (weighted - probs * drop).astype(jnp.bfloat16)
            acc_k[:, cols] += dot(grad_scores, query)
            parts.append(dot(kt_ref[cols, :], grad_scores))
        acc_q[at, :] = jnp.concatenate(parts, axis=0).T

    cosine = cos_ref[...] * SCALE
    sine = sin_ref[...] * -SCALE
    lane = lax.broadcasted_iota(jnp.int32, (rows, LANES), 1)
    dq_ref[...] = turn(acc_q[...], cosine, sine, lane).astype(jnp.bfloat16)
    dk_ref[...] = turn(acc_k[...], cosine, sine, lane).astype(jnp.bfloat16)
    dv_ref[...] = acc_v[...].astype(jnp.bfloat16)


def whole(shape):
    return pl.BlockSpec(shape, lambda pair: (0,) * len(shape))


def column_block(rows, first):
    return pl.BlockSpec((rows, LANES), lambda pair: (0, first + pair))


def attention_forward(normed_all, attn_pack, cosine, sine, starts, width_here):
    rows, width = normed_all.shape
    pairs = width_here // LANES
    heads_each = LANES // HEAD_DIM
    low = jax.ShapeDtypeStruct((rows, width_here), jnp.bfloat16)
    return pl.pallas_call(
        forward_kernel,
        grid=(pairs,),
        out_shape=(low, low, low, low, jax.ShapeDtypeStruct((pairs, heads_each, rows), jnp.float32)),
        in_specs=[
            whole((rows, width)),
            column_block(width, 0),
            column_block(width, pairs),
            column_block(width, 2 * pairs),
            whole((rows, LANES)),
            whole((rows, LANES)),
            whole((1, rows)),
            whole((rows, 1)),
        ],
        out_specs=[column_block(rows, 0)] * 4
        + [pl.BlockSpec((1, heads_each, rows), lambda pair: (pair, 0, 0))],
        scratch_shapes=[pltpu.VMEM((LANES, rows), jnp.bfloat16)],
        compiler_params=pltpu.CompilerParams(vmem_limit_bytes=VMEM_LIMIT),
        cost_estimate=pl.CostEstimate(
            flops=2 * rows * width * 3 * width_here + 4 * rows * rows * width_here,
            bytes_accessed=2 * (rows * width + 3 * width * width_here + 4 * rows * width_here),
            transcendentals=rows * rows * width_here // HEAD_DIM,
        ),
    )(normed_all, attn_pack, attn_pack, attn_pack, cosine, sine, starts[None, :], starts[:, None])


def attention_backward(grad_rows, attn_pack, queries, key_rows, values, cosine, sine, starts, lse):
    rows, width = grad_rows.shape
    width_here = queries.shape[1]
    pairs = width_here // LANES
    heads_each = LANES // HEAD_DIM
    low = jax.ShapeDtypeStruct((rows, width_here), jnp.bfloat16)
    return pl.pallas_call(
        backward_kernel,
        grid=(pairs,),
        out_shape=(low, low, low),
        in_specs=[
            whole((rows, width)),
            column_block(width, 0),
            column_block(rows, 0),
            column_block(rows, 0),
            column_block(rows, 0),
            whole((rows, LANES)),
            whole((rows, LANES)),
            whole((1, rows)),
            whole((rows, 1)),
            pl.BlockSpec((1, heads_each, rows), lambda pair: (pair, 0, 0)),
        ],
        out_specs=[column_block(rows, 0)] * 3,
        scratch_shapes=[
            pltpu.VMEM((rows, LANES), jnp.bfloat16),
            pltpu.VMEM((LANES, rows), jnp.bfloat16),
            pltpu.VMEM((rows, LANES), jnp.float32),
            pltpu.VMEM((rows, LANES), jnp.float32),
            pltpu.VMEM((rows, LANES), jnp.float32),
        ],
        compiler_params=pltpu.CompilerParams(vmem_limit_bytes=VMEM_LIMIT),
        cost_estimate=pl.CostEstimate(
            flops=2 * rows * width * width_here + 10 * rows * rows * width_here,
            bytes_accessed=2 * (rows * width + width * width_here + 7 * rows * width_here),
            transcendentals=rows * rows * width_here // HEAD_DIM,
        ),
    )(
        grad_rows, attn_pack, queries, key_rows, values, cosine, sine,
        starts[None, :], starts[:, None], lse,
    )


def shards(tokens, offsets, w_qkv, w_attn_out, w_in, w_mlp_out, gain_attn, gain_mlp, cotangent):
    rows_here = tokens.shape[0]
    group_rows = rows_here * lax.axis_size("tensor")
    model_here = w_qkv.shape[0]
    width_here = w_qkv.shape[2]
    hidden_here = w_in.shape[2]
    half_at = lax.axis_index("tensor") * rows_here
    position = (jnp.arange(group_rows, dtype=jnp.int32) + half_at) % group_rows
    starts = seq_starts(offsets[0], position)
    cosine_tab, sine_tab = rope_tables(position - starts)

    attn_pack, pending = gather_both(
        padded([w_qkv.reshape(model_here, 3 * width_here), gain_attn[:, None]]),
        padded(
            [w_attn_out.T, w_in.reshape(model_here, 2 * hidden_here), w_mlp_out.T, gain_mlp[:, None]]
        ),
    )
    gain_one = attn_pack[:, 3 * width_here].astype(jnp.float32)
    qkv_full = attn_pack[:, : 3 * width_here]

    token_rows = spread_rows(tokens)
    cotangent_rows = spread_rows(cotangent)
    grad_rows = cotangent_rows.astype(jnp.bfloat16)
    unit_one, scale_one = norm_parts(token_rows)
    normed_all = (unit_one * gain_one).astype(jnp.bfloat16)
    queries, key_rows, values, context, lse = attention_forward(
        normed_all, attn_pack, cosine_tab, sine_tab, starts, width_here
    )

    rest_pack = gather_rest(pending, lse)
    mlp_at = width_here
    mlp_end = width_here + 2 * hidden_here
    attn_out_full = rest_pack[:, :width_here]
    mlp_in_full = rest_pack[:, mlp_at:mlp_end]
    mlp_out_full = rest_pack[:, mlp_end : mlp_end + hidden_here]
    gain_two = rest_pack[:, mlp_end + hidden_here].astype(jnp.float32)
    attended = collect_all(dot_nt(context, attn_out_full), rows_here)
    hidden = token_rows + attended
    unit_two, scale_two = norm_parts(hidden)
    mlp_rows = (unit_two * gain_two).astype(jnp.bfloat16)
    gate_part = dot_nn(mlp_rows, mlp_in_full[:, :hidden_here])
    up_part = dot_nn(mlp_rows, mlp_in_full[:, hidden_here:])
    grad_product = dot_nn(grad_rows, mlp_out_full)
    bell = 0.5 * (1.0 + lax.erf(gate_part * math.sqrt(0.5)))
    activated = gate_part * bell
    slope = bell + gate_part * jnp.exp(-0.5 * gate_part * gate_part) * (1.0 / math.sqrt(2 * math.pi))
    product_rows = (activated * up_part).astype(jnp.bfloat16)
    grad_gate_up = jnp.concatenate(
        [
            (grad_product * up_part * slope).astype(jnp.bfloat16),
            (grad_product * activated).astype(jnp.bfloat16),
        ],
        axis=1,
    )
    grad_normed_two = collect_all(dot_nt(grad_gate_up, mlp_in_full), rows_here)
    grad_hidden = cotangent_rows + norm_backward(grad_normed_two, gain_two, unit_two, scale_two)
    grad_gain_two = jnp.sum((grad_normed_two * unit_two)[:rows_here], axis=0)
    grad_hidden_rows = grad_hidden.astype(jnp.bfloat16)
    grads_three = attention_backward(
        grad_hidden_rows, rest_pack, queries, key_rows, values,
        cosine_tab, sine_tab, starts, lse,
    )
    mlp_terms = padded(
        [
            dot_tn(mlp_rows, grad_gate_up).astype(jnp.bfloat16),
            dot_tn(grad_rows, product_rows).astype(jnp.bfloat16),
            two_terms(grad_gain_two),
        ]
    )
    mlp_sums = sum_blocks(mlp_terms, grads_three[0])
    branch = collect_own(dot_nt(product_rows, mlp_out_full), rows_here)
    outputs = hidden[:rows_here] + branch

    grad_projected = jnp.concatenate(grads_three, axis=1)
    grad_normed_one = collect_own(dot_nt(grad_projected, qkv_full), rows_here)
    grad_tokens = grad_hidden[:rows_here] + norm_backward(
        grad_normed_one, gain_one, unit_one[:rows_here], scale_one[:rows_here]
    )
    grad_gain_one = jnp.sum(grad_normed_one * unit_one[:rows_here], axis=0)
    attn_terms = padded(
        [
            dot_tn(normed_all, grad_projected).astype(jnp.bfloat16),
            dot_tn(grad_hidden_rows, context).astype(jnp.bfloat16),
            two_terms(grad_gain_one),
        ]
    )
    attn_sums = sum_blocks(attn_terms)

    gain_one_cols = attn_sums[:, 4 * width_here : 4 * width_here + 2].sum(axis=1)
    gain_two_cols = mlp_sums[:, 3 * hidden_here : 3 * hidden_here + 2].sum(axis=1)
    gains = jnp.stack([gain_one_cols, gain_two_cols])
    gains = gains + other_half(gains)
    return (
        outputs,
        grad_tokens,
        attn_sums[:, : 3 * width_here].reshape(model_here, 3, width_here),
        attn_sums[:, 3 * width_here : 4 * width_here].T,
        mlp_sums[:, : 2 * hidden_here].reshape(model_here, 2, hidden_here),
        mlp_sums[:, 2 * hidden_here : 3 * hidden_here].T,
        gains[0],
        gains[1],
    )


def fast_columns(width_here, hidden_here):
    main = hidden_here // LANES * LANES
    pairs = width_here // LANES
    at = {"gains": (0, LANES)}
    place = LANES
    for pair in range(pairs):
        at["pair%d" % pair] = (place, 3 * LANES)
        place += 3 * LANES
    for name, size in (
        ("out", width_here), ("mlp", main + LANES), ("gate", main), ("up", main), ("tail", LANES),
    ):
        at[name] = (place, size)
        place += size
    at["total"] = (0, place)
    return at


def pack_shards(w_qkv, w_attn_out, w_in, w_mlp_out, gain_attn, gain_mlp):
    height, _, width_here = w_qkv.shape
    hidden_here = w_in.shape[2]
    main = hidden_here // LANES * LANES
    pairs = width_here // LANES
    gains = jnp.concatenate(
        [gain_attn[:, None], gain_mlp[:, None], jnp.zeros((height, LANES - 2), jnp.bfloat16)], axis=1
    )
    by_pair = w_qkv.reshape(height, 3, pairs, LANES).transpose(0, 2, 1, 3)
    short = main + LANES - hidden_here
    return jnp.concatenate(
        [
            gains,
            by_pair.reshape(height, 3 * width_here),
            w_attn_out.T,
            w_mlp_out.T,
            jnp.zeros((height, short), jnp.bfloat16),
            w_in[:, 0, :main],
            w_in[:, 1, :main],
            w_in[:, 0, main:],
            w_in[:, 1, main:],
        ],
        axis=1,
    )


class Links:
    def __init__(self, ref):
        self.ref = ref
        self.dp = lax.axis_index("dp")
        self.core = lax.axis_index("tensor")
        self.x = self.dp % 2
        self.y = (self.dp // 2) % 2
        self.z = self.dp // 4
        plane = self.dp % 4
        self.x_side = self.dp + 1 - 2 * self.x
        self.y_side = self.dp + 2 - 4 * self.y
        self.z_of = [None, self.z + 1 - 2 * (self.z % 2), (self.z + 2) % 4, 3 - self.z]
        self.z_side = [None] + [place * 4 + plane for place in self.z_of[1:]]
        self.started = []

    def enter(self):
        barrier = pltpu.get_barrier_semaphore()
        others = [(self.x_side, self.core), (self.y_side, self.core), (self.dp, 1 - self.core)]
        others += [(place, self.core) for place in self.z_side[1:]]
        for other in others:
            pl.semaphore_signal(
                barrier, inc=1, device_id=other, device_id_type=pl.DeviceIdType.MESH
            )
        pl.semaphore_wait(barrier, len(others))

    def copy(self, source, target, sems, place, device):
        return pltpu.make_async_remote_copy(
            src_ref=source,
            dst_ref=target,
            send_sem=sems[0].at[place],
            recv_sem=sems[1].at[place],
            device_id=device,
            device_id_type=pl.DeviceIdType.MESH,
        )

    def start(self, *copies):
        for copy in copies:
            copy.start()
            self.started.append(copy)

    def to_core(self, source, target, place):
        copy = self.copy(
            source, target, (self.ref.core_out, self.ref.core_in), place, (self.dp, 1 - self.core)
        )
        self.start(copy)
        return copy

    def finish(self):
        for copy in self.started:
            copy.wait_send()


class Gather(Links):
    def __init__(self, ref, chunks):
        super().__init__(ref)
        self.chunks = chunks
        self.got = {}

    def send_z(self, name):
        chunk = list(self.chunks).index(name)
        cols = pl.ds(*self.chunks[name])
        block = self.ref.full.at[self.z, self.y, self.x, :, cols]
        copies = [
            self.copy(
                block, block, (self.ref.far_out, self.ref.far_in), 3 * chunk + step - 1,
                (self.z_side[step], self.core),
            )
            for step in (1, 2, 3)
        ]
        self.start(*copies)
        self.got[name] = copies

    def arrive(self, name):
        for copy in self.got[name]:
            copy.wait_recv()

    def near(self, name, stage, first, second):
        chunk = list(self.chunks).index(name)
        sems = (self.ref.near_out, self.ref.near_in)
        place = 4 * chunk + 2 * stage
        copies = [
            self.copy(first[0], first[0], sems, place, (first[1], self.core)),
            self.copy(second[0], second[0], sems, place + 1, (second[1], self.core)),
        ]
        self.arrive(name)
        self.start(*copies)
        self.got[name] = copies

    def send_one(self, name):
        cols = pl.ds(*self.chunks[name])
        low, high = pl.ds(0, 2), pl.ds(2, 2)
        full = self.ref.full
        self.near(
            name, 0,
            (full.at[low, self.y, self.x, :, cols], self.x_side),
            (full.at[high, self.y, self.x, :, cols], self.y_side),
        )

    def send_two(self, name):
        cols = pl.ds(*self.chunks[name])
        low, high = pl.ds(0, 2), pl.ds(2, 2)
        both = pl.ds(0, 2)
        full = self.ref.full
        self.near(
            name, 1,
            (full.at[low, self.y, both, :, cols], self.y_side),
            (full.at[high, both, self.x, :, cols], self.x_side),
        )


def weights_at(full, span):
    block = full[:, :, :, :, span[0] : span[0] + span[1]]
    return block.reshape(-1, span[1])


def row_loop(rows, block):
    def wrap(body):
        @pl.loop(0, rows // block)
        def _(step):
            body(pl.ds(pl.multiple_of(step * block, block), block))

    return wrap


def front_kernel(names, spans, *refs):
    ref = types.SimpleNamespace(**dict(zip(names, refs)))
    half, width = ref.tok.shape
    rows = 2 * half
    pairs = (spans["out"][1]) // LANES
    main = spans["gate"][1]
    chunk_names = ["gains"] + ["pair%d" % pair for pair in range(pairs)] + ["out", "mlp"]
    chunks = {name: spans[name] for name in chunk_names}
    chunks["gate"] = spans["gate"]
    chunks["up"] = (spans["up"][0], main + LANES)
    link = Gather(ref, chunks)
    core = link.core
    own = pl.ds(pl.multiple_of(core * half, half), half)
    own_at = core * half
    other_at = (1 - core) * half
    part = 256

    link.enter()
    ref.full[link.z, link.y, link.x] = ref.pack[...]
    link.send_z("gains")
    link.send_z("pair0")
    link.send_z("pair1")

    @row_loop(half, 128)
    def _(at):
        unit, scale = norm_parts(ref.tok[at, :])
        ref.unit_one[at, :] = unit
        ref.scale_one[at, :] = jnp.broadcast_to(scale, (128, LANES))
        here = pl.ds(pl.multiple_of(own_at + at.start, 128), 128)
        ref.grad_rows[here, :] = ref.cot[at, :].astype(jnp.bfloat16)

    got_grad = link.to_core(ref.grad_rows.at[own, :], ref.grad_rows.at[own, :], 0)
    link.send_one("gains")

    shift = jnp.int32(0)
    for slot in range(ref.offsets.shape[1]):
        entry = ref.offsets[0, slot]
        shift = jnp.maximum(shift, jnp.where(entry <= half - 1, entry, 0))

    def source_of(place):
        moved = place + shift
        return jnp.where(moved >= rows, moved - rows, moved)

    def start_of(place):
        start = jnp.zeros_like(place)
        for slot in range(ref.offsets.shape[1]):
            entry = ref.offsets[0, slot]
            start = jnp.maximum(start, jnp.where(place >= entry, entry, 0))
        return start

    @row_loop(rows, part)
    def _(at):
        place = source_of(lax.broadcasted_iota(jnp.int32, (part, LANES), 0) + at.start)
        start = start_of(place)
        angle = (place - start).astype(jnp.float32) * ref.inverse[...]
        lane = lax.broadcasted_iota(jnp.int32, (part, LANES), 1)
        sine = jnp.sin(angle)
        ref.cosine[at, :] = jnp.cos(angle)
        ref.sine[at, :] = jnp.where(lane % HEAD_DIM < HEAD_DIM // 2, -sine, sine)

    link.send_two("gains")
    link.send_z("pair2")
    key_start = start_of(source_of(lax.broadcasted_iota(jnp.int32, (half, 1), 0) + half))
    query_start = start_of(source_of(lax.broadcasted_iota(jnp.int32, (1, half), 1) + half))
    ref.bias[...] = jnp.where(key_start == query_start, 0.0, NEGATIVE)

    @row_loop(rows, part)
    def _(at):
        down = lax.broadcasted_iota(jnp.int32, (part, rows), 0) + at.start
        along = lax.broadcasted_iota(jnp.int32, (part, rows), 1)
        ref.perm[at, :] = jnp.where(source_of(down) == along, 1.0, 0.0).astype(jnp.bfloat16)
        ref.perm_back[at, :] = jnp.where(source_of(along) == down, 1.0, 0.0).astype(jnp.bfloat16)

    link.send_one("pair0")
    link.arrive("gains")
    slot = lax.broadcasted_iota(jnp.int32, (8, LANES), 0)
    lane = lax.broadcasted_iota(jnp.int32, (8, LANES), 1)
    pick = jnp.where(slot == lane, 1.0, 0.0).astype(jnp.bfloat16)
    ref.gain[...] = dot_nt(pick, weights_at(ref.full, spans["gains"]))

    @row_loop(half, 128)
    def _(at):
        here = pl.ds(pl.multiple_of(own_at + at.start, 128), 128)
        ref.normed[here, :] = (ref.unit_one[at, :] * ref.gain[0:1, :]).astype(jnp.bfloat16)

    got_normed = link.to_core(ref.normed.at[own, :], ref.normed.at[own, :], 1)
    link.send_one("pair1")
    link.send_two("pair0")
    link.send_z("out")
    got_normed.wait_recv()

    @row_loop(rows, part)
    def _(at):
        ref.rolled[at, :] = dot_nn(ref.perm[at, :], ref.normed[...]).astype(jnp.bfloat16)

    link.send_one("pair2")
    link.send_two("pair1")
    link.send_z("mlp")

    def project(pair):
        link.arrive("pair%d" % pair)
        cols = slice(pair * LANES, (pair + 1) * LANES)

        @row_loop(rows, part)
        def _(at):
            three = dot_nn(ref.rolled[at, :], weights_at(ref.full, spans["pair%d" % pair]))
            lane = lax.broadcasted_iota(jnp.int32, (part, LANES), 1)
            cosine, sine = ref.cosine[at, :], ref.sine[at, :]
            query = turn(three[:, :LANES], cosine, sine, lane) * SCALE
            ref.queries[at, cols] = query.astype(jnp.bfloat16)
            ref.keys[at, cols] = turn(
                three[:, LANES : 2 * LANES], cosine, sine, lane
            ).astype(jnp.bfloat16)
            ref.values[at, cols] = three[:, 2 * LANES :].astype(jnp.bfloat16)
            ref.values_t[:, at] = three[:, 2 * LANES :].T.astype(jnp.bfloat16)

    def attend(pair, first):
        cols = slice(pair * LANES, (pair + 1) * LANES)
        base = 0 if first else half

        @pl.loop(0, half // part)
        def _(step):
            at = pl.ds(pl.multiple_of(base + step * part, part), part)
            query_pair = ref.queries[at, cols]
            lane = lax.broadcasted_iota(jnp.int32, (part, LANES), 1)
            parts = []
            for head in range(LANES // HEAD_DIM):
                query = jnp.where(lane // HEAD_DIM == head, query_pair, 0)
                scores = dot_nt(ref.keys[base : base + half, cols], query)
                if not first:
                    scores = scores + ref.bias[:, pl.ds(pl.multiple_of(step * part, part), part)]
                top = jnp.max(scores, axis=0, keepdims=True)
                terms = jnp.exp(scores - top)
                total = jnp.sum(terms, axis=0, keepdims=True)
                mixed = dot_nn(
                    ref.values_t[head * HEAD_DIM : (head + 1) * HEAD_DIM, base : base + half],
                    terms.astype(jnp.bfloat16),
                )
                parts.append(mixed * (1.0 / total))
                ref.lse[pair, head : head + 1, at] = top + jnp.log(total)
            ref.context_rolled[at, cols] = jnp.concatenate(parts, axis=0).T.astype(jnp.bfloat16)

    project(0)
    attend(0, True)
    link.send_one("out")
    link.send_two("pair2")
    link.send_z("gate")
    attend(0, False)
    project(1)
    attend(1, True)
    link.send_one("mlp")
    link.send_two("out")
    link.send_z("up")
    attend(1, False)
    project(2)
    attend(2, True)
    link.send_one("gate")
    link.send_two("mlp")
    attend(2, False)

    @row_loop(rows, part)
    def _(at):
        ref.context[at, :] = dot_nn(ref.perm_back[at, :], ref.context_rolled[...]).astype(jnp.bfloat16)

    link.send_one("up")
    link.send_two("gate")
    link.arrive("out")

    def pair_sum(product, place, keep):
        @row_loop(half, part)
        def _(at):
            there = pl.ds(pl.multiple_of(other_at + at.start, part), part)
            ref.sent[place, at, :] = product(there).astype(jnp.bfloat16)

        got = link.to_core(ref.sent.at[place], ref.taken.at[place], 2 + place)

        @row_loop(half, part)
        def _(at):
            here = pl.ds(pl.multiple_of(own_at + at.start, part), part)
            keep[at, :] = product(here)

        return got

    got_attended = pair_sum(
        lambda at: dot_nt(ref.context[at, :], weights_at(ref.full, spans["out"])), 0, ref.hidden
    )
    got_attended.wait_recv()

    @row_loop(half, 128)
    def _(at):
        hidden = ref.tok[at, :] + ref.hidden[at, :] + ref.taken[0, at, :].astype(jnp.float32)
        ref.hidden[at, :] = hidden
        unit, scale = norm_parts(hidden)
        ref.unit_two[at, :] = unit
        ref.scale_two[at, :] = jnp.broadcast_to(scale, (128, LANES))
        here = pl.ds(pl.multiple_of(own_at + at.start, 128), 128)
        ref.normed_mlp[here, :] = (unit * ref.gain[1:2, :]).astype(jnp.bfloat16)

    got_mlp = link.to_core(ref.normed_mlp.at[own, :], ref.normed_mlp.at[own, :], 6)
    link.send_two("up")
    got_grad.wait_recv()
    link.arrive("mlp")

    @row_loop(rows, part)
    def _(at):
        ref.grad_product[at, :] = dot_nn(ref.grad_rows[at, :], weights_at(ref.full, spans["mlp"]))

    got_mlp.wait_recv()
    link.arrive("gate")
    link.arrive("up")

    def gated(gate, up, grad):
        bell = 0.5 * (1.0 + lax.erf(gate * math.sqrt(0.5)))
        activated = gate * bell
        slope = bell + gate * jnp.exp(-0.5 * gate * gate) * (1.0 / math.sqrt(2 * math.pi))
        return activated * up, grad * up * slope, grad * activated

    @row_loop(rows, part)
    def _(at):
        low = ref.normed_mlp[at, :]
        gate = dot_nn(low, weights_at(ref.full, spans["gate"]))
        up = dot_nn(low, weights_at(ref.full, spans["up"]))
        product, grad_gate, grad_up = gated(gate, up, ref.grad_product[at, :main])
        ref.product[at, :main] = product.astype(jnp.bfloat16)
        ref.grad_gate_up[at, :main] = grad_gate.astype(jnp.bfloat16)
        ref.grad_gate_up[at, main : 2 * main] = grad_up.astype(jnp.bfloat16)
        tail = dot_nn(low, weights_at(ref.full, spans["tail"]))
        product, grad_gate, grad_up = gated(
            tail, pltpu.roll(tail, LANES // 2, axis=1), ref.grad_product[at, main:]
        )
        lane = lax.broadcasted_iota(jnp.int32, (part, LANES), 1)
        lower = lane < LANES // 2
        ref.product[at, main:] = jnp.where(lower, product, 0.0).astype(jnp.bfloat16)
        ref.grad_gate_up[at, 2 * main :] = jnp.where(
            lower, grad_gate, pltpu.roll(grad_up, LANES // 2, axis=1)
        ).astype(jnp.bfloat16)

    inner = (spans["gate"][0], 2 * main + LANES)
    got_normed_two = pair_sum(
        lambda at: dot_nt(ref.grad_gate_up[at, :], weights_at(ref.full, inner)), 1, ref.grad_hidden
    )
    got_branch = pair_sum(
        lambda at: dot_nt(ref.product[at, :], weights_at(ref.full, spans["mlp"])), 2, ref.outputs
    )
    got_normed_two.wait_recv()
    ref.gain_rows[...] = jnp.zeros_like(ref.gain_rows)

    @row_loop(half, 128)
    def _(at):
        incoming = ref.grad_hidden[at, :] + ref.taken[1, at, :].astype(jnp.float32)
        unit = ref.unit_two[at, :]
        ref.gain_rows[1:2, :] += jnp.sum(incoming * unit, axis=0, keepdims=True)
        grad = ref.cot[at, :] + norm_backward(
            incoming, ref.gain[1:2, :], unit, ref.scale_two[at, 0:1]
        )
        ref.grad_hidden[at, :] = grad
        here = pl.ds(pl.multiple_of(own_at + at.start, 128), 128)
        ref.grad_low[here, :] = grad.astype(jnp.bfloat16)

    got_low = link.to_core(ref.grad_low.at[own, :], ref.grad_low.at[own, :], 7)
    got_branch.wait_recv()

    @row_loop(half, 128)
    def _(at):
        ref.outputs[at, :] = (
            ref.outputs[at, :] + ref.hidden[at, :] + ref.taken[2, at, :].astype(jnp.float32)
        )

    got_low.wait_recv()
    ref.weights[...] = weights_at(ref.full, spans["total"])
    link.finish()


def call_front(pack, tokens, cotangent, offsets, spans):
    half, width = tokens.shape
    rows = 2 * half
    height, total = pack.shape
    width_here = spans["out"][1]
    pairs = width_here // LANES
    main = spans["gate"][1]
    half_dim = HEAD_DIM // 2
    inverse = jnp.power(
        jnp.float32(ROPE_BASE), -2.0 * jnp.arange(half_dim, dtype=jnp.float32) / HEAD_DIM
    )
    inverse = jnp.tile(inverse, LANES // half_dim)[None, :]
    low, wide = jnp.bfloat16, jnp.float32
    outs = dict(
        outputs=((half, width), wide),
        grad_hidden=((half, width), wide),
        gain_rows=((8, width), wide),
        gain=((8, width), wide),
        unit_one=((half, width), wide),
        scale_one=((half, LANES), wide),
        cosine=((rows, LANES), wide),
        sine=((rows, LANES), wide),
        lse=((pairs, LANES // HEAD_DIM, rows), wide),
        rolled=((rows, width), low),
        queries=((rows, width_here), low),
        keys=((rows, width_here), low),
        values=((rows, width_here), low),
        context=((rows, width_here), low),
        grad_rows=((rows, width), low),
        normed_mlp=((rows, width), low),
        product=((rows, main + LANES), low),
        grad_gate_up=((rows, 2 * main + LANES), low),
        grad_low=((rows, width), low),
        weights=((width, total), low),
    )
    chunk_count = 1 + pairs + 4
    scratch = dict(
        full=pltpu.VMEM((4, 2, 2, height, total), low),
        normed=pltpu.VMEM((rows, width), low),
        perm=pltpu.VMEM((rows, rows), low),
        perm_back=pltpu.VMEM((rows, rows), low),
        bias=pltpu.VMEM((half, half), wide),
        values_t=pltpu.VMEM((LANES, rows), low),
        context_rolled=pltpu.VMEM((rows, width_here), low),
        sent=pltpu.VMEM((3, half, width), low),
        taken=pltpu.VMEM((3, half, width), low),
        hidden=pltpu.VMEM((half, width), wide),
        unit_two=pltpu.VMEM((half, width), wide),
        scale_two=pltpu.VMEM((half, LANES), wide),
        grad_product=pltpu.VMEM((rows, main + LANES), wide),
        far_out=pltpu.SemaphoreType.DMA((3 * chunk_count,)),
        far_in=pltpu.SemaphoreType.DMA((3 * chunk_count,)),
        near_out=pltpu.SemaphoreType.DMA((4 * chunk_count,)),
        near_in=pltpu.SemaphoreType.DMA((4 * chunk_count,)),
        core_out=pltpu.SemaphoreType.DMA((8,)),
        core_in=pltpu.SemaphoreType.DMA((8,)),
    )
    names = ["offsets", "pack", "tok", "cot", "inverse"] + list(outs) + list(scratch)
    vmem = pl.BlockSpec(memory_space=pltpu.VMEM)
    results = pl.pallas_call(
        functools.partial(front_kernel, names, spans),
        out_shape=[jax.ShapeDtypeStruct(*entry) for entry in outs.values()],
        in_specs=[pl.BlockSpec(memory_space=pltpu.SMEM)] + [vmem] * 4,
        out_specs=[vmem] * len(outs),
        scratch_shapes=list(scratch.values()),
        compiler_params=pltpu.CompilerParams(
            collective_id=0, has_side_effects=True, vmem_limit_bytes=60 * 1024 * 1024
        ),
        cost_estimate=pl.CostEstimate(
            flops=12 * 10**9, bytes_accessed=30 * 10**6, transcendentals=10**7
        ),
    )(offsets, pack, tokens, cotangent, inverse)
    return types.SimpleNamespace(**dict(zip(outs, results)))


def fast_shards(tokens, offsets, w_qkv, w_attn_out, w_in, w_mlp_out, gain_attn, gain_mlp, cotangent):
    half = tokens.shape[0]
    rows = 2 * half
    height, _, width_here = w_qkv.shape
    hidden_here = w_in.shape[2]
    pairs = width_here // LANES
    main = hidden_here // LANES * LANES
    spans = fast_columns(width_here, hidden_here)
    pack = pack_shards(w_qkv, w_attn_out, w_in, w_mlp_out, gain_attn, gain_mlp)
    f = call_front(pack, tokens, cotangent, offsets, spans)
    core = lax.axis_index("tensor")
    shift = seq_starts(offsets[0], jnp.full((1,), half - 1, jnp.int32))[0]
    place = (jnp.arange(rows, dtype=jnp.int32) + shift) % rows
    starts = seq_starts(offsets[0], place)
    pick = lambda name: f.weights[:, spans[name][0] : spans[name][0] + spans[name][1]]
    grads_three = attention_backward(
        jnp.roll(f.grad_low, -shift, axis=0), pick("out"), f.queries * 8, f.keys, f.values,
        f.cosine, f.sine, starts, f.lse,
    )
    grad_projected = jnp.concatenate(
        [g[:, p * LANES : (p + 1) * LANES] for p in range(pairs) for g in grads_three], axis=1
    )
    at = spans["pair0"][0]
    qkv_full = f.weights[:, at : at + 3 * width_here]
    mlp_terms = padded(
        [
            dot_tn(f.normed_mlp, f.grad_gate_up).astype(jnp.bfloat16),
            dot_tn(f.grad_rows, f.product[:, :hidden_here]).astype(jnp.bfloat16),
            two_terms(f.gain_rows[1]),
        ]
    )
    mlp_sums = sum_blocks(mlp_terms)
    partial_one = dot_nt(jnp.roll(grad_projected, shift, axis=0), qkv_full)
    mine = lax.dynamic_slice_in_dim(partial_one, core * half, half, 0)
    other = lax.dynamic_slice_in_dim(partial_one, (1 - core) * half, half, 0)
    grad_normed_one = mine + other_half(other.astype(jnp.bfloat16)).astype(jnp.float32)
    grad_tokens = f.grad_hidden + norm_backward(
        grad_normed_one, f.gain[0:1], f.unit_one, f.scale_one[:, 0:1]
    )
    attn_terms = padded(
        [
            dot_tn(f.rolled, grad_projected).astype(jnp.bfloat16),
            dot_tn(f.grad_low, f.context).astype(jnp.bfloat16),
            two_terms(jnp.sum(grad_normed_one * f.unit_one, axis=0)),
        ]
    )
    attn_sums = sum_blocks(attn_terms)
    gain_one_cols = attn_sums[:, 4 * width_here : 4 * width_here + 2].sum(axis=1)
    gain_two_cols = mlp_sums[:, 3 * hidden_here : 3 * hidden_here + 2].sum(axis=1)
    gains = jnp.stack([gain_one_cols, gain_two_cols])
    gains = gains + other_half(gains)
    tail = mlp_sums[:, 2 * main : 2 * hidden_here]
    grad_in = jnp.stack(
        [
            jnp.concatenate([mlp_sums[:, :main], tail[:, : hidden_here - main]], axis=1),
            jnp.concatenate([mlp_sums[:, main : 2 * main], tail[:, hidden_here - main :]], axis=1),
        ],
        axis=1,
    )
    return (
        f.outputs,
        grad_tokens,
        attn_sums[:, : 3 * width_here]
        .reshape(height, pairs, 3, LANES)
        .transpose(0, 2, 1, 3)
        .reshape(height, 3, width_here),
        attn_sums[:, 3 * width_here : 4 * width_here].T,
        grad_in,
        mlp_sums[:, 2 * hidden_here : 3 * hidden_here].T,
        gains[0],
        gains[1],
    )


def solution(mesh):
    in_specs = (
        P(("dp", "tensor"), None),
        P("dp", None),
        P("dp", None, "tensor"),
        P("tensor", "dp"),
        P("dp", None, "tensor"),
        P("tensor", "dp"),
        P("dp"),
        P("dp"),
        P(("dp", "tensor"), None),
    )
    out_specs = (
        P(("dp", "tensor"), None),
        P(("dp", "tensor"), None),
        P("dp", None, "tensor"),
        P("tensor", "dp"),
        P("dp", None, "tensor"),
        P("tensor", "dp"),
        P("dp"),
        P("dp"),
    )
    sizes = dict(mesh.shape)
    body = fast_shards if (sizes["dp"], sizes["tensor"]) == (16, 2) else shards
    return jax.shard_map(body, mesh=mesh, in_specs=in_specs, out_specs=out_specs, check_vma=False)
```

```python
import functools
import math
import types

import jax
import jax.numpy as jnp
from jax import lax
from jax.experimental import pallas as pl
from jax.experimental.pallas import tpu as pltpu
from jax.sharding import PartitionSpec as P

HEAD_DIM = 64


EPSILON = 1e-05
ROPE_BASE = 160000.0
NEGATIVE = -1e30
LANES = 128
QUERY_BLOCK = 256
SCALE = 1.0 / math.sqrt(HEAD_DIM)
VMEM_LIMIT = 48 * 1024 * 1024


def seq_starts(offset_row, position):
    before = offset_row[None, :] <= position[:, None]
    return jnp.max(jnp.where(before, offset_row[None, :], 0), axis=1)


def rope_tables(position):
    half_dim = HEAD_DIM // 2
    inverse = jnp.power(
        jnp.float32(ROPE_BASE), -2.0 * jnp.arange(half_dim, dtype=jnp.float32) / HEAD_DIM
    )
    angles = position.astype(jnp.float32)[:, None] * inverse[None, :]
    copies = LANES // half_dim
    cosine = jnp.cos(angles)
    sine = jnp.sin(angles)
    return (
        jnp.concatenate([cosine] * copies, axis=1),
        jnp.concatenate([-sine, sine] * (copies // 2), axis=1),
    )


def levels_of(count):
    out = []
    stride = 1
    while stride < count:
        size = min(4, count // stride)
        out.append((stride, size))
        stride *= size
    return out


def swap_pairs(count, mask):
    return [(place, place ^ mask) for place in range(count)]


def send_step(held, stride, size):
    count = lax.axis_size("dp")
    return [held] + [
        lax.ppermute(held, "dp", swap_pairs(count, step * stride)) for step in range(1, size)
    ]


def place_step(taken, stride, size):
    mine = (lax.axis_index("dp") // stride) % size
    outer, height, width = taken[0].shape
    spread = jnp.zeros((outer, size, height, width), taken[0].dtype)
    for step in range(size):
        spread = lax.dynamic_update_slice(spread, taken[step][:, None], (0, mine ^ step, 0, 0))
    return spread.reshape(outer * size, height, width)


def after(later, *earlier):
    return lax.optimization_barrier((later, *earlier))[0]


def gather_both(first, second):
    one, two = first[None], second[None]
    taken = None
    for level in reversed(levels_of(lax.axis_size("dp"))):
        if taken is not None:
            two = place_step(taken, *last)
        one = place_step(send_step(one, *level), *level)
        taken = send_step(after(two, one), *level)
        last = level
    return one.reshape(-1, one.shape[2]), (taken, last)


def gather_rest(pending, *earlier):
    taken, level = pending
    taken = lax.optimization_barrier((taken, *earlier))[0]
    full = place_step(taken, *level)
    return full.reshape(-1, full.shape[2])


def sum_blocks(terms, *earlier):
    count = lax.axis_size("dp")
    me = lax.axis_index("dp")
    height = terms.shape[0] // count
    width = terms.shape[1]
    held = terms
    for stride, size in levels_of(count):
        mine = (me // stride) % size
        parts = held.reshape(-1, size, height, width)
        pick = lambda place: lax.dynamic_index_in_dim(parts, place, 1, keepdims=False)
        got = [
            lax.ppermute(pick(mine ^ step), "dp", swap_pairs(count, step * stride))
            for step in range(1, size)
        ]
        if earlier:
            got = lax.optimization_barrier((got, *earlier))[0]
            earlier = ()
        total = pick(mine).astype(jnp.float32)
        for other in got:
            total = total + other.astype(jnp.float32)
        held = total.astype(jnp.bfloat16)
    return total.reshape(height, width)


def other_half(local_rows):
    return lax.ppermute(local_rows, "tensor", [(0, 1), (1, 0)])


def spread_rows(local_rows):
    return jnp.concatenate([local_rows, other_half(local_rows)], axis=0)


def collect_own(partial_sums, rows_here):
    sent = other_half(partial_sums[rows_here:].astype(jnp.bfloat16))
    return partial_sums[:rows_here] + sent.astype(jnp.float32)


def collect_all(partial_sums, rows_here):
    got = other_half(partial_sums.astype(jnp.bfloat16))
    swapped = jnp.concatenate([got[rows_here:], got[:rows_here]], axis=0)
    return partial_sums + swapped.astype(jnp.float32)


def norm_parts(inputs_v):
    centre = inputs_v - jnp.mean(inputs_v, axis=-1, keepdims=True)
    spread = jnp.mean(centre * centre, axis=-1, keepdims=True)
    scale_v = lax.rsqrt(spread + EPSILON)
    return centre * scale_v, scale_v


def norm_backward(incoming, gain_v, unit, scale_v):
    scaled = incoming * gain_v
    mean_one = jnp.mean(scaled, axis=-1, keepdims=True)
    mean_two = jnp.mean(scaled * unit, axis=-1, keepdims=True)
    return scale_v * (scaled - mean_one - unit * mean_two)


def two_terms(column):
    high = column.astype(jnp.bfloat16)
    rest = (column - lax.reduce_precision(column, 8, 7)).astype(jnp.bfloat16)
    return jnp.stack([high, rest], axis=1)


def padded(pieces):
    width = sum(piece.shape[1] for piece in pieces)
    short = -width % 128
    height = pieces[0].shape[0]
    if short:
        pieces = pieces + [jnp.zeros((height, short), jnp.bfloat16)]
    return jnp.concatenate(pieces, axis=1)


def dot_nn(left, right):
    return jnp.dot(left, right, preferred_element_type=jnp.float32)


def dot_nt(left, right):
    return lax.dot_general(
        left, right, (((1,), (1,)), ((), ())), preferred_element_type=jnp.float32
    )


def dot_tn(left, right):
    return lax.dot_general(
        left, right, (((0,), (0,)), ((), ())), preferred_element_type=jnp.float32
    )


def turn(rows, cosine, sine_signed, lane):
    half_dim = HEAD_DIM // 2
    ahead = pltpu.roll(rows, rows.shape[1] - half_dim, axis=1)
    behind = pltpu.roll(rows, half_dim, axis=1)
    swapped = jnp.where(lane % HEAD_DIM < half_dim, ahead, behind)
    return rows * cosine + swapped * sine_signed


def forward_kernel(
    normed_ref, wq_ref, wk_ref, wv_ref, cos_ref, sin_ref, srow_ref, scol_ref,
    q_ref, k_ref, v_ref, ctx_ref, lse_ref, vt_ref,
):
    rows = normed_ref.shape[0]
    block = min(QUERY_BLOCK, rows)
    normed = normed_ref[...]
    cosine = cos_ref[...]
    sine = sin_ref[...]
    lane = lax.broadcasted_iota(jnp.int32, (rows, LANES), 1)
    dot = functools.partial(jnp.dot, preferred_element_type=jnp.float32)
    q_ref[...] = turn(dot(normed, wq_ref[...]), cosine, sine, lane).astype(jnp.bfloat16)
    k_ref[...] = turn(dot(normed, wk_ref[...]), cosine, sine, lane).astype(jnp.bfloat16)
    values = dot(normed, wv_ref[...])
    v_ref[...] = values.astype(jnp.bfloat16)
    vt_ref[...] = values.T.astype(jnp.bfloat16)

    @pl.loop(0, rows // block)
    def _(step):
        at = pl.ds(pl.multiple_of(step * block, block), block)
        same = scol_ref[...] == srow_ref[:, at]
        parts = []
        for head in range(LANES // HEAD_DIM):
            cols = slice(head * HEAD_DIM, (head + 1) * HEAD_DIM)
            scores = dot_nt(k_ref[:, cols], q_ref[at, cols]) * SCALE
            scores = jnp.where(same, scores, NEGATIVE)
            top = jnp.max(scores, axis=0, keepdims=True)
            terms = jnp.exp(scores - top)
            total = jnp.sum(terms, axis=0, keepdims=True)
            weights = (terms * (1.0 / total)).astype(jnp.bfloat16)
            parts.append(dot(vt_ref[cols, :], weights))
            lse_ref[0, head : head + 1, at] = top + jnp.log(total)
        ctx_ref[at, :] = jnp.concatenate(parts, axis=0).T.astype(jnp.bfloat16)


def backward_kernel(
    grad_ref, wo_ref, q_ref, k_ref, v_ref, cos_ref, sin_ref, srow_ref, scol_ref, lse_ref,
    dq_ref, dk_ref, dv_ref, g_ref, kt_ref, acc_q, acc_k, acc_v,
):
    rows = grad_ref.shape[0]
    block = min(QUERY_BLOCK, rows)
    dot = functools.partial(jnp.dot, preferred_element_type=jnp.float32)
    g_ref[...] = dot(grad_ref[...], wo_ref[...]).astype(jnp.bfloat16)
    kt_ref[...] = k_ref[...].astype(jnp.float32).T.astype(jnp.bfloat16)
    acc_k[...] = jnp.zeros_like(acc_k)
    acc_v[...] = jnp.zeros_like(acc_v)

    @pl.loop(0, rows // block)
    def _(step):
        at = pl.ds(pl.multiple_of(step * block, block), block)
        same = scol_ref[...] == srow_ref[:, at]
        parts = []
        for head in range(LANES // HEAD_DIM):
            cols = slice(head * HEAD_DIM, (head + 1) * HEAD_DIM)
            query = q_ref[at, cols]
            grad = g_ref[at, cols]
            scores = dot_nt(k_ref[:, cols], query) * SCALE
            probs = jnp.exp(jnp.where(same, scores - lse_ref[0, head : head + 1, at], NEGATIVE))
            acc_v[:, cols] += dot(probs.astype(jnp.bfloat16), grad)
            grad_probs = dot_nt(v_ref[:, cols], grad)
            weighted = probs * grad_probs
            drop = jnp.sum(weighted, axis=0, keepdims=True)
            grad_scores = (weighted - probs * drop).astype(jnp.bfloat16)
            acc_k[:, cols] += dot(grad_scores, query)
            parts.append(dot(kt_ref[cols, :], grad_scores))
        acc_q[at, :] = jnp.concatenate(parts, axis=0).T

    cosine = cos_ref[...] * SCALE
    sine = sin_ref[...] * -SCALE
    lane = lax.broadcasted_iota(jnp.int32, (rows, LANES), 1)
    dq_ref[...] = turn(acc_q[...], cosine, sine, lane).astype(jnp.bfloat16)
    dk_ref[...] = turn(acc_k[...], cosine, sine, lane).astype(jnp.bfloat16)
    dv_ref[...] = acc_v[...].astype(jnp.bfloat16)


def whole(shape):
    return pl.BlockSpec(shape, lambda pair: (0,) * len(shape))


def column_block(rows, first):
    return pl.BlockSpec((rows, LANES), lambda pair: (0, first + pair))


def attention_forward(normed_all, attn_pack, cosine, sine, starts, width_here):
    rows, width = normed_all.shape
    pairs = width_here // LANES
    heads_each = LANES // HEAD_DIM
    low = jax.ShapeDtypeStruct((rows, width_here), jnp.bfloat16)
    return pl.pallas_call(
        forward_kernel,
        grid=(pairs,),
        out_shape=(low, low, low, low, jax.ShapeDtypeStruct((pairs, heads_each, rows), jnp.float32)),
        in_specs=[
            whole((rows, width)),
            column_block(width, 0),
            column_block(width, pairs),
            column_block(width, 2 * pairs),
            whole((rows, LANES)),
            whole((rows, LANES)),
            whole((1, rows)),
            whole((rows, 1)),
        ],
        out_specs=[column_block(rows, 0)] * 4
        + [pl.BlockSpec((1, heads_each, rows), lambda pair: (pair, 0, 0))],
        scratch_shapes=[pltpu.VMEM((LANES, rows), jnp.bfloat16)],
        compiler_params=pltpu.CompilerParams(vmem_limit_bytes=VMEM_LIMIT),
        cost_estimate=pl.CostEstimate(
            flops=2 * rows * width * 3 * width_here + 4 * rows * rows * width_here,
            bytes_accessed=2 * (rows * width + 3 * width * width_here + 4 * rows * width_here),
            transcendentals=rows * rows * width_here // HEAD_DIM,
        ),
    )(normed_all, attn_pack, attn_pack, attn_pack, cosine, sine, starts[None, :], starts[:, None])


def attention_backward(grad_rows, attn_pack, queries, key_rows, values, cosine, sine, starts, lse):
    rows, width = grad_rows.shape
    width_here = queries.shape[1]
    pairs = width_here // LANES
    heads_each = LANES // HEAD_DIM
    low = jax.ShapeDtypeStruct((rows, width_here), jnp.bfloat16)
    return pl.pallas_call(
        backward_kernel,
        grid=(pairs,),
        out_shape=(low, low, low),
        in_specs=[
            whole((rows, width)),
            column_block(width, 0),
            column_block(rows, 0),
            column_block(rows, 0),
            column_block(rows, 0),
            whole((rows, LANES)),
            whole((rows, LANES)),
            whole((1, rows)),
            whole((rows, 1)),
            pl.BlockSpec((1, heads_each, rows), lambda pair: (pair, 0, 0)),
        ],
        out_specs=[column_block(rows, 0)] * 3,
        scratch_shapes=[
            pltpu.VMEM((rows, LANES), jnp.bfloat16),
            pltpu.VMEM((LANES, rows), jnp.bfloat16),
            pltpu.VMEM((rows, LANES), jnp.float32),
            pltpu.VMEM((rows, LANES), jnp.float32),
            pltpu.VMEM((rows, LANES), jnp.float32),
        ],
        compiler_params=pltpu.CompilerParams(vmem_limit_bytes=VMEM_LIMIT),
        cost_estimate=pl.CostEstimate(
            flops=2 * rows * width * width_here + 10 * rows * rows * width_here,
            bytes_accessed=2 * (rows * width + width * width_here + 7 * rows * width_here),
            transcendentals=rows * rows * width_here // HEAD_DIM,
        ),
    )(
        grad_rows, attn_pack, queries, key_rows, values, cosine, sine,
        starts[None, :], starts[:, None], lse,
    )


def shards(tokens, offsets, w_qkv, w_attn_out, w_in, w_mlp_out, gain_attn, gain_mlp, cotangent):
    rows_here = tokens.shape[0]
    group_rows = rows_here * lax.axis_size("tensor")
    model_here = w_qkv.shape[0]
    width_here = w_qkv.shape[2]
    hidden_here = w_in.shape[2]
    half_at = lax.axis_index("tensor") * rows_here
    position = (jnp.arange(group_rows, dtype=jnp.int32) + half_at) % group_rows
    starts = seq_starts(offsets[0], position)
    cosine_tab, sine_tab = rope_tables(position - starts)

    attn_pack, pending = gather_both(
        padded([w_qkv.reshape(model_here, 3 * width_here), gain_attn[:, None]]),
        padded(
            [w_attn_out.T, w_in.reshape(model_here, 2 * hidden_here), w_mlp_out.T, gain_mlp[:, None]]
        ),
    )
    gain_one = attn_pack[:, 3 * width_here].astype(jnp.float32)
    qkv_full = attn_pack[:, : 3 * width_here]

    token_rows = spread_rows(tokens)
    cotangent_rows = spread_rows(cotangent)
    grad_rows = cotangent_rows.astype(jnp.bfloat16)
    unit_one, scale_one = norm_parts(token_rows)
    normed_all = (unit_one * gain_one).astype(jnp.bfloat16)
    queries, key_rows, values, context, lse = attention_forward(
        normed_all, attn_pack, cosine_tab, sine_tab, starts, width_here
    )

    rest_pack = gather_rest(pending, lse)
    mlp_at = width_here
    mlp_end = width_here + 2 * hidden_here
    attn_out_full = rest_pack[:, :width_here]
    mlp_in_full = rest_pack[:, mlp_at:mlp_end]
    mlp_out_full = rest_pack[:, mlp_end : mlp_end + hidden_here]
    gain_two = rest_pack[:, mlp_end + hidden_here].astype(jnp.float32)
    attended = collect_all(dot_nt(context, attn_out_full), rows_here)
    hidden = token_rows + attended
    unit_two, scale_two = norm_parts(hidden)
    mlp_rows = (unit_two * gain_two).astype(jnp.bfloat16)
    gate_part = dot_nn(mlp_rows, mlp_in_full[:, :hidden_here])
    up_part = dot_nn(mlp_rows, mlp_in_full[:, hidden_here:])
    grad_product = dot_nn(grad_rows, mlp_out_full)
    bell = 0.5 * (1.0 + lax.erf(gate_part * math.sqrt(0.5)))
    activated = gate_part * bell
    slope = bell + gate_part * jnp.exp(-0.5 * gate_part * gate_part) * (1.0 / math.sqrt(2 * math.pi))
    product_rows = (activated * up_part).astype(jnp.bfloat16)
    grad_gate_up = jnp.concatenate(
        [
            (grad_product * up_part * slope).astype(jnp.bfloat16),
            (grad_product * activated).astype(jnp.bfloat16),
        ],
        axis=1,
    )
    grad_normed_two = collect_all(dot_nt(grad_gate_up, mlp_in_full), rows_here)
    grad_hidden = cotangent_rows + norm_backward(grad_normed_two, gain_two, unit_two, scale_two)
    grad_gain_two = jnp.sum((grad_normed_two * unit_two)[:rows_here], axis=0)
    grad_hidden_rows = grad_hidden.astype(jnp.bfloat16)
    grads_three = attention_backward(
        grad_hidden_rows, rest_pack, queries, key_rows, values,
        cosine_tab, sine_tab, starts, lse,
    )
    mlp_terms = padded(
        [
            dot_tn(mlp_rows, grad_gate_up).astype(jnp.bfloat16),
            dot_tn(grad_rows, product_rows).astype(jnp.bfloat16),
            two_terms(grad_gain_two),
        ]
    )
    mlp_sums = sum_blocks(mlp_terms, grads_three[0])
    branch = collect_own(dot_nt(product_rows, mlp_out_full), rows_here)
    outputs = hidden[:rows_here] + branch

    grad_projected = jnp.concatenate(grads_three, axis=1)
    grad_normed_one = collect_own(dot_nt(grad_projected, qkv_full), rows_here)
    grad_tokens = grad_hidden[:rows_here] + norm_backward(
        grad_normed_one, gain_one, unit_one[:rows_here], scale_one[:rows_here]
    )
    grad_gain_one = jnp.sum(grad_normed_one * unit_one[:rows_here], axis=0)
    attn_terms = padded(
        [
            dot_tn(normed_all, grad_projected).astype(jnp.bfloat16),
            dot_tn(grad_hidden_rows, context).astype(jnp.bfloat16),
            two_terms(grad_gain_one),
        ]
    )
    attn_sums = sum_blocks(attn_terms)

    gain_one_cols = attn_sums[:, 4 * width_here : 4 * width_here + 2].sum(axis=1)
    gain_two_cols = mlp_sums[:, 3 * hidden_here : 3 * hidden_here + 2].sum(axis=1)
    gains = jnp.stack([gain_one_cols, gain_two_cols])
    gains = gains + other_half(gains)
    return (
        outputs,
        grad_tokens,
        attn_sums[:, : 3 * width_here].reshape(model_here, 3, width_here),
        attn_sums[:, 3 * width_here : 4 * width_here].T,
        mlp_sums[:, : 2 * hidden_here].reshape(model_here, 2, hidden_here),
        mlp_sums[:, 2 * hidden_here : 3 * hidden_here].T,
        gains[0],
        gains[1],
    )


def fast_columns(width_here, hidden_here):
    main = hidden_here // LANES * LANES
    pairs = width_here // LANES
    at = {"gains": (0, LANES)}
    place = LANES
    for pair in range(pairs):
        at["pair%d" % pair] = (place, 3 * LANES)
        place += 3 * LANES
    for name, size in (
        ("out", width_here), ("mlp", main + LANES), ("gate", main), ("up", main), ("tail", LANES),
    ):
        at[name] = (place, size)
        place += size
    at["total"] = (0, place)
    return at


def pack_shards(w_qkv, w_attn_out, w_in, w_mlp_out, gain_attn, gain_mlp):
    height, _, width_here = w_qkv.shape
    hidden_here = w_in.shape[2]
    main = hidden_here // LANES * LANES
    pairs = width_here // LANES
    gains = jnp.concatenate(
        [gain_attn[:, None], gain_mlp[:, None], jnp.zeros((height, LANES - 2), jnp.bfloat16)], axis=1
    )
    by_pair = w_qkv.reshape(height, 3, pairs, LANES).transpose(0, 2, 1, 3)
    short = main + LANES - hidden_here
    return jnp.concatenate(
        [
            gains,
            by_pair.reshape(height, 3 * width_here),
            w_attn_out.T,
            w_mlp_out.T,
            jnp.zeros((height, short), jnp.bfloat16),
            w_in[:, 0, :main],
            w_in[:, 1, :main],
            w_in[:, 0, main:],
            w_in[:, 1, main:],
        ],
        axis=1,
    )


class Links:
    def __init__(self, ref):
        self.ref = ref
        self.dp = lax.axis_index("dp")
        self.core = lax.axis_index("tensor")
        self.x = self.dp % 2
        self.y = (self.dp // 2) % 2
        self.z = self.dp // 4
        plane = self.dp % 4
        self.x_side = self.dp + 1 - 2 * self.x
        self.y_side = self.dp + 2 - 4 * self.y
        self.z_of = [None, self.z + 1 - 2 * (self.z % 2), (self.z + 2) % 4, 3 - self.z]
        self.z_side = [None] + [place * 4 + plane for place in self.z_of[1:]]
        self.started = []

    def enter(self):
        barrier = pltpu.get_barrier_semaphore()
        others = [(self.x_side, self.core), (self.y_side, self.core), (self.dp, 1 - self.core)]
        others += [(place, self.core) for place in self.z_side[1:]]
        for other in others:
            pl.semaphore_signal(
                barrier, inc=1, device_id=other, device_id_type=pl.DeviceIdType.MESH
            )
        pl.semaphore_wait(barrier, len(others))

    def copy(self, source, target, sems, place, device):
        return pltpu.make_async_remote_copy(
            src_ref=source,
            dst_ref=target,
            send_sem=sems[0].at[place],
            recv_sem=sems[1].at[place],
            device_id=device,
            device_id_type=pl.DeviceIdType.MESH,
        )

    def start(self, *copies):
        for copy in copies:
            copy.start()
            self.started.append(copy)

    def to_core(self, source, target, place):
        copy = self.copy(
            source, target, (self.ref.core_out, self.ref.core_in), place, (self.dp, 1 - self.core)
        )
        self.start(copy)
        return copy

    def finish(self):
        for copy in self.started:
            copy.wait_send()
        self.started = []


class Gather(Links):
    def __init__(self, ref, chunks):
        super().__init__(ref)
        self.chunks = chunks
        self.got = {}

    def send_z(self, name):
        chunk = list(self.chunks).index(name)
        cols = pl.ds(*self.chunks[name])
        block = self.ref.full.at[self.z, self.y, self.x, :, cols]
        copies = [
            self.copy(
                block, block, (self.ref.far_out, self.ref.far_in), 3 * chunk + step - 1,
                (self.z_side[step], self.core),
            )
            for step in (1, 2, 3)
        ]
        self.start(*copies)
        self.got[name] = copies

    def arrive(self, name):
        for copy in self.got[name]:
            copy.wait_recv()

    def near(self, name, stage, first, second):
        chunk = list(self.chunks).index(name)
        sems = (self.ref.near_out, self.ref.near_in)
        place = 4 * chunk + 2 * stage
        copies = [
            self.copy(first[0], first[0], sems, place, (first[1], self.core)),
            self.copy(second[0], second[0], sems, place + 1, (second[1], self.core)),
        ]
        self.arrive(name)
        self.start(*copies)
        self.got[name] = copies

    def send_one(self, name):
        cols = pl.ds(*self.chunks[name])
        low, high = pl.ds(0, 2), pl.ds(2, 2)
        full = self.ref.full
        self.near(
            name, 0,
            (full.at[low, self.y, self.x, :, cols], self.x_side),
            (full.at[high, self.y, self.x, :, cols], self.y_side),
        )

    def send_two(self, name):
        cols = pl.ds(*self.chunks[name])
        low, high = pl.ds(0, 2), pl.ds(2, 2)
        both = pl.ds(0, 2)
        full = self.ref.full
        self.near(
            name, 1,
            (full.at[low, self.y, both, :, cols], self.y_side),
            (full.at[high, both, self.x, :, cols], self.x_side),
        )


class Scatter:
    def __init__(self, link, chunks):
        self.link = link
        self.ref = link.ref
        self.chunks = chunks
        self.got = {}

    def send(self, name, stage, moves):
        sems = (self.ref.sum_out, self.ref.sum_in)
        place = 7 * list(self.chunks).index(name) + 2 * stage
        copies = [
            self.link.copy(source, target, sems, place + step, (side, self.link.core))
            for step, (source, target, side) in enumerate(moves)
        ]
        self.link.start(*copies)
        self.got[name] = copies

    def arrive(self, name):
        for copy in self.got[name]:
            copy.wait_recv()

    def parts(self, name):
        held, span, place = self.chunks[name]
        return held, pl.ds(*span), pl.ds(place, span[1])

    def one(self, name):
        link, ref = self.link, self.ref
        held, cols, to = self.parts(name)
        both = pl.ds(0, 2)
        self.send(name, 0, [
            (held.at[pl.ds(0, 2), 1 - link.y, both, :, cols], ref.low_one.at[:, :, :, to], link.y_side),
            (held.at[pl.ds(2, 2), both, 1 - link.x, :, cols], ref.high_one.at[:, :, :, to], link.x_side),
        ])

    def two(self, name):
        link, ref = self.link, self.ref
        held, cols, to = self.parts(name)
        both = pl.ds(0, 2)
        self.arrive(name)
        at = (pl.ds(0, 2), link.y, both, slice(None), cols)
        held[at] = held[at] + ref.low_one[:, :, :, to]
        at = (pl.ds(2, 2), both, link.x, slice(None), cols)
        held[at] = held[at] + ref.high_one[:, :, :, to]
        self.send(name, 1, [
            (held.at[pl.ds(0, 2), link.y, 1 - link.x, :, cols], ref.low_two.at[:, :, to], link.x_side),
            (held.at[pl.ds(2, 2), 1 - link.y, link.x, :, cols], ref.high_two.at[:, :, to], link.y_side),
        ])

    def three(self, name):
        link, ref = self.link, self.ref
        held, cols, to = self.parts(name)
        self.arrive(name)
        at = (pl.ds(0, 2), link.y, link.x, slice(None), cols)
        held[at] = held[at] + ref.low_two[:, :, to]
        at = (pl.ds(2, 2), link.y, link.x, slice(None), cols)
        held[at] = held[at] + ref.high_two[:, :, to]
        self.send(name, 2, [
            (
                held.at[link.z_of[step], link.y, link.x, :, cols],
                ref.far_sum.at[step - 1, :, to],
                link.z_side[step],
            )
            for step in (1, 2, 3)
        ])

    def four(self, name):
        link, ref = self.link, self.ref
        held, cols, to = self.parts(name)
        self.arrive(name)
        total = held[link.z, link.y, link.x, :, cols].astype(jnp.float32)
        for step in range(3):
            total = total + ref.far_sum[step, :, to].astype(jnp.float32)
        ref.sums[:, to] = total


def weights_at(full, span):
    block = full[:, :, :, :, span[0] : span[0] + span[1]]
    return block.reshape(-1, span[1])


def row_loop(rows, block):
    def wrap(body):
        @pl.loop(0, rows // block)
        def _(step):
            body(pl.ds(pl.multiple_of(step * block, block), block))

    return wrap


def layer_kernel(names, spans, *refs):
    ref = types.SimpleNamespace(**dict(zip(names, refs)))
    half, width = ref.tok.shape
    rows = 2 * half
    pairs = (spans["out"][1]) // LANES
    main = spans["gate"][1]
    chunk_names = ["gains"] + ["pair%d" % pair for pair in range(pairs)] + ["out", "mlp"]
    chunks = {name: spans[name] for name in chunk_names}
    chunks["gate"] = spans["gate"]
    chunks["up"] = (spans["up"][0], main + LANES)
    link = Gather(ref, chunks)
    core = link.core
    own = pl.ds(pl.multiple_of(core * half, half), half)
    own_at = core * half
    other_at = (1 - core) * half
    part = 256

    ref.grad_low = ref.normed
    ref.grad_rolled = ref.context_rolled
    scatter = Scatter(
        link,
        {
            "inner": (ref.full, (spans["gate"][0], 2 * main + LANES), spans["gate"][0]),
            "mlp": (ref.full, spans["mlp"], spans["mlp"][0]),
            "out": (ref.full, spans["out"], spans["out"][0]),
            **{
                "pair%d" % pair: (
                    ref.grad_qkv,
                    (3 * LANES * pair, 3 * LANES),
                    spans["pair%d" % pair][0],
                )
                for pair in range(pairs)
            },
            "gains": (ref.full, spans["gains"], spans["gains"][0]),
        },
    )

    link.enter()
    ref.full[link.z, link.y, link.x] = ref.pack[...]
    link.send_z("gains")
    link.send_z("pair0")
    link.send_z("pair1")

    @row_loop(half, 128)
    def _(at):
        unit, scale = norm_parts(ref.tok[at, :])
        ref.unit_one[at, :] = unit
        ref.scale_one[at, :] = jnp.broadcast_to(scale, (128, LANES))
        here = pl.ds(pl.multiple_of(own_at + at.start, 128), 128)
        ref.grad_rows[here, :] = ref.cot[at, :].astype(jnp.bfloat16)

    got_grad = link.to_core(ref.grad_rows.at[own, :], ref.grad_rows.at[own, :], 0)
    link.send_one("gains")

    shift = jnp.int32(0)
    for slot in range(ref.offsets.shape[1]):
        entry = ref.offsets[0, slot]
        shift = jnp.maximum(shift, jnp.where(entry <= half - 1, entry, 0))

    def source_of(place):
        moved = place + shift
        return jnp.where(moved >= rows, moved - rows, moved)

    def start_of(place):
        start = jnp.zeros_like(place)
        for slot in range(ref.offsets.shape[1]):
            entry = ref.offsets[0, slot]
            start = jnp.maximum(start, jnp.where(place >= entry, entry, 0))
        return start

    @row_loop(rows, part)
    def _(at):
        place = source_of(lax.broadcasted_iota(jnp.int32, (part, LANES), 0) + at.start)
        start = start_of(place)
        angle = (place - start).astype(jnp.float32) * ref.inverse[...]
        lane = lax.broadcasted_iota(jnp.int32, (part, LANES), 1)
        sine = jnp.sin(angle)
        ref.cosine[at, :] = jnp.cos(angle)
        ref.sine[at, :] = jnp.where(lane % HEAD_DIM < HEAD_DIM // 2, -sine, sine)

    link.send_two("gains")
    link.send_z("pair2")
    key_start = start_of(source_of(lax.broadcasted_iota(jnp.int32, (half, 1), 0) + half))
    query_start = start_of(source_of(lax.broadcasted_iota(jnp.int32, (1, half), 1) + half))
    ref.bias[...] = jnp.where(key_start == query_start, 0.0, NEGATIVE)

    @row_loop(rows, part)
    def _(at):
        down = lax.broadcasted_iota(jnp.int32, (part, rows), 0) + at.start
        along = lax.broadcasted_iota(jnp.int32, (part, rows), 1)
        ref.perm[at, :] = jnp.where(source_of(down) == along, 1.0, 0.0).astype(jnp.bfloat16)
        ref.perm_back[at, :] = jnp.where(source_of(along) == down, 1.0, 0.0).astype(jnp.bfloat16)

    link.send_one("pair0")
    link.arrive("gains")
    slot = lax.broadcasted_iota(jnp.int32, (8, LANES), 0)
    lane = lax.broadcasted_iota(jnp.int32, (8, LANES), 1)
    pick = jnp.where(slot == lane, 1.0, 0.0).astype(jnp.bfloat16)
    ref.gain[...] = dot_nt(pick, weights_at(ref.full, spans["gains"]))

    @row_loop(half, 128)
    def _(at):
        here = pl.ds(pl.multiple_of(own_at + at.start, 128), 128)
        ref.normed[here, :] = (ref.unit_one[at, :] * ref.gain[0:1, :]).astype(jnp.bfloat16)

    got_normed = link.to_core(ref.normed.at[own, :], ref.normed.at[own, :], 1)
    link.send_one("pair1")
    link.send_two("pair0")
    link.send_z("out")
    got_normed.wait_recv()

    @row_loop(rows, part)
    def _(at):
        ref.rolled[at, :] = dot_nn(ref.perm[at, :], ref.normed[...]).astype(jnp.bfloat16)

    link.send_one("pair2")
    link.send_two("pair1")
    link.send_z("mlp")

    def project(pair):
        link.arrive("pair%d" % pair)
        cols = slice(pair * LANES, (pair + 1) * LANES)

        @row_loop(rows, part)
        def _(at):
            three = dot_nn(ref.rolled[at, :], weights_at(ref.full, spans["pair%d" % pair]))
            lane = lax.broadcasted_iota(jnp.int32, (part, LANES), 1)
            cosine, sine = ref.cosine[at, :], ref.sine[at, :]
            query = turn(three[:, :LANES], cosine, sine, lane) * SCALE
            ref.queries[at, cols] = query.astype(jnp.bfloat16)
            ref.keys[at, cols] = turn(
                three[:, LANES : 2 * LANES], cosine, sine, lane
            ).astype(jnp.bfloat16)
            ref.values[at, cols] = three[:, 2 * LANES :].astype(jnp.bfloat16)
            ref.values_t[:, at] = three[:, 2 * LANES :].T.astype(jnp.bfloat16)

    def attend(pair, first):
        cols = slice(pair * LANES, (pair + 1) * LANES)
        base = 0 if first else half

        @pl.loop(0, half // part)
        def _(step):
            at = pl.ds(pl.multiple_of(base + step * part, part), part)
            query_pair = ref.queries[at, cols]
            lane = lax.broadcasted_iota(jnp.int32, (part, LANES), 1)
            parts = []
            for head in range(LANES // HEAD_DIM):
                query = jnp.where(lane // HEAD_DIM == head, query_pair, 0)
                scores = dot_nt(ref.keys[base : base + half, cols], query)
                if not first:
                    scores = scores + ref.bias[:, pl.ds(pl.multiple_of(step * part, part), part)]
                top = jnp.max(scores, axis=0, keepdims=True)
                terms = jnp.exp(scores - top)
                total = jnp.sum(terms, axis=0, keepdims=True)
                mixed = dot_nn(
                    ref.values_t[head * HEAD_DIM : (head + 1) * HEAD_DIM, base : base + half],
                    terms.astype(jnp.bfloat16),
                )
                parts.append(mixed * (1.0 / total))
                ref.lse[pair, head : head + 1, at] = top + jnp.log(total)
            ref.context_rolled[at, cols] = jnp.concatenate(parts, axis=0).T.astype(jnp.bfloat16)

    project(0)
    attend(0, True)
    link.send_one("out")
    link.send_two("pair2")
    link.send_z("gate")
    attend(0, False)
    project(1)
    attend(1, True)
    link.send_one("mlp")
    link.send_two("out")
    link.send_z("up")
    attend(1, False)
    project(2)
    attend(2, True)
    link.send_one("gate")
    link.send_two("mlp")
    attend(2, False)

    @row_loop(rows, part)
    def _(at):
        ref.context[at, :] = dot_nn(ref.perm_back[at, :], ref.context_rolled[...]).astype(jnp.bfloat16)

    link.send_one("up")
    link.send_two("gate")
    link.arrive("out")

    def pair_sum(product, place, sem, keep):
        @row_loop(half, part)
        def _(at):
            there = pl.ds(pl.multiple_of(other_at + at.start, part), part)
            ref.sent[place, at, :] = product(there).astype(jnp.bfloat16)

        got = link.to_core(ref.sent.at[place], ref.taken.at[place], sem)

        @row_loop(half, part)
        def _(at):
            here = pl.ds(pl.multiple_of(own_at + at.start, part), part)
            keep[at, :] = product(here)

        return got

    got_attended = pair_sum(
        lambda at: dot_nt(ref.context[at, :], weights_at(ref.full, spans["out"])), 0, 2, ref.hidden
    )
    got_attended.wait_recv()

    @row_loop(half, 128)
    def _(at):
        hidden = ref.tok[at, :] + ref.hidden[at, :] + ref.taken[0, at, :].astype(jnp.float32)
        ref.hidden[at, :] = hidden
        unit, scale = norm_parts(hidden)
        ref.unit_two[at, :] = unit
        ref.scale_two[at, :] = jnp.broadcast_to(scale, (128, LANES))
        here = pl.ds(pl.multiple_of(own_at + at.start, 128), 128)
        ref.normed_mlp[here, :] = (unit * ref.gain[1:2, :]).astype(jnp.bfloat16)

    got_mlp = link.to_core(ref.normed_mlp.at[own, :], ref.normed_mlp.at[own, :], 6)
    link.send_two("up")
    got_grad.wait_recv()
    link.arrive("mlp")

    @row_loop(rows, part)
    def _(at):
        ref.grad_product[at, :] = dot_nn(ref.grad_rows[at, :], weights_at(ref.full, spans["mlp"]))

    got_mlp.wait_recv()
    link.arrive("gate")
    link.arrive("up")

    def gated(gate, up, grad):
        bell = 0.5 * (1.0 + lax.erf(gate * math.sqrt(0.5)))
        activated = gate * bell
        slope = bell + gate * jnp.exp(-0.5 * gate * gate) * (1.0 / math.sqrt(2 * math.pi))
        return activated * up, grad * up * slope, grad * activated

    @row_loop(rows, part)
    def _(at):
        low = ref.normed_mlp[at, :]
        gate = dot_nn(low, weights_at(ref.full, spans["gate"]))
        up = dot_nn(low, weights_at(ref.full, spans["up"]))
        product, grad_gate, grad_up = gated(gate, up, ref.grad_product[at, :main])
        ref.product[at, :main] = product.astype(jnp.bfloat16)
        ref.grad_gate_up[at, :main] = grad_gate.astype(jnp.bfloat16)
        ref.grad_gate_up[at, main : 2 * main] = grad_up.astype(jnp.bfloat16)
        tail = dot_nn(low, weights_at(ref.full, spans["tail"]))
        product, grad_gate, grad_up = gated(
            tail, pltpu.roll(tail, LANES // 2, axis=1), ref.grad_product[at, main:]
        )
        lane = lax.broadcasted_iota(jnp.int32, (part, LANES), 1)
        lower = lane < LANES // 2
        ref.product[at, main:] = jnp.where(lower, product, 0.0).astype(jnp.bfloat16)
        ref.grad_gate_up[at, 2 * main :] = jnp.where(
            lower, grad_gate, pltpu.roll(grad_up, LANES // 2, axis=1)
        ).astype(jnp.bfloat16)

    inner = (spans["gate"][0], 2 * main + LANES)
    got_normed_two = pair_sum(
        lambda at: dot_nt(ref.grad_gate_up[at, :], weights_at(ref.full, inner)), 1, 3, ref.grad_hidden
    )
    link.finish()

    def weight_grad(left, right, held, first):
        wide = right.shape[1]

        @pl.loop(0, 2)
        def _(step):
            cols = pl.ds(pl.multiple_of(step * (width // 2), LANES), width // 2)
            block = dot_tn(left[:, cols], right[...]).astype(jnp.bfloat16)
            held[pl.ds(2 * step, 2), :, :, :, first : first + wide] = block.reshape(
                2, 2, 2, width // 16, wide
            )

    weight_grad(ref.normed_mlp, ref.grad_gate_up, ref.full, inner[0])
    scatter.one("inner")
    got_normed_two.wait_recv()
    ref.gain_rows[...] = jnp.zeros_like(ref.gain_rows)

    @row_loop(half, 128)
    def _(at):
        incoming = ref.grad_hidden[at, :] + ref.taken[1, at, :].astype(jnp.float32)
        unit = ref.unit_two[at, :]
        ref.gain_rows[1:2, :] += jnp.sum(incoming * unit, axis=0, keepdims=True)
        grad = ref.cot[at, :] + norm_backward(
            incoming, ref.gain[1:2, :], unit, ref.scale_two[at, 0:1]
        )
        ref.grad_hidden[at, :] = grad
        here = pl.ds(pl.multiple_of(own_at + at.start, 128), 128)
        ref.grad_low[here, :] = grad.astype(jnp.bfloat16)

    got_low = link.to_core(ref.grad_low.at[own, :], ref.grad_low.at[own, :], 7)
    got_branch = pair_sum(
        lambda at: dot_nt(ref.product[at, :], weights_at(ref.full, spans["mlp"])), 2, 4, ref.outputs
    )
    weight_grad(ref.grad_rows, ref.product, ref.full, spans["mlp"][0])
    scatter.one("mlp")
    scatter.two("inner")
    got_low.wait_recv()

    @row_loop(rows, part)
    def _(at):
        ref.grad_context[at, :] = dot_nn(
            ref.grad_low[at, :], weights_at(ref.full, spans["out"])
        ).astype(jnp.bfloat16)

    @row_loop(rows, part)
    def _(at):
        ref.grad_rolled[at, :] = dot_nn(ref.perm[at, :], ref.grad_context[...]).astype(jnp.bfloat16)

    weight_grad(ref.grad_low, ref.context, ref.full, spans["out"][0])
    scatter.one("out")
    scatter.two("mlp")
    scatter.three("inner")
    got_branch.wait_recv()

    @row_loop(half, 128)
    def _(at):
        ref.outputs[at, :] = (
            ref.outputs[at, :] + ref.hidden[at, :] + ref.taken[2, at, :].astype(jnp.float32)
        )

    def pull(pair, first):
        cols = slice(pair * LANES, (pair + 1) * LANES)
        base = 0 if first else half
        span = slice(base, base + half)

        @row_loop(half, part)
        def _(at):
            at = pl.ds(pl.multiple_of(base + at.start, part), part)
            ref.keys_t[:, at] = ref.keys[at, cols].astype(jnp.float32).T.astype(jnp.bfloat16)

        @pl.loop(0, half // part)
        def _(step):
            at = pl.ds(pl.multiple_of(base + step * part, part), part)
            lane = lax.broadcasted_iota(jnp.int32, (part, LANES), 1)
            query_pair = ref.queries[at, cols]
            grad_pair = ref.grad_rolled[at, cols]
            parts, all_probs, all_grads, all_queries, all_pulls = [], [], [], [], []
            for head in range(LANES // HEAD_DIM):
                query = jnp.where(lane // HEAD_DIM == head, query_pair, 0)
                grad = jnp.where(lane // HEAD_DIM == head, grad_pair, 0)
                scores = dot_nt(ref.keys[span, cols], query)
                if not first:
                    scores = scores + ref.bias[:, pl.ds(pl.multiple_of(step * part, part), part)]
                probs = jnp.exp(scores - ref.lse[pair, head : head + 1, at])
                grad_probs = dot_nt(ref.values[span, cols], grad)
                weighted = probs * grad_probs
                drop = jnp.sum(weighted, axis=0, keepdims=True)
                pulled = (weighted - probs * drop).astype(jnp.bfloat16)
                all_probs.append(probs.astype(jnp.bfloat16))
                all_grads.append(grad)
                all_queries.append(query)
                all_pulls.append(pulled)
                parts.append(
                    dot_nn(ref.keys_t[head * HEAD_DIM : (head + 1) * HEAD_DIM, span], pulled)
                )
            grad_values = dot_nn(
                jnp.concatenate(all_probs, axis=1), jnp.concatenate(all_grads, axis=0)
            )
            grad_keys = dot_nn(
                jnp.concatenate(all_pulls, axis=1), jnp.concatenate(all_queries, axis=0)
            )

            @pl.when(step == 0)
            def _():
                ref.acc[span, LANES : 2 * LANES] = grad_keys
                ref.acc[span, 2 * LANES :] = grad_values

            @pl.when(step > 0)
            def _():
                ref.acc[span, LANES : 2 * LANES] += grad_keys
                ref.acc[span, 2 * LANES :] += grad_values

            ref.acc[at, :LANES] = jnp.concatenate(parts, axis=0).T

    def unproject(pair):
        first = 3 * LANES * pair

        @row_loop(rows, part)
        def _(at):
            lane = lax.broadcasted_iota(jnp.int32, (part, LANES), 1)
            cosine, sine = ref.cosine[at, :], -ref.sine[at, :]
            grad_query = turn(ref.acc[at, :LANES], cosine, sine, lane) * SCALE
            grad_key = turn(ref.acc[at, LANES : 2 * LANES], cosine, sine, lane)
            ref.grad_three[at, :LANES] = grad_query.astype(jnp.bfloat16)
            ref.grad_three[at, LANES : 2 * LANES] = grad_key.astype(jnp.bfloat16)
            ref.grad_three[at, 2 * LANES :] = ref.acc[at, 2 * LANES :].astype(jnp.bfloat16)

        weight_grad(ref.rolled, ref.grad_three, ref.grad_qkv, first)
        scatter.one("pair%d" % pair)

        @row_loop(rows, part)
        def _(at):
            ref.grad_projected[at, first : first + 3 * LANES] = dot_nn(
                ref.perm_back[at, :], ref.grad_three[...]
            ).astype(jnp.bfloat16)

    pull(0, True)
    scatter.two("out")
    scatter.three("mlp")
    pull(0, False)
    scatter.four("inner")
    unproject(0)
    scatter.three("out")
    pull(1, True)
    scatter.two("pair0")
    scatter.four("mlp")
    pull(1, False)
    scatter.three("pair0")
    unproject(1)
    scatter.four("out")
    pull(2, True)
    scatter.two("pair1")
    scatter.four("pair0")
    pull(2, False)
    scatter.three("pair1")
    unproject(2)
    qkv_span = (spans["pair0"][0], 3 * pairs * LANES)
    got_one = pair_sum(
        lambda at: dot_nt(ref.grad_projected[at, :], weights_at(ref.full, qkv_span)),
        0, 5, ref.grad_tokens,
    )
    scatter.two("pair2")
    scatter.four("pair1")
    got_one.wait_recv()

    @row_loop(half, 128)
    def _(at):
        incoming = ref.grad_tokens[at, :] + ref.taken[0, at, :].astype(jnp.float32)
        unit = ref.unit_one[at, :]
        ref.gain_rows[0:1, :] += jnp.sum(incoming * unit, axis=0, keepdims=True)
        ref.grad_tokens[at, :] = ref.grad_hidden[at, :] + norm_backward(
            incoming, ref.gain[0:1, :], unit, ref.scale_one[at, 0:1]
        )

    got_gain = link.to_core(ref.gain_rows, ref.gain_other, 8)
    scatter.three("pair2")
    got_gain.wait_recv()
    gain_rows = ref.gain_rows[...] + ref.gain_other[...]
    high = gain_rows.astype(jnp.bfloat16)
    rest = (gain_rows - high.astype(jnp.float32)).astype(jnp.bfloat16)
    slot = lax.broadcasted_iota(jnp.int32, (16, LANES), 0)
    lane = lax.broadcasted_iota(jnp.int32, (16, LANES), 1)
    pick = jnp.where(slot == lane, 1.0, 0.0).astype(jnp.bfloat16)
    columns = dot_tn(jnp.concatenate([high, rest], axis=0), pick).astype(jnp.bfloat16)
    ref.full[:, :, :, :, 0:LANES] = columns.reshape(4, 2, 2, width // 16, LANES)
    scatter.one("gains")
    scatter.four("pair2")
    scatter.two("gains")
    scatter.three("gains")
    scatter.four("gains")
    link.finish()


def call_layer(pack, tokens, cotangent, offsets, spans):
    half, width = tokens.shape
    rows = 2 * half
    height, total = pack.shape
    width_here = spans["out"][1]
    pairs = width_here // LANES
    main = spans["gate"][1]
    half_dim = HEAD_DIM // 2
    inverse = jnp.power(
        jnp.float32(ROPE_BASE), -2.0 * jnp.arange(half_dim, dtype=jnp.float32) / HEAD_DIM
    )
    inverse = jnp.tile(inverse, LANES // half_dim)[None, :]
    low, wide = jnp.bfloat16, jnp.float32
    outs = dict(
        outputs=((half, width), wide),
        grad_tokens=((half, width), wide),
        sums=((height, total), wide),
    )
    chunk_count = 1 + pairs + 4
    kept = dict(
        full=((4, 2, 2, height, total), low),
        grad_qkv=((4, 2, 2, height, 3 * width_here), low),
        low_one=((2, 2, height, total), low),
        high_one=((2, 2, height, total), low),
        low_two=((2, height, total), low),
        high_two=((2, height, total), low),
        far_sum=((3, height, total), low),
        normed=((rows, width), low),
        rolled=((rows, width), low),
        grad_rows=((rows, width), low),
        normed_mlp=((rows, width), low),
        perm=((rows, rows), low),
        perm_back=((rows, rows), low),
        bias=((half, half), wide),
        values_t=((LANES, rows), low),
        keys_t=((LANES, rows), low),
        queries=((rows, width_here), low),
        keys=((rows, width_here), low),
        values=((rows, width_here), low),
        context=((rows, width_here), low),
        context_rolled=((rows, width_here), low),
        grad_context=((rows, width_here), low),
        grad_three=((rows, 3 * LANES), low),
        grad_projected=((rows, 3 * width_here), low),
        acc=((rows, 3 * LANES), wide),
        lse=((pairs, LANES // HEAD_DIM, rows), wide),
        product=((rows, main + LANES), low),
        grad_gate_up=((rows, 2 * main + LANES), low),
        grad_product=((rows, main + LANES), wide),
        sent=((3, half, width), low),
        taken=((3, half, width), low),
        hidden=((half, width), wide),
        grad_hidden=((half, width), wide),
        unit_one=((half, width), wide),
        unit_two=((half, width), wide),
        scale_one=((half, LANES), wide),
        scale_two=((half, LANES), wide),
        cosine=((rows, LANES), wide),
        sine=((rows, LANES), wide),
        gain=((8, width), wide),
        gain_rows=((8, width), wide),
        gain_other=((8, width), wide),
    )
    scratch = {name: pltpu.VMEM(*entry) for name, entry in kept.items()}
    for name, count in (
        ("far", 3 * chunk_count), ("near", 4 * chunk_count), ("core", 9), ("sum", 7 * (pairs + 4)),
    ):
        scratch[name + "_out"] = pltpu.SemaphoreType.DMA((count,))
        scratch[name + "_in"] = pltpu.SemaphoreType.DMA((count,))
    names = ["offsets", "pack", "tok", "cot", "inverse"] + list(outs) + list(scratch)
    vmem = pl.BlockSpec(memory_space=pltpu.VMEM)
    results = pl.pallas_call(
        functools.partial(layer_kernel, names, spans),
        out_shape=[jax.ShapeDtypeStruct(*entry) for entry in outs.values()],
        in_specs=[pl.BlockSpec(memory_space=pltpu.SMEM)] + [vmem] * 4,
        out_specs=[vmem] * len(outs),
        scratch_shapes=list(scratch.values()),
        compiler_params=pltpu.CompilerParams(
            collective_id=0, has_side_effects=True, vmem_limit_bytes=63 * 1024 * 1024
        ),
        cost_estimate=pl.CostEstimate(
            flops=12 * 10**9, bytes_accessed=30 * 10**6, transcendentals=10**7
        ),
    )(offsets, pack, tokens, cotangent, inverse)
    return types.SimpleNamespace(**dict(zip(outs, results)))


def fast_shards(tokens, offsets, w_qkv, w_attn_out, w_in, w_mlp_out, gain_attn, gain_mlp, cotangent):
    half = tokens.shape[0]
    rows = 2 * half
    height, _, width_here = w_qkv.shape
    hidden_here = w_in.shape[2]
    pairs = width_here // LANES
    main = hidden_here // LANES * LANES
    spans = fast_columns(width_here, hidden_here)
    pack = pack_shards(w_qkv, w_attn_out, w_in, w_mlp_out, gain_attn, gain_mlp)
    f = call_layer(pack, tokens, cotangent, offsets, spans)
    pick = lambda name: f.sums[:, spans[name][0] : spans[name][0] + spans[name][1]]
    at = spans["pair0"][0]
    tail = pick("tail")
    gate = jnp.concatenate([pick("gate"), tail[:, : hidden_here - main]], axis=1)
    up = jnp.concatenate([pick("up"), tail[:, hidden_here - main :]], axis=1)
    return (
        f.outputs,
        f.grad_tokens,
        f.sums[:, at : at + 3 * width_here]
        .reshape(height, pairs, 3, LANES)
        .transpose(0, 2, 1, 3)
        .reshape(height, 3, width_here),
        pick("out").T,
        jnp.stack([gate, up], axis=1),
        pick("mlp")[:, :hidden_here].T,
        f.sums[:, 0] + f.sums[:, 8],
        f.sums[:, 1] + f.sums[:, 9],
    )


def solution(mesh):
    in_specs = (
        P(("dp", "tensor"), None),
        P("dp", None),
        P("dp", None, "tensor"),
        P("tensor", "dp"),
        P("dp", None, "tensor"),
        P("tensor", "dp"),
        P("dp"),
        P("dp"),
        P(("dp", "tensor"), None),
    )
    out_specs = (
        P(("dp", "tensor"), None),
        P(("dp", "tensor"), None),
        P("dp", None, "tensor"),
        P("tensor", "dp"),
        P("dp", None, "tensor"),
        P("tensor", "dp"),
        P("dp"),
        P("dp"),
    )
    sizes = dict(mesh.shape)
    body = fast_shards if (sizes["dp"], sizes["tensor"]) == (16, 2) else shards
    return jax.shard_map(body, mesh=mesh, in_specs=in_specs, out_specs=out_specs, check_vma=False)
```

```python
import functools
import math
import types

import jax
import jax.numpy as jnp
from jax import lax
from jax.experimental import pallas as pl
from jax.experimental.pallas import tpu as pltpu
from jax.sharding import PartitionSpec as P

HEAD_DIM = 64


EPSILON = 1e-05
ROPE_BASE = 160000.0
NEGATIVE = -1e30
LANES = 128
QUERY_BLOCK = 256
SCALE = 1.0 / math.sqrt(HEAD_DIM)
VMEM_LIMIT = 48 * 1024 * 1024


def seq_starts(offset_row, position):
    before = offset_row[None, :] <= position[:, None]
    return jnp.max(jnp.where(before, offset_row[None, :], 0), axis=1)


def rope_tables(position):
    half_dim = HEAD_DIM // 2
    inverse = jnp.power(
        jnp.float32(ROPE_BASE), -2.0 * jnp.arange(half_dim, dtype=jnp.float32) / HEAD_DIM
    )
    angles = position.astype(jnp.float32)[:, None] * inverse[None, :]
    copies = LANES // half_dim
    cosine = jnp.cos(angles)
    sine = jnp.sin(angles)
    return (
        jnp.concatenate([cosine] * copies, axis=1),
        jnp.concatenate([-sine, sine] * (copies // 2), axis=1),
    )


def levels_of(count):
    out = []
    stride = 1
    while stride < count:
        size = min(4, count // stride)
        out.append((stride, size))
        stride *= size
    return out


def swap_pairs(count, mask):
    return [(place, place ^ mask) for place in range(count)]


def send_step(held, stride, size):
    count = lax.axis_size("dp")
    return [held] + [
        lax.ppermute(held, "dp", swap_pairs(count, step * stride)) for step in range(1, size)
    ]


def place_step(taken, stride, size):
    mine = (lax.axis_index("dp") // stride) % size
    outer, height, width = taken[0].shape
    spread = jnp.zeros((outer, size, height, width), taken[0].dtype)
    for step in range(size):
        spread = lax.dynamic_update_slice(spread, taken[step][:, None], (0, mine ^ step, 0, 0))
    return spread.reshape(outer * size, height, width)


def after(later, *earlier):
    return lax.optimization_barrier((later, *earlier))[0]


def gather_both(first, second):
    one, two = first[None], second[None]
    taken = None
    for level in reversed(levels_of(lax.axis_size("dp"))):
        if taken is not None:
            two = place_step(taken, *last)
        one = place_step(send_step(one, *level), *level)
        taken = send_step(after(two, one), *level)
        last = level
    return one.reshape(-1, one.shape[2]), (taken, last)


def gather_rest(pending, *earlier):
    taken, level = pending
    taken = lax.optimization_barrier((taken, *earlier))[0]
    full = place_step(taken, *level)
    return full.reshape(-1, full.shape[2])


def sum_blocks(terms, *earlier):
    count = lax.axis_size("dp")
    me = lax.axis_index("dp")
    height = terms.shape[0] // count
    width = terms.shape[1]
    held = terms
    for stride, size in levels_of(count):
        mine = (me // stride) % size
        parts = held.reshape(-1, size, height, width)
        pick = lambda place: lax.dynamic_index_in_dim(parts, place, 1, keepdims=False)
        got = [
            lax.ppermute(pick(mine ^ step), "dp", swap_pairs(count, step * stride))
            for step in range(1, size)
        ]
        if earlier:
            got = lax.optimization_barrier((got, *earlier))[0]
            earlier = ()
        total = pick(mine).astype(jnp.float32)
        for other in got:
            total = total + other.astype(jnp.float32)
        held = total.astype(jnp.bfloat16)
    return total.reshape(height, width)


def other_half(local_rows):
    return lax.ppermute(local_rows, "tensor", [(0, 1), (1, 0)])


def spread_rows(local_rows):
    return jnp.concatenate([local_rows, other_half(local_rows)], axis=0)


def collect_own(partial_sums, rows_here):
    sent = other_half(partial_sums[rows_here:].astype(jnp.bfloat16))
    return partial_sums[:rows_here] + sent.astype(jnp.float32)


def collect_all(partial_sums, rows_here):
    got = other_half(partial_sums.astype(jnp.bfloat16))
    swapped = jnp.concatenate([got[rows_here:], got[:rows_here]], axis=0)
    return partial_sums + swapped.astype(jnp.float32)


def norm_parts(inputs_v):
    centre = inputs_v - jnp.mean(inputs_v, axis=-1, keepdims=True)
    spread = jnp.mean(centre * centre, axis=-1, keepdims=True)
    scale_v = lax.rsqrt(spread + EPSILON)
    return centre * scale_v, scale_v


def norm_backward(incoming, gain_v, unit, scale_v):
    scaled = incoming * gain_v
    mean_one = jnp.mean(scaled, axis=-1, keepdims=True)
    mean_two = jnp.mean(scaled * unit, axis=-1, keepdims=True)
    return scale_v * (scaled - mean_one - unit * mean_two)


def two_terms(column):
    high = column.astype(jnp.bfloat16)
    rest = (column - lax.reduce_precision(column, 8, 7)).astype(jnp.bfloat16)
    return jnp.stack([high, rest], axis=1)


def padded(pieces):
    width = sum(piece.shape[1] for piece in pieces)
    short = -width % 128
    height = pieces[0].shape[0]
    if short:
        pieces = pieces + [jnp.zeros((height, short), jnp.bfloat16)]
    return jnp.concatenate(pieces, axis=1)


def dot_nn(left, right):
    return jnp.dot(left, right, preferred_element_type=jnp.float32)


def dot_nt(left, right):
    return lax.dot_general(
        left, right, (((1,), (1,)), ((), ())), preferred_element_type=jnp.float32
    )


def dot_tn(left, right):
    return lax.dot_general(
        left, right, (((0,), (0,)), ((), ())), preferred_element_type=jnp.float32
    )


def turn(rows, cosine, sine_signed, lane):
    half_dim = HEAD_DIM // 2
    ahead = pltpu.roll(rows, rows.shape[1] - half_dim, axis=1)
    behind = pltpu.roll(rows, half_dim, axis=1)
    swapped = jnp.where(lane % HEAD_DIM < half_dim, ahead, behind)
    return rows * cosine + swapped * sine_signed


def forward_kernel(
    normed_ref, wq_ref, wk_ref, wv_ref, cos_ref, sin_ref, srow_ref, scol_ref,
    q_ref, k_ref, v_ref, ctx_ref, lse_ref, vt_ref,
):
    rows = normed_ref.shape[0]
    block = min(QUERY_BLOCK, rows)
    normed = normed_ref[...]
    cosine = cos_ref[...]
    sine = sin_ref[...]
    lane = lax.broadcasted_iota(jnp.int32, (rows, LANES), 1)
    dot = functools.partial(jnp.dot, preferred_element_type=jnp.float32)
    q_ref[...] = turn(dot(normed, wq_ref[...]), cosine, sine, lane).astype(jnp.bfloat16)
    k_ref[...] = turn(dot(normed, wk_ref[...]), cosine, sine, lane).astype(jnp.bfloat16)
    values = dot(normed, wv_ref[...])
    v_ref[...] = values.astype(jnp.bfloat16)
    vt_ref[...] = values.T.astype(jnp.bfloat16)

    @pl.loop(0, rows // block)
    def _(step):
        at = pl.ds(pl.multiple_of(step * block, block), block)
        same = scol_ref[...] == srow_ref[:, at]
        parts = []
        for head in range(LANES // HEAD_DIM):
            cols = slice(head * HEAD_DIM, (head + 1) * HEAD_DIM)
            scores = dot_nt(k_ref[:, cols], q_ref[at, cols]) * SCALE
            scores = jnp.where(same, scores, NEGATIVE)
            top = jnp.max(scores, axis=0, keepdims=True)
            terms = jnp.exp(scores - top)
            total = jnp.sum(terms, axis=0, keepdims=True)
            weights = (terms * (1.0 / total)).astype(jnp.bfloat16)
            parts.append(dot(vt_ref[cols, :], weights))
            lse_ref[0, head : head + 1, at] = top + jnp.log(total)
        ctx_ref[at, :] = jnp.concatenate(parts, axis=0).T.astype(jnp.bfloat16)


def backward_kernel(
    grad_ref, wo_ref, q_ref, k_ref, v_ref, cos_ref, sin_ref, srow_ref, scol_ref, lse_ref,
    dq_ref, dk_ref, dv_ref, g_ref, kt_ref, acc_q, acc_k, acc_v,
):
    rows = grad_ref.shape[0]
    block = min(QUERY_BLOCK, rows)
    dot = functools.partial(jnp.dot, preferred_element_type=jnp.float32)
    g_ref[...] = dot(grad_ref[...], wo_ref[...]).astype(jnp.bfloat16)
    kt_ref[...] = k_ref[...].astype(jnp.float32).T.astype(jnp.bfloat16)
    acc_k[...] = jnp.zeros_like(acc_k)
    acc_v[...] = jnp.zeros_like(acc_v)

    @pl.loop(0, rows // block)
    def _(step):
        at = pl.ds(pl.multiple_of(step * block, block), block)
        same = scol_ref[...] == srow_ref[:, at]
        parts = []
        for head in range(LANES // HEAD_DIM):
            cols = slice(head * HEAD_DIM, (head + 1) * HEAD_DIM)
            query = q_ref[at, cols]
            grad = g_ref[at, cols]
            scores = dot_nt(k_ref[:, cols], query) * SCALE
            probs = jnp.exp(jnp.where(same, scores - lse_ref[0, head : head + 1, at], NEGATIVE))
            acc_v[:, cols] += dot(probs.astype(jnp.bfloat16), grad)
            grad_probs = dot_nt(v_ref[:, cols], grad)
            weighted = probs * grad_probs
            drop = jnp.sum(weighted, axis=0, keepdims=True)
            grad_scores = (weighted - probs * drop).astype(jnp.bfloat16)
            acc_k[:, cols] += dot(grad_scores, query)
            parts.append(dot(kt_ref[cols, :], grad_scores))
        acc_q[at, :] = jnp.concatenate(parts, axis=0).T

    cosine = cos_ref[...] * SCALE
    sine = sin_ref[...] * -SCALE
    lane = lax.broadcasted_iota(jnp.int32, (rows, LANES), 1)
    dq_ref[...] = turn(acc_q[...], cosine, sine, lane).astype(jnp.bfloat16)
    dk_ref[...] = turn(acc_k[...], cosine, sine, lane).astype(jnp.bfloat16)
    dv_ref[...] = acc_v[...].astype(jnp.bfloat16)


def whole(shape):
    return pl.BlockSpec(shape, lambda pair: (0,) * len(shape))


def column_block(rows, first):
    return pl.BlockSpec((rows, LANES), lambda pair: (0, first + pair))


def attention_forward(normed_all, attn_pack, cosine, sine, starts, width_here):
    rows, width = normed_all.shape
    pairs = width_here // LANES
    heads_each = LANES // HEAD_DIM
    low = jax.ShapeDtypeStruct((rows, width_here), jnp.bfloat16)
    return pl.pallas_call(
        forward_kernel,
        grid=(pairs,),
        out_shape=(low, low, low, low, jax.ShapeDtypeStruct((pairs, heads_each, rows), jnp.float32)),
        in_specs=[
            whole((rows, width)),
            column_block(width, 0),
            column_block(width, pairs),
            column_block(width, 2 * pairs),
            whole((rows, LANES)),
            whole((rows, LANES)),
            whole((1, rows)),
            whole((rows, 1)),
        ],
        out_specs=[column_block(rows, 0)] * 4
        + [pl.BlockSpec((1, heads_each, rows), lambda pair: (pair, 0, 0))],
        scratch_shapes=[pltpu.VMEM((LANES, rows), jnp.bfloat16)],
        compiler_params=pltpu.CompilerParams(vmem_limit_bytes=VMEM_LIMIT),
        cost_estimate=pl.CostEstimate(
            flops=2 * rows * width * 3 * width_here + 4 * rows * rows * width_here,
            bytes_accessed=2 * (rows * width + 3 * width * width_here + 4 * rows * width_here),
            transcendentals=rows * rows * width_here // HEAD_DIM,
        ),
    )(normed_all, attn_pack, attn_pack, attn_pack, cosine, sine, starts[None, :], starts[:, None])


def attention_backward(grad_rows, attn_pack, queries, key_rows, values, cosine, sine, starts, lse):
    rows, width = grad_rows.shape
    width_here = queries.shape[1]
    pairs = width_here // LANES
    heads_each = LANES // HEAD_DIM
    low = jax.ShapeDtypeStruct((rows, width_here), jnp.bfloat16)
    return pl.pallas_call(
        backward_kernel,
        grid=(pairs,),
        out_shape=(low, low, low),
        in_specs=[
            whole((rows, width)),
            column_block(width, 0),
            column_block(rows, 0),
            column_block(rows, 0),
            column_block(rows, 0),
            whole((rows, LANES)),
            whole((rows, LANES)),
            whole((1, rows)),
            whole((rows, 1)),
            pl.BlockSpec((1, heads_each, rows), lambda pair: (pair, 0, 0)),
        ],
        out_specs=[column_block(rows, 0)] * 3,
        scratch_shapes=[
            pltpu.VMEM((rows, LANES), jnp.bfloat16),
            pltpu.VMEM((LANES, rows), jnp.bfloat16),
            pltpu.VMEM((rows, LANES), jnp.float32),
            pltpu.VMEM((rows, LANES), jnp.float32),
            pltpu.VMEM((rows, LANES), jnp.float32),
        ],
        compiler_params=pltpu.CompilerParams(vmem_limit_bytes=VMEM_LIMIT),
        cost_estimate=pl.CostEstimate(
            flops=2 * rows * width * width_here + 10 * rows * rows * width_here,
            bytes_accessed=2 * (rows * width + width * width_here + 7 * rows * width_here),
            transcendentals=rows * rows * width_here // HEAD_DIM,
        ),
    )(
        grad_rows, attn_pack, queries, key_rows, values, cosine, sine,
        starts[None, :], starts[:, None], lse,
    )


def shards(tokens, offsets, w_qkv, w_attn_out, w_in, w_mlp_out, gain_attn, gain_mlp, cotangent):
    rows_here = tokens.shape[0]
    group_rows = rows_here * lax.axis_size("tensor")
    model_here = w_qkv.shape[0]
    width_here = w_qkv.shape[2]
    hidden_here = w_in.shape[2]
    half_at = lax.axis_index("tensor") * rows_here
    position = (jnp.arange(group_rows, dtype=jnp.int32) + half_at) % group_rows
    starts = seq_starts(offsets[0], position)
    cosine_tab, sine_tab = rope_tables(position - starts)

    attn_pack, pending = gather_both(
        padded([w_qkv.reshape(model_here, 3 * width_here), gain_attn[:, None]]),
        padded(
            [w_attn_out.T, w_in.reshape(model_here, 2 * hidden_here), w_mlp_out.T, gain_mlp[:, None]]
        ),
    )
    gain_one = attn_pack[:, 3 * width_here].astype(jnp.float32)
    qkv_full = attn_pack[:, : 3 * width_here]

    token_rows = spread_rows(tokens)
    cotangent_rows = spread_rows(cotangent)
    grad_rows = cotangent_rows.astype(jnp.bfloat16)
    unit_one, scale_one = norm_parts(token_rows)
    normed_all = (unit_one * gain_one).astype(jnp.bfloat16)
    queries, key_rows, values, context, lse = attention_forward(
        normed_all, attn_pack, cosine_tab, sine_tab, starts, width_here
    )

    rest_pack = gather_rest(pending, lse)
    mlp_at = width_here
    mlp_end = width_here + 2 * hidden_here
    attn_out_full = rest_pack[:, :width_here]
    mlp_in_full = rest_pack[:, mlp_at:mlp_end]
    mlp_out_full = rest_pack[:, mlp_end : mlp_end + hidden_here]
    gain_two = rest_pack[:, mlp_end + hidden_here].astype(jnp.float32)
    attended = collect_all(dot_nt(context, attn_out_full), rows_here)
    hidden = token_rows + attended
    unit_two, scale_two = norm_parts(hidden)
    mlp_rows = (unit_two * gain_two).astype(jnp.bfloat16)
    gate_part = dot_nn(mlp_rows, mlp_in_full[:, :hidden_here])
    up_part = dot_nn(mlp_rows, mlp_in_full[:, hidden_here:])
    grad_product = dot_nn(grad_rows, mlp_out_full)
    bell = 0.5 * (1.0 + lax.erf(gate_part * math.sqrt(0.5)))
    activated = gate_part * bell
    slope = bell + gate_part * jnp.exp(-0.5 * gate_part * gate_part) * (1.0 / math.sqrt(2 * math.pi))
    product_rows = (activated * up_part).astype(jnp.bfloat16)
    grad_gate_up = jnp.concatenate(
        [
            (grad_product * up_part * slope).astype(jnp.bfloat16),
            (grad_product * activated).astype(jnp.bfloat16),
        ],
        axis=1,
    )
    grad_normed_two = collect_all(dot_nt(grad_gate_up, mlp_in_full), rows_here)
    grad_hidden = cotangent_rows + norm_backward(grad_normed_two, gain_two, unit_two, scale_two)
    grad_gain_two = jnp.sum((grad_normed_two * unit_two)[:rows_here], axis=0)
    grad_hidden_rows = grad_hidden.astype(jnp.bfloat16)
    grads_three = attention_backward(
        grad_hidden_rows, rest_pack, queries, key_rows, values,
        cosine_tab, sine_tab, starts, lse,
    )
    mlp_terms = padded(
        [
            dot_tn(mlp_rows, grad_gate_up).astype(jnp.bfloat16),
            dot_tn(grad_rows, product_rows).astype(jnp.bfloat16),
            two_terms(grad_gain_two),
        ]
    )
    mlp_sums = sum_blocks(mlp_terms, grads_three[0])
    branch = collect_own(dot_nt(product_rows, mlp_out_full), rows_here)
    outputs = hidden[:rows_here] + branch

    grad_projected = jnp.concatenate(grads_three, axis=1)
    grad_normed_one = collect_own(dot_nt(grad_projected, qkv_full), rows_here)
    grad_tokens = grad_hidden[:rows_here] + norm_backward(
        grad_normed_one, gain_one, unit_one[:rows_here], scale_one[:rows_here]
    )
    grad_gain_one = jnp.sum(grad_normed_one * unit_one[:rows_here], axis=0)
    attn_terms = padded(
        [
            dot_tn(normed_all, grad_projected).astype(jnp.bfloat16),
            dot_tn(grad_hidden_rows, context).astype(jnp.bfloat16),
            two_terms(grad_gain_one),
        ]
    )
    attn_sums = sum_blocks(attn_terms)

    gain_one_cols = attn_sums[:, 4 * width_here : 4 * width_here + 2].sum(axis=1)
    gain_two_cols = mlp_sums[:, 3 * hidden_here : 3 * hidden_here + 2].sum(axis=1)
    gains = jnp.stack([gain_one_cols, gain_two_cols])
    gains = gains + other_half(gains)
    return (
        outputs,
        grad_tokens,
        attn_sums[:, : 3 * width_here].reshape(model_here, 3, width_here),
        attn_sums[:, 3 * width_here : 4 * width_here].T,
        mlp_sums[:, : 2 * hidden_here].reshape(model_here, 2, hidden_here),
        mlp_sums[:, 2 * hidden_here : 3 * hidden_here].T,
        gains[0],
        gains[1],
    )


def fast_columns(width_here, hidden_here):
    main = hidden_here // LANES * LANES
    pairs = width_here // LANES
    at = {"gains": (0, LANES)}
    place = LANES
    for pair in range(pairs):
        at["pair%d" % pair] = (place, 3 * LANES)
        place += 3 * LANES
    for name, size in (
        ("out", width_here), ("mlp", main + LANES), ("gate", main), ("up", main), ("tail", LANES),
    ):
        at[name] = (place, size)
        place += size
    at["total"] = (0, place)
    return at


def pack_shards(w_qkv, w_attn_out, w_in, w_mlp_out, gain_attn, gain_mlp):
    height, _, width_here = w_qkv.shape
    hidden_here = w_in.shape[2]
    main = hidden_here // LANES * LANES
    pairs = width_here // LANES
    gains = jnp.concatenate(
        [gain_attn[:, None], gain_mlp[:, None], jnp.zeros((height, LANES - 2), jnp.bfloat16)], axis=1
    )
    by_pair = w_qkv.reshape(height, 3, pairs, LANES).transpose(0, 2, 1, 3)
    short = main + LANES - hidden_here
    return jnp.concatenate(
        [
            gains,
            by_pair.reshape(height, 3 * width_here),
            w_attn_out.T,
            w_mlp_out.T,
            jnp.zeros((height, short), jnp.bfloat16),
            w_in[:, 0, :main],
            w_in[:, 1, :main],
            w_in[:, 0, main:],
            w_in[:, 1, main:],
        ],
        axis=1,
    )


class Links:
    def __init__(self, ref):
        self.ref = ref
        self.dp = lax.axis_index("dp")
        self.core = lax.axis_index("tensor")
        self.x = self.dp % 2
        self.y = (self.dp // 2) % 2
        self.z = self.dp // 4
        plane = self.dp % 4
        self.x_side = self.dp + 1 - 2 * self.x
        self.y_side = self.dp + 2 - 4 * self.y
        self.z_of = [None, self.z + 1 - 2 * (self.z % 2), (self.z + 2) % 4, 3 - self.z]
        self.z_side = [None] + [place * 4 + plane for place in self.z_of[1:]]
        self.started = []

    def enter(self):
        barrier = pltpu.get_barrier_semaphore()
        others = [(self.x_side, self.core), (self.y_side, self.core), (self.dp, 1 - self.core)]
        others += [(place, self.core) for place in self.z_side[1:]]
        for other in others:
            pl.semaphore_signal(
                barrier, inc=1, device_id=other, device_id_type=pl.DeviceIdType.MESH
            )
        pl.semaphore_wait(barrier, len(others))

    def copy(self, source, target, sems, place, device):
        return pltpu.make_async_remote_copy(
            src_ref=source,
            dst_ref=target,
            send_sem=sems[0].at[place],
            recv_sem=sems[1].at[place],
            device_id=device,
            device_id_type=pl.DeviceIdType.MESH,
        )

    def start(self, *copies):
        for copy in copies:
            copy.start()
            self.started.append(copy)

    def to_core(self, source, target, place):
        copy = self.copy(
            source, target, (self.ref.core_out, self.ref.core_in), place, (self.dp, 1 - self.core)
        )
        self.start(copy)
        return copy

    def finish(self):
        for copy in self.started:
            copy.wait_send()
        self.started = []


class Gather(Links):
    def __init__(self, ref, chunks):
        super().__init__(ref)
        self.chunks = chunks
        self.got = {}

    def send_z(self, name):
        chunk = list(self.chunks).index(name)
        cols = pl.ds(*self.chunks[name])
        block = self.ref.full.at[self.z, self.y, self.x, :, cols]
        copies = [
            self.copy(
                block, block, (self.ref.far_out, self.ref.far_in), 3 * chunk + step - 1,
                (self.z_side[step], self.core),
            )
            for step in (1, 2, 3)
        ]
        self.start(*copies)
        self.got[name] = copies

    def arrive(self, name):
        for copy in self.got[name]:
            copy.wait_recv()

    def near(self, name, stage, first, second):
        chunk = list(self.chunks).index(name)
        sems = (self.ref.near_out, self.ref.near_in)
        place = 4 * chunk + 2 * stage
        copies = [
            self.copy(first[0], first[0], sems, place, (first[1], self.core)),
            self.copy(second[0], second[0], sems, place + 1, (second[1], self.core)),
        ]
        self.arrive(name)
        self.start(*copies)
        self.got[name] = copies

    def send_one(self, name):
        cols = pl.ds(*self.chunks[name])
        low, high = pl.ds(0, 2), pl.ds(2, 2)
        full = self.ref.full
        self.near(
            name, 0,
            (full.at[low, self.y, self.x, :, cols], self.x_side),
            (full.at[high, self.y, self.x, :, cols], self.y_side),
        )

    def send_two(self, name):
        cols = pl.ds(*self.chunks[name])
        low, high = pl.ds(0, 2), pl.ds(2, 2)
        both = pl.ds(0, 2)
        full = self.ref.full
        self.near(
            name, 1,
            (full.at[low, self.y, both, :, cols], self.y_side),
            (full.at[high, both, self.x, :, cols], self.x_side),
        )


class Scatter:
    def __init__(self, link, chunks):
        self.link = link
        self.ref = link.ref
        self.chunks = chunks
        self.got = {}

    def send(self, name, stage, moves):
        sems = (self.ref.sum_out, self.ref.sum_in)
        place = 7 * list(self.chunks).index(name) + 2 * stage
        copies = [
            self.link.copy(source, target, sems, place + step, (side, self.link.core))
            for step, (source, target, side) in enumerate(moves)
        ]
        self.link.start(*copies)
        self.got[name] = copies

    def arrive(self, name):
        for copy in self.got[name]:
            copy.wait_recv()

    def parts(self, name):
        held, span, place = self.chunks[name]
        return held, pl.ds(*span), pl.ds(place, span[1])

    def one(self, name):
        link, ref = self.link, self.ref
        held, cols, to = self.parts(name)
        both = pl.ds(0, 2)
        self.send(name, 0, [
            (held.at[pl.ds(0, 2), 1 - link.y, both, :, cols], ref.low_one.at[:, :, :, to], link.y_side),
            (held.at[pl.ds(2, 2), both, 1 - link.x, :, cols], ref.high_one.at[:, :, :, to], link.x_side),
        ])

    def two(self, name):
        link, ref = self.link, self.ref
        held, cols, to = self.parts(name)
        both = pl.ds(0, 2)
        self.arrive(name)
        at = (pl.ds(0, 2), link.y, both, slice(None), cols)
        held[at] = held[at] + ref.low_one[:, :, :, to]
        at = (pl.ds(2, 2), both, link.x, slice(None), cols)
        held[at] = held[at] + ref.high_one[:, :, :, to]
        self.send(name, 1, [
            (held.at[pl.ds(0, 2), link.y, 1 - link.x, :, cols], ref.low_two.at[:, :, to], link.x_side),
            (held.at[pl.ds(2, 2), 1 - link.y, link.x, :, cols], ref.high_two.at[:, :, to], link.y_side),
        ])

    def three(self, name):
        link, ref = self.link, self.ref
        held, cols, to = self.parts(name)
        self.arrive(name)
        at = (pl.ds(0, 2), link.y, link.x, slice(None), cols)
        held[at] = held[at] + ref.low_two[:, :, to]
        at = (pl.ds(2, 2), link.y, link.x, slice(None), cols)
        held[at] = held[at] + ref.high_two[:, :, to]
        self.send(name, 2, [
            (
                held.at[link.z_of[step], link.y, link.x, :, cols],
                ref.far_sum.at[step - 1, :, to],
                link.z_side[step],
            )
            for step in (1, 2, 3)
        ])

    def four(self, name):
        link, ref = self.link, self.ref
        held, cols, to = self.parts(name)
        self.arrive(name)
        total = held[link.z, link.y, link.x, :, cols].astype(jnp.float32)
        for step in range(3):
            total = total + ref.far_sum[step, :, to].astype(jnp.float32)
        ref.sums[:, to] = total


def weights_at(full, span):
    block = full[:, :, :, :, span[0] : span[0] + span[1]]
    return block.reshape(-1, span[1])


def row_loop(rows, block):
    def wrap(body):
        @pl.loop(0, rows // block)
        def _(step):
            body(pl.ds(pl.multiple_of(step * block, block), block))

    return wrap


def layer_kernel(names, spans, *refs):
    ref = types.SimpleNamespace(**dict(zip(names, refs)))
    half, width = ref.tok.shape
    rows = 2 * half
    pairs = (spans["out"][1]) // LANES
    main = spans["gate"][1]
    chunk_names = ["gains"] + ["pair%d" % pair for pair in range(pairs)] + ["out", "mlp"]
    chunks = {name: spans[name] for name in chunk_names}
    chunks["gate"] = spans["gate"]
    chunks["up"] = (spans["up"][0], main + LANES)
    link = Gather(ref, chunks)
    core = link.core
    own = pl.ds(pl.multiple_of(core * half, half), half)
    own_at = core * half
    other_at = (1 - core) * half
    part = 256

    ref.grad_low = ref.normed
    ref.grad_context = ref.product.at[:, : pairs * LANES]
    ref.grad_three = ref.product.at[:, : 3 * LANES]
    ref.grad_projected = ref.grad_gate_up
    ref.acc = ref.grad_product.at[:, : 3 * LANES]
    scatter = Scatter(
        link,
        {
            "inner": (ref.grad_inner, (0, 2 * main + LANES), spans["gate"][0]),
            "mlp": (ref.full, spans["mlp"], spans["mlp"][0]),
            "out": (ref.full, spans["out"], spans["out"][0]),
            **{
                "pair%d" % pair: (
                    ref.full,
                    (spans["gate"][0] + 3 * LANES * pair, 3 * LANES),
                    spans["pair%d" % pair][0],
                )
                for pair in range(pairs)
            },
            "gains": (ref.full, spans["gains"], spans["gains"][0]),
        },
    )

    link.enter()
    ref.full[link.z, link.y, link.x] = ref.pack[...]
    link.send_z("gains")
    link.send_z("pair0")
    link.send_z("pair1")

    @row_loop(half, 128)
    def _(at):
        unit, scale = norm_parts(ref.tok[at, :])
        ref.unit_one[at, :] = unit
        ref.scale_one[at, :] = jnp.broadcast_to(scale, (128, LANES))

    link.send_one("gains")

    shift = jnp.int32(0)
    for slot in range(ref.offsets.shape[1]):
        entry = ref.offsets[0, slot]
        shift = jnp.maximum(shift, jnp.where(entry <= half - 1, entry, 0))

    def source_of(place):
        moved = place + shift
        return jnp.where(moved >= rows, moved - rows, moved)

    def start_of(place):
        start = jnp.zeros_like(place)
        for slot in range(ref.offsets.shape[1]):
            entry = ref.offsets[0, slot]
            start = jnp.maximum(start, jnp.where(place >= entry, entry, 0))
        return start

    @row_loop(rows, part)
    def _(at):
        down = source_of(lax.broadcasted_iota(jnp.int32, (part, 1), 0) + at.start)
        along = lax.broadcasted_iota(jnp.int32, (part, rows), 1)
        ref.perm[at, :] = jnp.where(down == along, 1.0, 0.0).astype(jnp.bfloat16)
        down = lax.broadcasted_iota(jnp.int32, (part, rows), 0) + at.start
        along = source_of(lax.broadcasted_iota(jnp.int32, (1, rows), 1))
        ref.perm_back[at, :] = jnp.where(down == along, 1.0, 0.0).astype(jnp.bfloat16)

    link.send_two("gains")
    link.send_one("pair0")
    link.send_z("pair2")

    @row_loop(half, 128)
    def _(at):
        here = pl.ds(pl.multiple_of(own_at + at.start, 128), 128)
        ref.grad_rows[here, :] = ref.cot[at, :].astype(jnp.bfloat16)

    def table(at):
        place = source_of(lax.broadcasted_iota(jnp.int32, (part, LANES), 0) + at.start)
        start = start_of(place)
        angle = (place - start).astype(jnp.float32) * ref.inverse[...]
        lane = lax.broadcasted_iota(jnp.int32, (part, LANES), 1)
        sine = jnp.sin(angle)
        ref.cosine[at, :] = jnp.cos(angle)
        ref.sine[at, :] = jnp.where(lane % HEAD_DIM < HEAD_DIM // 2, -sine, sine)

    row_loop(half, part)(table)
    link.arrive("gains")
    slot = lax.broadcasted_iota(jnp.int32, (8, LANES), 0)
    lane = lax.broadcasted_iota(jnp.int32, (8, LANES), 1)
    pick = jnp.where(slot == lane, 1.0, 0.0).astype(jnp.bfloat16)
    ref.gain[...] = dot_nt(pick, weights_at(ref.full, spans["gains"]))

    @row_loop(half, 128)
    def _(at):
        here = pl.ds(pl.multiple_of(own_at + at.start, 128), 128)
        ref.normed[here, :] = (ref.unit_one[at, :] * ref.gain[0:1, :]).astype(jnp.bfloat16)

    got_normed = link.to_core(ref.normed.at[own, :], ref.normed.at[own, :], 1)
    got_grad = link.to_core(ref.grad_rows.at[own, :], ref.grad_rows.at[own, :], 0)
    link.send_one("pair1")
    link.send_z("out")

    @row_loop(half, part)
    def _(at):
        table(pl.ds(pl.multiple_of(half + at.start, part), part))

    key_start = start_of(source_of(lax.broadcasted_iota(jnp.int32, (half, 1), 0) + half))
    query_start = start_of(source_of(lax.broadcasted_iota(jnp.int32, (1, half), 1) + half))
    ref.bias[...] = jnp.where(key_start == query_start, 0.0, NEGATIVE)
    got_normed.wait_recv()
    link.send_two("pair0")

    @row_loop(rows, part)
    def _(at):
        ref.rolled[at, :] = dot_nn(ref.perm[at, :], ref.normed[...]).astype(jnp.bfloat16)

    link.send_one("pair2")
    link.send_z("mlp")

    def project(pair):
        if pair:
            link.arrive("pair%d" % pair)
        cols = slice(pair * LANES, (pair + 1) * LANES)

        @row_loop(rows, part)
        def _(at):
            three = dot_nn(ref.rolled[at, :], weights_at(ref.full, spans["pair%d" % pair]))
            lane = lax.broadcasted_iota(jnp.int32, (part, LANES), 1)
            cosine, sine = ref.cosine[at, :], ref.sine[at, :]
            query = turn(three[:, :LANES], cosine, sine, lane) * SCALE
            ref.queries[at, cols] = query.astype(jnp.bfloat16)
            ref.keys[at, cols] = turn(
                three[:, LANES : 2 * LANES], cosine, sine, lane
            ).astype(jnp.bfloat16)
            ref.values[at, cols] = three[:, 2 * LANES :].astype(jnp.bfloat16)
            ref.values_t[:, at] = three[:, 2 * LANES :].T.astype(jnp.bfloat16)

    def unit_of(pair, head, first):
        return (pair * (LANES // HEAD_DIM) + head) * 2 + (0 if first else 1)

    def attend(pair, first):
        cols = slice(pair * LANES, (pair + 1) * LANES)
        base = 0 if first else half

        for step in range(half // part):
            at = pl.ds(base + step * part, part)
            query_pair = ref.queries[at, cols]
            lane = lax.broadcasted_iota(jnp.int32, (part, LANES), 1)
            parts = []
            for head in range(LANES // HEAD_DIM):
                query = jnp.where(lane // HEAD_DIM == head, query_pair, 0)
                scores = dot_nt(ref.keys[base : base + half, cols], query)
                if not first:
                    scores = scores + ref.bias[:, step * part : (step + 1) * part]
                top = jnp.max(scores, axis=0, keepdims=True)
                terms = jnp.exp(scores - top)
                total = jnp.sum(terms, axis=0, keepdims=True)
                probs = (terms * (1.0 / total)).astype(jnp.bfloat16)
                ref.probs[
                    unit_of(pair, head, first), :, step * part : (step + 1) * part
                ] = probs
                parts.append(
                    dot_nn(
                        ref.values_t[head * HEAD_DIM : (head + 1) * HEAD_DIM, base : base + half],
                        probs,
                    )
                )
            ref.context_rolled[at, cols] = jnp.concatenate(parts, axis=0).T.astype(jnp.bfloat16)

    link.arrive("pair0")
    link.send_two("pair1")
    link.send_z("gate")
    project(0)
    link.send_one("out")
    attend(0, True)
    link.send_two("pair2")
    link.send_z("up")
    attend(0, False)
    link.send_one("mlp")
    project(1)
    link.send_two("out")
    attend(1, True)
    link.send_one("gate")
    attend(1, False)
    link.send_two("mlp")
    project(2)
    link.send_one("up")
    attend(2, True)
    link.send_two("gate")
    attend(2, False)

    @row_loop(rows, part)
    def _(at):
        ref.context[at, :] = dot_nn(ref.perm_back[at, :], ref.context_rolled[...]).astype(jnp.bfloat16)

    link.send_two("up")
    link.arrive("out")

    def pair_sum(product, place, sem, keep):
        @row_loop(half, part)
        def _(at):
            there = pl.ds(pl.multiple_of(other_at + at.start, part), part)
            ref.sent[place, at, :] = product(there).astype(jnp.bfloat16)

        got = link.to_core(ref.sent.at[place], ref.taken.at[place], sem)

        @row_loop(half, part)
        def _(at):
            here = pl.ds(pl.multiple_of(own_at + at.start, part), part)
            keep[at, :] = product(here)

        return got

    got_attended = pair_sum(
        lambda at: dot_nt(ref.context[at, :], weights_at(ref.full, spans["out"])), 0, 2, ref.hidden
    )
    got_attended.wait_recv()

    @row_loop(half, 128)
    def _(at):
        hidden = ref.tok[at, :] + ref.hidden[at, :] + ref.taken[0, at, :].astype(jnp.float32)
        ref.hidden[at, :] = hidden
        unit, scale = norm_parts(hidden)
        ref.unit_two[at, :] = unit
        ref.scale_two[at, :] = jnp.broadcast_to(scale, (128, LANES))
        here = pl.ds(pl.multiple_of(own_at + at.start, 128), 128)
        ref.normed_mlp[here, :] = (unit * ref.gain[1:2, :]).astype(jnp.bfloat16)

    got_mlp = link.to_core(ref.normed_mlp.at[own, :], ref.normed_mlp.at[own, :], 6)
    got_grad.wait_recv()
    link.arrive("mlp")

    @row_loop(rows, part)
    def _(at):
        ref.grad_product[at, :] = dot_nn(ref.grad_rows[at, :], weights_at(ref.full, spans["mlp"]))

    got_mlp.wait_recv()
    link.arrive("gate")
    link.arrive("up")

    def gated(gate, up, grad):
        bell = 0.5 * (1.0 + lax.erf(gate * math.sqrt(0.5)))
        activated = gate * bell
        slope = bell + gate * jnp.exp(-0.5 * gate * gate) * (1.0 / math.sqrt(2 * math.pi))
        return activated * up, grad * up * slope, grad * activated

    @row_loop(rows, part)
    def _(at):
        low = ref.normed_mlp[at, :]
        gate = dot_nn(low, weights_at(ref.full, spans["gate"]))
        up = dot_nn(low, weights_at(ref.full, spans["up"]))
        product, grad_gate, grad_up = gated(gate, up, ref.grad_product[at, :main])
        ref.product[at, :main] = product.astype(jnp.bfloat16)
        ref.grad_gate_up[at, :main] = grad_gate.astype(jnp.bfloat16)
        ref.grad_gate_up[at, main : 2 * main] = grad_up.astype(jnp.bfloat16)
        tail = dot_nn(low, weights_at(ref.full, spans["tail"]))
        product, grad_gate, grad_up = gated(
            tail, pltpu.roll(tail, LANES // 2, axis=1), ref.grad_product[at, main:]
        )
        lane = lax.broadcasted_iota(jnp.int32, (part, LANES), 1)
        lower = lane < LANES // 2
        ref.product[at, main:] = jnp.where(lower, product, 0.0).astype(jnp.bfloat16)
        ref.grad_gate_up[at, 2 * main :] = jnp.where(
            lower, grad_gate, pltpu.roll(grad_up, LANES // 2, axis=1)
        ).astype(jnp.bfloat16)

    inner = (spans["gate"][0], 2 * main + LANES)
    link.finish()

    def weight_grad(left, right, held, first):
        wide = right.shape[1]

        @pl.loop(0, 2)
        def _(step):
            cols = pl.ds(pl.multiple_of(step * (width // 2), LANES), width // 2)
            block = dot_tn(left[:, cols], right[...]).astype(jnp.bfloat16)
            held[pl.ds(2 * step, 2), :, :, :, first : first + wide] = block.reshape(
                2, 2, 2, width // 16, wide
            )

    weight_grad(ref.normed_mlp, ref.grad_gate_up, ref.grad_inner, 0)
    scatter.one("inner")
    got_normed_two = pair_sum(
        lambda at: dot_nt(ref.grad_gate_up[at, :], weights_at(ref.full, inner)), 1, 3, ref.grad_hidden
    )
    got_branch = pair_sum(
        lambda at: dot_nt(ref.product[at, :], weights_at(ref.full, spans["mlp"])), 2, 4, ref.outputs
    )
    got_normed_two.wait_recv()
    ref.gain_rows[...] = jnp.zeros_like(ref.gain_rows)

    @row_loop(half, 128)
    def _(at):
        incoming = ref.grad_hidden[at, :] + ref.taken[1, at, :].astype(jnp.float32)
        unit = ref.unit_two[at, :]
        ref.gain_rows[1:2, :] += jnp.sum(incoming * unit, axis=0, keepdims=True)
        grad = ref.cot[at, :] + norm_backward(
            incoming, ref.gain[1:2, :], unit, ref.scale_two[at, 0:1]
        )
        ref.grad_hidden[at, :] = grad
        here = pl.ds(pl.multiple_of(own_at + at.start, 128), 128)
        ref.grad_low[here, :] = grad.astype(jnp.bfloat16)

    got_low = link.to_core(ref.grad_low.at[own, :], ref.grad_low.at[own, :], 7)
    weight_grad(ref.grad_rows, ref.product, ref.full, spans["mlp"][0])
    scatter.one("mlp")
    got_branch.wait_recv()

    @row_loop(half, 128)
    def _(at):
        ref.outputs[at, :] = (
            ref.outputs[at, :] + ref.hidden[at, :] + ref.taken[2, at, :].astype(jnp.float32)
        )

    got_low.wait_recv()

    @row_loop(rows, part)
    def _(at):
        ref.grad_context[at, :] = dot_nn(
            ref.grad_low[at, :], weights_at(ref.full, spans["out"])
        ).astype(jnp.bfloat16)

    @row_loop(rows, part)
    def _(at):
        ref.grad_rolled[at, :] = dot_nn(ref.perm[at, :], ref.grad_context[...]).astype(jnp.bfloat16)

    weight_grad(ref.grad_low, ref.context, ref.full, spans["out"][0])
    scatter.one("out")
    scatter.two("inner")

    def pull(pair, first):
        cols = slice(pair * LANES, (pair + 1) * LANES)
        base = 0 if first else half
        span = slice(base, base + half)

        @row_loop(half, part)
        def _(at):
            at = pl.ds(pl.multiple_of(base + at.start, part), part)
            ref.keys_t[:, at] = ref.keys[at, cols].astype(jnp.float32).T.astype(jnp.bfloat16)

        for step in range(half // part):
            at = pl.ds(base + step * part, part)
            lane = lax.broadcasted_iota(jnp.int32, (part, LANES), 1)
            query_pair = ref.queries[at, cols]
            grad_pair = ref.grad_rolled[at, cols]
            product = grad_pair.astype(jnp.float32) * ref.context_rolled[at, cols].astype(jnp.float32)
            product = product.T
            parts, all_probs, all_grads, all_queries, all_pulls = [], [], [], [], []
            for head in range(LANES // HEAD_DIM):
                query = jnp.where(lane // HEAD_DIM == head, query_pair, 0)
                grad = jnp.where(lane // HEAD_DIM == head, grad_pair, 0)
                probs = ref.probs[
                    unit_of(pair, head, first), :, step * part : (step + 1) * part
                ]
                grad_probs = dot_nt(ref.values[span, cols], grad)
                drop = jnp.sum(
                    product[head * HEAD_DIM : (head + 1) * HEAD_DIM], axis=0, keepdims=True
                )
                pulled = (probs.astype(jnp.float32) * (grad_probs - drop)).astype(jnp.bfloat16)
                all_probs.append(probs)
                all_grads.append(grad)
                all_queries.append(query)
                all_pulls.append(pulled)
                parts.append(
                    dot_nn(ref.keys_t[head * HEAD_DIM : (head + 1) * HEAD_DIM, span], pulled)
                )
            grad_values = dot_nn(
                jnp.concatenate(all_probs, axis=1), jnp.concatenate(all_grads, axis=0)
            )
            grad_keys = dot_nn(
                jnp.concatenate(all_pulls, axis=1), jnp.concatenate(all_queries, axis=0)
            )

            if step == 0:
                ref.acc[span, LANES : 2 * LANES] = grad_keys
                ref.acc[span, 2 * LANES :] = grad_values
            else:
                ref.acc[span, LANES : 2 * LANES] += grad_keys
                ref.acc[span, 2 * LANES :] += grad_values

            ref.acc[at, :LANES] = jnp.concatenate(parts, axis=0).T

    def unproject(pair):
        first = 3 * LANES * pair

        @row_loop(rows, part)
        def _(at):
            lane = lax.broadcasted_iota(jnp.int32, (part, LANES), 1)
            cosine, sine = ref.cosine[at, :], -ref.sine[at, :]
            grad_query = turn(ref.acc[at, :LANES], cosine, sine, lane) * SCALE
            grad_key = turn(ref.acc[at, LANES : 2 * LANES], cosine, sine, lane)
            ref.grad_three[at, :LANES] = grad_query.astype(jnp.bfloat16)
            ref.grad_three[at, LANES : 2 * LANES] = grad_key.astype(jnp.bfloat16)
            ref.grad_three[at, 2 * LANES :] = ref.acc[at, 2 * LANES :].astype(jnp.bfloat16)

        weight_grad(ref.rolled, ref.grad_three, ref.full, spans["gate"][0] + first)
        scatter.one("pair%d" % pair)

        @row_loop(rows, part)
        def _(at):
            ref.grad_projected[at, first : first + 3 * LANES] = dot_nn(
                ref.perm_back[at, :], ref.grad_three[...]
            ).astype(jnp.bfloat16)

    pull(0, True)
    scatter.two("mlp")
    pull(0, False)
    unproject(0)
    scatter.three("inner")
    pull(1, True)
    scatter.two("out")
    pull(1, False)
    scatter.three("mlp")
    unproject(1)
    pull(2, True)
    scatter.two("pair0")
    scatter.three("out")
    scatter.four("inner")
    pull(2, False)
    unproject(2)
    scatter.three("pair0")
    scatter.two("pair1")
    scatter.four("mlp")
    qkv_span = (spans["pair0"][0], 3 * pairs * LANES)
    got_one = pair_sum(
        lambda at: dot_nt(ref.grad_projected[at, :], weights_at(ref.full, qkv_span)),
        0, 5, ref.grad_tokens,
    )
    scatter.three("pair1")
    got_one.wait_recv()

    @row_loop(half, 128)
    def _(at):
        incoming = ref.grad_tokens[at, :] + ref.taken[0, at, :].astype(jnp.float32)
        unit = ref.unit_one[at, :]
        ref.gain_rows[0:1, :] += jnp.sum(incoming * unit, axis=0, keepdims=True)
        ref.grad_tokens[at, :] = ref.grad_hidden[at, :] + norm_backward(
            incoming, ref.gain[0:1, :], unit, ref.scale_one[at, 0:1]
        )

    got_gain = link.to_core(ref.gain_rows, ref.gain_other, 8)
    scatter.two("pair2")
    scatter.four("out")
    got_gain.wait_recv()
    gain_rows = ref.gain_rows[...] + ref.gain_other[...]
    high = gain_rows.astype(jnp.bfloat16)
    rest = (gain_rows - high.astype(jnp.float32)).astype(jnp.bfloat16)
    slot = lax.broadcasted_iota(jnp.int32, (16, LANES), 0)
    lane = lax.broadcasted_iota(jnp.int32, (16, LANES), 1)
    pick = jnp.where(slot == lane, 1.0, 0.0).astype(jnp.bfloat16)
    columns = dot_tn(jnp.concatenate([high, rest], axis=0), pick).astype(jnp.bfloat16)
    ref.full[:, :, :, :, 0:LANES] = columns.reshape(4, 2, 2, width // 16, LANES)
    scatter.one("gains")
    scatter.four("pair0")
    scatter.three("pair2")
    scatter.two("gains")
    scatter.four("pair1")
    scatter.three("gains")
    scatter.four("pair2")
    scatter.four("gains")
    link.finish()


def call_layer(pack, tokens, cotangent, offsets, spans):
    half, width = tokens.shape
    rows = 2 * half
    height, total = pack.shape
    width_here = spans["out"][1]
    pairs = width_here // LANES
    main = spans["gate"][1]
    half_dim = HEAD_DIM // 2
    inverse = jnp.power(
        jnp.float32(ROPE_BASE), -2.0 * jnp.arange(half_dim, dtype=jnp.float32) / HEAD_DIM
    )
    inverse = jnp.tile(inverse, LANES // half_dim)[None, :]
    low, wide = jnp.bfloat16, jnp.float32
    outs = dict(
        outputs=((half, width), wide),
        grad_tokens=((half, width), wide),
        sums=((height, total), wide),
    )
    chunk_count = 1 + pairs + 4
    kept = dict(
        full=((4, 2, 2, height, total), low),
        grad_inner=((4, 2, 2, height, 2 * main + LANES), low),
        low_one=((2, 2, height, total), low),
        high_one=((2, 2, height, total), low),
        low_two=((2, height, total), low),
        high_two=((2, height, total), low),
        far_sum=((3, height, total), low),
        normed=((rows, width), low),
        rolled=((rows, width), low),
        grad_rows=((rows, width), low),
        normed_mlp=((rows, width), low),
        perm=((rows, rows), low),
        perm_back=((rows, rows), low),
        bias=((half, half), wide),
        values_t=((LANES, rows), low),
        keys_t=((LANES, rows), low),
        queries=((rows, width_here), low),
        keys=((rows, width_here), low),
        values=((rows, width_here), low),
        context=((rows, width_here), low),
        context_rolled=((rows, width_here), low),
        probs=((2 * width_here // HEAD_DIM, half, half), low),
        grad_rolled=((rows, width_here), low),
        product=((rows, main + LANES), low),
        grad_gate_up=((rows, 2 * main + LANES), low),
        grad_product=((rows, main + LANES), wide),
        sent=((3, half, width), low),
        taken=((3, half, width), low),
        hidden=((half, width), wide),
        grad_hidden=((half, width), wide),
        unit_one=((half, width), wide),
        unit_two=((half, width), wide),
        scale_one=((half, LANES), wide),
        scale_two=((half, LANES), wide),
        cosine=((rows, LANES), wide),
        sine=((rows, LANES), wide),
        gain=((8, width), wide),
        gain_rows=((8, width), wide),
        gain_other=((8, width), wide),
    )
    scratch = {name: pltpu.VMEM(*entry) for name, entry in kept.items()}
    for name, count in (
        ("far", 3 * chunk_count), ("near", 4 * chunk_count), ("core", 9), ("sum", 7 * (pairs + 4)),
    ):
        scratch[name + "_out"] = pltpu.SemaphoreType.DMA((count,))
        scratch[name + "_in"] = pltpu.SemaphoreType.DMA((count,))
    names = ["offsets", "pack", "tok", "cot", "inverse"] + list(outs) + list(scratch)
    vmem = pl.BlockSpec(memory_space=pltpu.VMEM)
    results = pl.pallas_call(
        functools.partial(layer_kernel, names, spans),
        out_shape=[jax.ShapeDtypeStruct(*entry) for entry in outs.values()],
        in_specs=[pl.BlockSpec(memory_space=pltpu.SMEM)] + [vmem] * 4,
        out_specs=[vmem] * len(outs),
        scratch_shapes=list(scratch.values()),
        compiler_params=pltpu.CompilerParams(
            collective_id=0, has_side_effects=True, vmem_limit_bytes=63 * 1024 * 1024
        ),
        cost_estimate=pl.CostEstimate(
            flops=12 * 10**9, bytes_accessed=30 * 10**6, transcendentals=10**7
        ),
    )(offsets, pack, tokens, cotangent, inverse)
    return types.SimpleNamespace(**dict(zip(outs, results)))


def fast_shards(tokens, offsets, w_qkv, w_attn_out, w_in, w_mlp_out, gain_attn, gain_mlp, cotangent):
    half = tokens.shape[0]
    rows = 2 * half
    height, _, width_here = w_qkv.shape
    hidden_here = w_in.shape[2]
    pairs = width_here // LANES
    main = hidden_here // LANES * LANES
    spans = fast_columns(width_here, hidden_here)
    pack = pack_shards(w_qkv, w_attn_out, w_in, w_mlp_out, gain_attn, gain_mlp)
    f = call_layer(pack, tokens, cotangent, offsets, spans)
    pick = lambda name: f.sums[:, spans[name][0] : spans[name][0] + spans[name][1]]
    at = spans["pair0"][0]
    tail = pick("tail")
    gate = jnp.concatenate([pick("gate"), tail[:, : hidden_here - main]], axis=1)
    up = jnp.concatenate([pick("up"), tail[:, hidden_here - main :]], axis=1)
    return (
        f.outputs,
        f.grad_tokens,
        f.sums[:, at : at + 3 * width_here]
        .reshape(height, pairs, 3, LANES)
        .transpose(0, 2, 1, 3)
        .reshape(height, 3, width_here),
        pick("out").T,
        jnp.stack([gate, up], axis=1),
        pick("mlp")[:, :hidden_here].T,
        f.sums[:, 0] + f.sums[:, 8],
        f.sums[:, 1] + f.sums[:, 9],
    )


def solution(mesh):
    in_specs = (
        P(("dp", "tensor"), None),
        P("dp", None),
        P("dp", None, "tensor"),
        P("tensor", "dp"),
        P("dp", None, "tensor"),
        P("tensor", "dp"),
        P("dp"),
        P("dp"),
        P(("dp", "tensor"), None),
    )
    out_specs = (
        P(("dp", "tensor"), None),
        P(("dp", "tensor"), None),
        P("dp", None, "tensor"),
        P("tensor", "dp"),
        P("dp", None, "tensor"),
        P("tensor", "dp"),
        P("dp"),
        P("dp"),
    )
    sizes = dict(mesh.shape)
    body = fast_shards if (sizes["dp"], sizes["tensor"]) == (16, 2) else shards
    return jax.shard_map(body, mesh=mesh, in_specs=in_specs, out_specs=out_specs, check_vma=False)
```

```python
import functools
import math
import types

import jax
import jax.numpy as jnp
import numpy as np
from jax import lax
from jax.experimental import pallas as pl
from jax.experimental.pallas import tpu as pltpu
from jax.sharding import PartitionSpec as P

HEAD_DIM = 64


EPSILON = 1e-05
ROPE_BASE = 160000.0
NEGATIVE = -1e30
LANES = 128
QUERY_BLOCK = 256
SCALE = 1.0 / math.sqrt(HEAD_DIM)
VMEM_LIMIT = 48 * 1024 * 1024


def seq_starts(offset_row, position):
    before = offset_row[None, :] <= position[:, None]
    return jnp.max(jnp.where(before, offset_row[None, :], 0), axis=1)


def rope_tables(position):
    half_dim = HEAD_DIM // 2
    inverse = jnp.power(
        jnp.float32(ROPE_BASE), -2.0 * jnp.arange(half_dim, dtype=jnp.float32) / HEAD_DIM
    )
    angles = position.astype(jnp.float32)[:, None] * inverse[None, :]
    copies = LANES // half_dim
    cosine = jnp.cos(angles)
    sine = jnp.sin(angles)
    return (
        jnp.concatenate([cosine] * copies, axis=1),
        jnp.concatenate([-sine, sine] * (copies // 2), axis=1),
    )


def levels_of(count):
    out = []
    stride = 1
    while stride < count:
        size = min(4, count // stride)
        out.append((stride, size))
        stride *= size
    return out


def swap_pairs(count, mask):
    return [(place, place ^ mask) for place in range(count)]


def send_step(held, stride, size):
    count = lax.axis_size("dp")
    return [held] + [
        lax.ppermute(held, "dp", swap_pairs(count, step * stride)) for step in range(1, size)
    ]


def place_step(taken, stride, size):
    mine = (lax.axis_index("dp") // stride) % size
    outer, height, width = taken[0].shape
    spread = jnp.zeros((outer, size, height, width), taken[0].dtype)
    for step in range(size):
        spread = lax.dynamic_update_slice(spread, taken[step][:, None], (0, mine ^ step, 0, 0))
    return spread.reshape(outer * size, height, width)


def after(later, *earlier):
    return lax.optimization_barrier((later, *earlier))[0]


def gather_both(first, second):
    one, two = first[None], second[None]
    taken = None
    for level in reversed(levels_of(lax.axis_size("dp"))):
        if taken is not None:
            two = place_step(taken, *last)
        one = place_step(send_step(one, *level), *level)
        taken = send_step(after(two, one), *level)
        last = level
    return one.reshape(-1, one.shape[2]), (taken, last)


def gather_rest(pending, *earlier):
    taken, level = pending
    taken = lax.optimization_barrier((taken, *earlier))[0]
    full = place_step(taken, *level)
    return full.reshape(-1, full.shape[2])


def sum_blocks(terms, *earlier):
    count = lax.axis_size("dp")
    me = lax.axis_index("dp")
    height = terms.shape[0] // count
    width = terms.shape[1]
    held = terms
    for stride, size in levels_of(count):
        mine = (me // stride) % size
        parts = held.reshape(-1, size, height, width)
        pick = lambda place: lax.dynamic_index_in_dim(parts, place, 1, keepdims=False)
        got = [
            lax.ppermute(pick(mine ^ step), "dp", swap_pairs(count, step * stride))
            for step in range(1, size)
        ]
        if earlier:
            got = lax.optimization_barrier((got, *earlier))[0]
            earlier = ()
        total = pick(mine).astype(jnp.float32)
        for other in got:
            total = total + other.astype(jnp.float32)
        held = total.astype(jnp.bfloat16)
    return total.reshape(height, width)


def other_half(local_rows):
    return lax.ppermute(local_rows, "tensor", [(0, 1), (1, 0)])


def spread_rows(local_rows):
    return jnp.concatenate([local_rows, other_half(local_rows)], axis=0)


def collect_own(partial_sums, rows_here):
    sent = other_half(partial_sums[rows_here:].astype(jnp.bfloat16))
    return partial_sums[:rows_here] + sent.astype(jnp.float32)


def collect_all(partial_sums, rows_here):
    got = other_half(partial_sums.astype(jnp.bfloat16))
    swapped = jnp.concatenate([got[rows_here:], got[:rows_here]], axis=0)
    return partial_sums + swapped.astype(jnp.float32)


def norm_parts(inputs_v):
    centre = inputs_v - jnp.mean(inputs_v, axis=-1, keepdims=True)
    spread = jnp.mean(centre * centre, axis=-1, keepdims=True)
    scale_v = lax.rsqrt(spread + EPSILON)
    return centre * scale_v, scale_v


def norm_backward(incoming, gain_v, unit, scale_v):
    scaled = incoming * gain_v
    mean_one = jnp.mean(scaled, axis=-1, keepdims=True)
    mean_two = jnp.mean(scaled * unit, axis=-1, keepdims=True)
    return scale_v * (scaled - mean_one - unit * mean_two)


def two_terms(column):
    high = column.astype(jnp.bfloat16)
    rest = (column - lax.reduce_precision(column, 8, 7)).astype(jnp.bfloat16)
    return jnp.stack([high, rest], axis=1)


def padded(pieces):
    width = sum(piece.shape[1] for piece in pieces)
    short = -width % 128
    height = pieces[0].shape[0]
    if short:
        pieces = pieces + [jnp.zeros((height, short), jnp.bfloat16)]
    return jnp.concatenate(pieces, axis=1)


def dot_nn(left, right):
    return jnp.dot(left, right, preferred_element_type=jnp.float32)


def dot_nt(left, right):
    return lax.dot_general(
        left, right, (((1,), (1,)), ((), ())), preferred_element_type=jnp.float32
    )


def dot_tn(left, right):
    return lax.dot_general(
        left, right, (((0,), (0,)), ((), ())), preferred_element_type=jnp.float32
    )


def turn(rows, cosine, sine_signed, lane):
    half_dim = HEAD_DIM // 2
    ahead = pltpu.roll(rows, rows.shape[1] - half_dim, axis=1)
    behind = pltpu.roll(rows, half_dim, axis=1)
    swapped = jnp.where(lane % HEAD_DIM < half_dim, ahead, behind)
    return rows * cosine + swapped * sine_signed


def forward_kernel(
    normed_ref, wq_ref, wk_ref, wv_ref, cos_ref, sin_ref, srow_ref, scol_ref,
    q_ref, k_ref, v_ref, ctx_ref, lse_ref, vt_ref,
):
    rows = normed_ref.shape[0]
    block = min(QUERY_BLOCK, rows)
    normed = normed_ref[...]
    cosine = cos_ref[...]
    sine = sin_ref[...]
    lane = lax.broadcasted_iota(jnp.int32, (rows, LANES), 1)
    dot = functools.partial(jnp.dot, preferred_element_type=jnp.float32)
    q_ref[...] = turn(dot(normed, wq_ref[...]), cosine, sine, lane).astype(jnp.bfloat16)
    k_ref[...] = turn(dot(normed, wk_ref[...]), cosine, sine, lane).astype(jnp.bfloat16)
    values = dot(normed, wv_ref[...])
    v_ref[...] = values.astype(jnp.bfloat16)
    vt_ref[...] = values.T.astype(jnp.bfloat16)

    @pl.loop(0, rows // block)
    def _(step):
        at = pl.ds(pl.multiple_of(step * block, block), block)
        same = scol_ref[...] == srow_ref[:, at]
        parts = []
        for head in range(LANES // HEAD_DIM):
            cols = slice(head * HEAD_DIM, (head + 1) * HEAD_DIM)
            scores = dot_nt(k_ref[:, cols], q_ref[at, cols]) * SCALE
            scores = jnp.where(same, scores, NEGATIVE)
            top = jnp.max(scores, axis=0, keepdims=True)
            terms = jnp.exp(scores - top)
            total = jnp.sum(terms, axis=0, keepdims=True)
            weights = (terms * (1.0 / total)).astype(jnp.bfloat16)
            parts.append(dot(vt_ref[cols, :], weights))
            lse_ref[0, head : head + 1, at] = top + jnp.log(total)
        ctx_ref[at, :] = jnp.concatenate(parts, axis=0).T.astype(jnp.bfloat16)


def backward_kernel(
    grad_ref, wo_ref, q_ref, k_ref, v_ref, cos_ref, sin_ref, srow_ref, scol_ref, lse_ref,
    dq_ref, dk_ref, dv_ref, g_ref, kt_ref, acc_q, acc_k, acc_v,
):
    rows = grad_ref.shape[0]
    block = min(QUERY_BLOCK, rows)
    dot = functools.partial(jnp.dot, preferred_element_type=jnp.float32)
    g_ref[...] = dot(grad_ref[...], wo_ref[...]).astype(jnp.bfloat16)
    kt_ref[...] = k_ref[...].astype(jnp.float32).T.astype(jnp.bfloat16)
    acc_k[...] = jnp.zeros_like(acc_k)
    acc_v[...] = jnp.zeros_like(acc_v)

    @pl.loop(0, rows // block)
    def _(step):
        at = pl.ds(pl.multiple_of(step * block, block), block)
        same = scol_ref[...] == srow_ref[:, at]
        parts = []
        for head in range(LANES // HEAD_DIM):
            cols = slice(head * HEAD_DIM, (head + 1) * HEAD_DIM)
            query = q_ref[at, cols]
            grad = g_ref[at, cols]
            scores = dot_nt(k_ref[:, cols], query) * SCALE
            probs = jnp.exp(jnp.where(same, scores - lse_ref[0, head : head + 1, at], NEGATIVE))
            acc_v[:, cols] += dot(probs.astype(jnp.bfloat16), grad)
            grad_probs = dot_nt(v_ref[:, cols], grad)
            weighted = probs * grad_probs
            drop = jnp.sum(weighted, axis=0, keepdims=True)
            grad_scores = (weighted - probs * drop).astype(jnp.bfloat16)
            acc_k[:, cols] += dot(grad_scores, query)
            parts.append(dot(kt_ref[cols, :], grad_scores))
        acc_q[at, :] = jnp.concatenate(parts, axis=0).T

    cosine = cos_ref[...] * SCALE
    sine = sin_ref[...] * -SCALE
    lane = lax.broadcasted_iota(jnp.int32, (rows, LANES), 1)
    dq_ref[...] = turn(acc_q[...], cosine, sine, lane).astype(jnp.bfloat16)
    dk_ref[...] = turn(acc_k[...], cosine, sine, lane).astype(jnp.bfloat16)
    dv_ref[...] = acc_v[...].astype(jnp.bfloat16)


def whole(shape):
    return pl.BlockSpec(shape, lambda pair: (0,) * len(shape))


def column_block(rows, first):
    return pl.BlockSpec((rows, LANES), lambda pair: (0, first + pair))


def attention_forward(normed_all, attn_pack, cosine, sine, starts, width_here):
    rows, width = normed_all.shape
    pairs = width_here // LANES
    heads_each = LANES // HEAD_DIM
    low = jax.ShapeDtypeStruct((rows, width_here), jnp.bfloat16)
    return pl.pallas_call(
        forward_kernel,
        grid=(pairs,),
        out_shape=(low, low, low, low, jax.ShapeDtypeStruct((pairs, heads_each, rows), jnp.float32)),
        in_specs=[
            whole((rows, width)),
            column_block(width, 0),
            column_block(width, pairs),
            column_block(width, 2 * pairs),
            whole((rows, LANES)),
            whole((rows, LANES)),
            whole((1, rows)),
            whole((rows, 1)),
        ],
        out_specs=[column_block(rows, 0)] * 4
        + [pl.BlockSpec((1, heads_each, rows), lambda pair: (pair, 0, 0))],
        scratch_shapes=[pltpu.VMEM((LANES, rows), jnp.bfloat16)],
        compiler_params=pltpu.CompilerParams(vmem_limit_bytes=VMEM_LIMIT),
        cost_estimate=pl.CostEstimate(
            flops=2 * rows * width * 3 * width_here + 4 * rows * rows * width_here,
            bytes_accessed=2 * (rows * width + 3 * width * width_here + 4 * rows * width_here),
            transcendentals=rows * rows * width_here // HEAD_DIM,
        ),
    )(normed_all, attn_pack, attn_pack, attn_pack, cosine, sine, starts[None, :], starts[:, None])


def attention_backward(grad_rows, attn_pack, queries, key_rows, values, cosine, sine, starts, lse):
    rows, width = grad_rows.shape
    width_here = queries.shape[1]
    pairs = width_here // LANES
    heads_each = LANES // HEAD_DIM
    low = jax.ShapeDtypeStruct((rows, width_here), jnp.bfloat16)
    return pl.pallas_call(
        backward_kernel,
        grid=(pairs,),
        out_shape=(low, low, low),
        in_specs=[
            whole((rows, width)),
            column_block(width, 0),
            column_block(rows, 0),
            column_block(rows, 0),
            column_block(rows, 0),
            whole((rows, LANES)),
            whole((rows, LANES)),
            whole((1, rows)),
            whole((rows, 1)),
            pl.BlockSpec((1, heads_each, rows), lambda pair: (pair, 0, 0)),
        ],
        out_specs=[column_block(rows, 0)] * 3,
        scratch_shapes=[
            pltpu.VMEM((rows, LANES), jnp.bfloat16),
            pltpu.VMEM((LANES, rows), jnp.bfloat16),
            pltpu.VMEM((rows, LANES), jnp.float32),
            pltpu.VMEM((rows, LANES), jnp.float32),
            pltpu.VMEM((rows, LANES), jnp.float32),
        ],
        compiler_params=pltpu.CompilerParams(vmem_limit_bytes=VMEM_LIMIT),
        cost_estimate=pl.CostEstimate(
            flops=2 * rows * width * width_here + 10 * rows * rows * width_here,
            bytes_accessed=2 * (rows * width + width * width_here + 7 * rows * width_here),
            transcendentals=rows * rows * width_here // HEAD_DIM,
        ),
    )(
        grad_rows, attn_pack, queries, key_rows, values, cosine, sine,
        starts[None, :], starts[:, None], lse,
    )


def shards(tokens, offsets, w_qkv, w_attn_out, w_in, w_mlp_out, gain_attn, gain_mlp, cotangent):
    rows_here = tokens.shape[0]
    group_rows = rows_here * lax.axis_size("tensor")
    model_here = w_qkv.shape[0]
    width_here = w_qkv.shape[2]
    hidden_here = w_in.shape[2]
    half_at = lax.axis_index("tensor") * rows_here
    position = (jnp.arange(group_rows, dtype=jnp.int32) + half_at) % group_rows
    starts = seq_starts(offsets[0], position)
    cosine_tab, sine_tab = rope_tables(position - starts)

    attn_pack, pending = gather_both(
        padded([w_qkv.reshape(model_here, 3 * width_here), gain_attn[:, None]]),
        padded(
            [w_attn_out.T, w_in.reshape(model_here, 2 * hidden_here), w_mlp_out.T, gain_mlp[:, None]]
        ),
    )
    gain_one = attn_pack[:, 3 * width_here].astype(jnp.float32)
    qkv_full = attn_pack[:, : 3 * width_here]

    token_rows = spread_rows(tokens)
    cotangent_rows = spread_rows(cotangent)
    grad_rows = cotangent_rows.astype(jnp.bfloat16)
    unit_one, scale_one = norm_parts(token_rows)
    normed_all = (unit_one * gain_one).astype(jnp.bfloat16)
    queries, key_rows, values, context, lse = attention_forward(
        normed_all, attn_pack, cosine_tab, sine_tab, starts, width_here
    )

    rest_pack = gather_rest(pending, lse)
    mlp_at = width_here
    mlp_end = width_here + 2 * hidden_here
    attn_out_full = rest_pack[:, :width_here]
    mlp_in_full = rest_pack[:, mlp_at:mlp_end]
    mlp_out_full = rest_pack[:, mlp_end : mlp_end + hidden_here]
    gain_two = rest_pack[:, mlp_end + hidden_here].astype(jnp.float32)
    attended = collect_all(dot_nt(context, attn_out_full), rows_here)
    hidden = token_rows + attended
    unit_two, scale_two = norm_parts(hidden)
    mlp_rows = (unit_two * gain_two).astype(jnp.bfloat16)
    gate_part = dot_nn(mlp_rows, mlp_in_full[:, :hidden_here])
    up_part = dot_nn(mlp_rows, mlp_in_full[:, hidden_here:])
    grad_product = dot_nn(grad_rows, mlp_out_full)
    bell = 0.5 * (1.0 + lax.erf(gate_part * math.sqrt(0.5)))
    activated = gate_part * bell
    slope = bell + gate_part * jnp.exp(-0.5 * gate_part * gate_part) * (1.0 / math.sqrt(2 * math.pi))
    product_rows = (activated * up_part).astype(jnp.bfloat16)
    grad_gate_up = jnp.concatenate(
        [
            (grad_product * up_part * slope).astype(jnp.bfloat16),
            (grad_product * activated).astype(jnp.bfloat16),
        ],
        axis=1,
    )
    grad_normed_two = collect_all(dot_nt(grad_gate_up, mlp_in_full), rows_here)
    grad_hidden = cotangent_rows + norm_backward(grad_normed_two, gain_two, unit_two, scale_two)
    grad_gain_two = jnp.sum((grad_normed_two * unit_two)[:rows_here], axis=0)
    grad_hidden_rows = grad_hidden.astype(jnp.bfloat16)
    grads_three = attention_backward(
        grad_hidden_rows, rest_pack, queries, key_rows, values,
        cosine_tab, sine_tab, starts, lse,
    )
    mlp_terms = padded(
        [
            dot_tn(mlp_rows, grad_gate_up).astype(jnp.bfloat16),
            dot_tn(grad_rows, product_rows).astype(jnp.bfloat16),
            two_terms(grad_gain_two),
        ]
    )
    mlp_sums = sum_blocks(mlp_terms, grads_three[0])
    branch = collect_own(dot_nt(product_rows, mlp_out_full), rows_here)
    outputs = hidden[:rows_here] + branch

    grad_projected = jnp.concatenate(grads_three, axis=1)
    grad_normed_one = collect_own(dot_nt(grad_projected, qkv_full), rows_here)
    grad_tokens = grad_hidden[:rows_here] + norm_backward(
        grad_normed_one, gain_one, unit_one[:rows_here], scale_one[:rows_here]
    )
    grad_gain_one = jnp.sum(grad_normed_one * unit_one[:rows_here], axis=0)
    attn_terms = padded(
        [
            dot_tn(normed_all, grad_projected).astype(jnp.bfloat16),
            dot_tn(grad_hidden_rows, context).astype(jnp.bfloat16),
            two_terms(grad_gain_one),
        ]
    )
    attn_sums = sum_blocks(attn_terms)

    gain_one_cols = attn_sums[:, 4 * width_here : 4 * width_here + 2].sum(axis=1)
    gain_two_cols = mlp_sums[:, 3 * hidden_here : 3 * hidden_here + 2].sum(axis=1)
    gains = jnp.stack([gain_one_cols, gain_two_cols])
    gains = gains + other_half(gains)
    return (
        outputs,
        grad_tokens,
        attn_sums[:, : 3 * width_here].reshape(model_here, 3, width_here),
        attn_sums[:, 3 * width_here : 4 * width_here].T,
        mlp_sums[:, : 2 * hidden_here].reshape(model_here, 2, hidden_here),
        mlp_sums[:, 2 * hidden_here : 3 * hidden_here].T,
        gains[0],
        gains[1],
    )


def fast_columns(width_here, hidden_here):
    main = hidden_here // LANES * LANES
    pairs = width_here // LANES
    at = {"gains": (0, LANES)}
    place = LANES
    for pair in range(pairs):
        at["pair%d" % pair] = (place, 3 * LANES)
        place += 3 * LANES
    for name, size in (
        ("out", width_here), ("mlp", main + LANES), ("gate", main), ("up", main), ("tail", LANES),
    ):
        at[name] = (place, size)
        place += size
    at["total"] = (0, place)
    return at


def pack_shards(ref, spans):
    height = ref.w_attn_out.shape[0]
    main = spans["gate"][1]
    hidden_here = ref.w_in.shape[1] // 2
    pairs = spans["out"][1] // LANES
    wide = jnp.float32
    down = lax.broadcasted_iota(jnp.int32, (height, height), 0)
    along = lax.broadcasted_iota(jnp.int32, (height, height), 1)
    lane = lax.broadcasted_iota(jnp.int32, (height, LANES), 1)
    gains = jnp.zeros((height, LANES), wide)
    for place, row in enumerate((ref.gain_one, ref.gain_two)):
        column = jnp.sum(jnp.where(down == along, row[...].astype(wide), 0.0), axis=1, keepdims=True)
        gains = jnp.where(lane == place, column, gains)
    pieces = [gains.astype(jnp.bfloat16)]
    for pair in range(pairs):
        for kind in range(3):
            pieces.append(ref.w_qkv[kind, :, pair * LANES : (pair + 1) * LANES])
    tail = jnp.concatenate(
        [ref.w_in[:, main:hidden_here], ref.w_in[:, hidden_here + main :]], axis=1
    )
    mlp = jnp.concatenate(
        [ref.w_mlp_out[...], jnp.zeros((height, main + LANES - hidden_here), jnp.bfloat16)], axis=1
    )
    pieces += [
        ref.w_attn_out[...],
        mlp,
        ref.w_in[:, :main],
        ref.w_in[:, hidden_here : hidden_here + main],
        tail,
    ]
    return pieces


class Links:
    def __init__(self, ref):
        self.ref = ref
        self.dp = lax.axis_index("dp")
        self.core = lax.axis_index("tensor")
        self.x = self.dp % 2
        self.y = (self.dp // 2) % 2
        self.z = self.dp // 4
        plane = self.dp % 4
        self.x_side = self.dp + 1 - 2 * self.x
        self.y_side = self.dp + 2 - 4 * self.y
        self.z_of = [None, self.z + 1 - 2 * (self.z % 2), (self.z + 2) % 4, 3 - self.z]
        self.z_side = [None] + [place * 4 + plane for place in self.z_of[1:]]
        self.started = []

    def enter(self):
        barrier = pltpu.get_barrier_semaphore()
        others = [(self.x_side, self.core), (self.y_side, self.core), (self.dp, 1 - self.core)]
        others += [(place, self.core) for place in self.z_side[1:]]
        for other in others:
            pl.semaphore_signal(
                barrier, inc=1, device_id=other, device_id_type=pl.DeviceIdType.MESH
            )
        pl.semaphore_wait(barrier, len(others))

    def copy(self, source, target, sems, place, device):
        return pltpu.make_async_remote_copy(
            src_ref=source,
            dst_ref=target,
            send_sem=sems[0].at[place],
            recv_sem=sems[1].at[place],
            device_id=device,
            device_id_type=pl.DeviceIdType.MESH,
        )

    def start(self, *copies):
        for copy in copies:
            copy.start()
            self.started.append(copy)

    def to_core(self, source, target, place):
        copy = self.copy(
            source, target, (self.ref.core_out, self.ref.core_in), place, (self.dp, 1 - self.core)
        )
        self.start(copy)
        return copy

    def finish(self):
        for copy in self.started:
            copy.wait_send()
        self.started = []


class Gather(Links):
    def __init__(self, ref, chunks):
        super().__init__(ref)
        self.chunks = chunks
        self.got = {}

    def send_z(self, name):
        chunk = list(self.chunks).index(name)
        cols = pl.ds(*self.chunks[name])
        block = self.ref.full.at[self.z, self.y, self.x, :, cols]
        copies = [
            self.copy(
                block, block, (self.ref.far_out, self.ref.far_in), 3 * chunk + step - 1,
                (self.z_side[step], self.core),
            )
            for step in (1, 2, 3)
        ]
        self.start(*copies)
        self.got[name] = copies

    def arrive(self, name):
        for copy in self.got[name]:
            copy.wait_recv()

    def near(self, name, stage, first, second):
        chunk = list(self.chunks).index(name)
        sems = (self.ref.near_out, self.ref.near_in)
        place = 4 * chunk + 2 * stage
        copies = [
            self.copy(first[0], first[0], sems, place, (first[1], self.core)),
            self.copy(second[0], second[0], sems, place + 1, (second[1], self.core)),
        ]
        self.arrive(name)
        self.start(*copies)
        self.got[name] = copies

    def send_one(self, name):
        cols = pl.ds(*self.chunks[name])
        low, high = pl.ds(0, 2), pl.ds(2, 2)
        full = self.ref.full
        self.near(
            name, 0,
            (full.at[low, self.y, self.x, :, cols], self.x_side),
            (full.at[high, self.y, self.x, :, cols], self.y_side),
        )

    def send_two(self, name):
        cols = pl.ds(*self.chunks[name])
        low, high = pl.ds(0, 2), pl.ds(2, 2)
        both = pl.ds(0, 2)
        full = self.ref.full
        self.near(
            name, 1,
            (full.at[low, self.y, both, :, cols], self.y_side),
            (full.at[high, both, self.x, :, cols], self.x_side),
        )


class Scatter:
    def __init__(self, link, chunks):
        self.link = link
        self.ref = link.ref
        self.chunks = chunks
        self.got = {}

    def send(self, name, stage, moves):
        sems = (self.ref.sum_out, self.ref.sum_in)
        place = 7 * list(self.chunks).index(name) + 2 * stage
        copies = [
            self.link.copy(source, target, sems, place + step, (side, self.link.core))
            for step, (source, target, side) in enumerate(moves)
        ]
        self.link.start(*copies)
        self.got[name] = copies

    def arrive(self, name):
        for copy in self.got[name]:
            copy.wait_recv()

    def parts(self, name):
        held, span, place = self.chunks[name]
        return held, pl.ds(*span), pl.ds(place, span[1])

    def one(self, name):
        link, ref = self.link, self.ref
        held, cols, to = self.parts(name)
        both = pl.ds(0, 2)
        self.send(name, 0, [
            (held.at[pl.ds(0, 2), 1 - link.y, both, :, cols], ref.low_one.at[:, :, :, to], link.y_side),
            (held.at[pl.ds(2, 2), both, 1 - link.x, :, cols], ref.high_one.at[:, :, :, to], link.x_side),
        ])

    def two(self, name):
        link, ref = self.link, self.ref
        held, cols, to = self.parts(name)
        both = pl.ds(0, 2)
        self.arrive(name)
        at = (pl.ds(0, 2), link.y, both, slice(None), cols)
        held[at] = held[at] + ref.low_one[:, :, :, to]
        at = (pl.ds(2, 2), both, link.x, slice(None), cols)
        held[at] = held[at] + ref.high_one[:, :, :, to]
        self.send(name, 1, [
            (held.at[pl.ds(0, 2), link.y, 1 - link.x, :, cols], ref.low_two.at[:, :, to], link.x_side),
            (held.at[pl.ds(2, 2), 1 - link.y, link.x, :, cols], ref.high_two.at[:, :, to], link.y_side),
        ])

    def three(self, name):
        link, ref = self.link, self.ref
        held, cols, to = self.parts(name)
        self.arrive(name)
        at = (pl.ds(0, 2), link.y, link.x, slice(None), cols)
        held[at] = held[at] + ref.low_two[:, :, to]
        at = (pl.ds(2, 2), link.y, link.x, slice(None), cols)
        held[at] = held[at] + ref.high_two[:, :, to]
        self.send(name, 2, [
            (
                held.at[link.z_of[step], link.y, link.x, :, cols],
                ref.far_sum.at[step - 1, :, to],
                link.z_side[step],
            )
            for step in (1, 2, 3)
        ])

    def four(self, name):
        link, ref = self.link, self.ref
        held, cols, to = self.parts(name)
        self.arrive(name)
        total = held[link.z, link.y, link.x, :, cols].astype(jnp.float32)
        for step in range(3):
            total = total + ref.far_sum[step, :, to].astype(jnp.float32)
        return total


def weights_at(full, span):
    block = full[:, :, :, :, span[0] : span[0] + span[1]]
    return block.reshape(-1, span[1])


def row_loop(rows, block):
    def wrap(body):
        @pl.loop(0, rows // block)
        def _(step):
            body(pl.ds(pl.multiple_of(step * block, block), block))

    return wrap


def layer_kernel(names, spans, *refs):
    ref = types.SimpleNamespace(**dict(zip(names, refs)))
    half, width = ref.tok.shape
    rows = 2 * half
    fetch_tok = pltpu.make_async_copy(ref.tokens, ref.tok, ref.fetch.at[0])
    fetch_cot = pltpu.make_async_copy(ref.cotangent, ref.cot, ref.fetch.at[1])
    fetch_tok.start()
    fetch_cot.start()
    pairs = (spans["out"][1]) // LANES
    main = spans["gate"][1]
    chunk_names = ["gains"] + ["pair%d" % pair for pair in range(pairs)] + ["out", "mlp"]
    chunks = {name: spans[name] for name in chunk_names}
    chunks["gate"] = spans["gate"]
    chunks["up"] = (spans["up"][0], main + LANES)
    link = Gather(ref, chunks)
    core = link.core
    own = pl.ds(pl.multiple_of(core * half, half), half)
    own_at = core * half
    other_at = (1 - core) * half
    part = 256

    ref.grad_low = ref.normed
    ref.grad_context = ref.product.at[:, : pairs * LANES]
    ref.grad_three = ref.product.at[:, : 3 * LANES]
    ref.grad_projected = ref.grad_gate_up
    ref.acc = ref.grad_product.at[:, : 3 * LANES]
    scatter = Scatter(
        link,
        {
            "inner": (ref.grad_inner, (0, 2 * main + LANES), spans["gate"][0]),
            "mlp": (ref.full, spans["mlp"], spans["mlp"][0]),
            "out": (ref.full, spans["out"], spans["out"][0]),
            **{
                "pair%d" % pair: (
                    ref.full,
                    (spans["gate"][0] + 3 * LANES * pair, 3 * LANES),
                    spans["pair%d" % pair][0],
                )
                for pair in range(pairs)
            },
            "gains": (ref.full, spans["gains"], spans["gains"][0]),
        },
    )

    place = 0
    for piece in pack_shards(ref, spans):
        wide = piece.shape[1]
        ref.full[link.z, link.y, link.x, :, place : place + wide] = piece
        place += wide
    link.enter()
    link.send_z("gains")
    link.send_z("pair0")
    link.send_z("pair1")

    fetch_tok.wait()

    @row_loop(half, 128)
    def _(at):
        unit, scale = norm_parts(ref.tok[at, :])
        ref.unit_one[at, :] = unit
        ref.scale_one[at, :] = jnp.broadcast_to(scale, (128, LANES))

    link.send_one("gains")

    shift = jnp.int32(0)
    for slot in range(ref.offsets.shape[1]):
        entry = ref.offsets[0, slot]
        shift = jnp.maximum(shift, jnp.where(entry <= half - 1, entry, 0))

    def source_of(place):
        moved = place + shift
        return jnp.where(moved >= rows, moved - rows, moved)

    def start_of(place):
        start = jnp.zeros_like(place)
        for slot in range(ref.offsets.shape[1]):
            entry = ref.offsets[0, slot]
            start = jnp.maximum(start, jnp.where(place >= entry, entry, 0))
        return start

    @row_loop(rows, part)
    def _(at):
        down = source_of(lax.broadcasted_iota(jnp.int32, (part, 1), 0) + at.start)
        along = lax.broadcasted_iota(jnp.int32, (part, rows), 1)
        ref.perm[at, :] = jnp.where(down == along, 1.0, 0.0).astype(jnp.bfloat16)
        down = lax.broadcasted_iota(jnp.int32, (part, rows), 0) + at.start
        along = source_of(lax.broadcasted_iota(jnp.int32, (1, rows), 1))
        ref.perm_back[at, :] = jnp.where(down == along, 1.0, 0.0).astype(jnp.bfloat16)

    link.send_two("gains")
    link.send_one("pair0")
    link.send_z("pair2")

    fetch_cot.wait()

    @row_loop(half, 128)
    def _(at):
        here = pl.ds(pl.multiple_of(own_at + at.start, 128), 128)
        ref.grad_rows[here, :] = ref.cot[at, :].astype(jnp.bfloat16)

    def table(at):
        place = source_of(lax.broadcasted_iota(jnp.int32, (part, LANES), 0) + at.start)
        start = start_of(place)
        angle = (place - start).astype(jnp.float32) * ref.inverse[...]
        lane = lax.broadcasted_iota(jnp.int32, (part, LANES), 1)
        sine = jnp.sin(angle)
        ref.cosine[at, :] = jnp.cos(angle)
        ref.sine[at, :] = jnp.where(lane % HEAD_DIM < HEAD_DIM // 2, -sine, sine)

    row_loop(half, part)(table)
    link.arrive("gains")
    slot = lax.broadcasted_iota(jnp.int32, (8, LANES), 0)
    lane = lax.broadcasted_iota(jnp.int32, (8, LANES), 1)
    pick = jnp.where(slot == lane, 1.0, 0.0).astype(jnp.bfloat16)
    ref.gain[...] = dot_nt(pick, weights_at(ref.full, spans["gains"]))

    @row_loop(half, 128)
    def _(at):
        here = pl.ds(pl.multiple_of(own_at + at.start, 128), 128)
        ref.normed[here, :] = (ref.unit_one[at, :] * ref.gain[0:1, :]).astype(jnp.bfloat16)

    got_normed = link.to_core(ref.normed.at[own, :], ref.normed.at[own, :], 1)
    got_grad = link.to_core(ref.grad_rows.at[own, :], ref.grad_rows.at[own, :], 0)
    link.send_one("pair1")
    link.send_z("out")

    @row_loop(half, part)
    def _(at):
        table(pl.ds(pl.multiple_of(half + at.start, part), part))

    key_start = start_of(source_of(lax.broadcasted_iota(jnp.int32, (half, 1), 0) + half))
    query_start = start_of(source_of(lax.broadcasted_iota(jnp.int32, (1, half), 1) + half))
    ref.bias[...] = jnp.where(key_start == query_start, 0.0, NEGATIVE)
    got_normed.wait_recv()
    link.send_two("pair0")

    @row_loop(rows, part)
    def _(at):
        ref.rolled[at, :] = dot_nn(ref.perm[at, :], ref.normed[...]).astype(jnp.bfloat16)

    link.send_one("pair2")
    link.send_z("mlp")

    def project(pair):
        if pair:
            link.arrive("pair%d" % pair)
        cols = slice(pair * LANES, (pair + 1) * LANES)

        @row_loop(rows, part)
        def _(at):
            three = dot_nn(ref.rolled[at, :], weights_at(ref.full, spans["pair%d" % pair]))
            lane = lax.broadcasted_iota(jnp.int32, (part, LANES), 1)
            cosine, sine = ref.cosine[at, :], ref.sine[at, :]
            query = turn(three[:, :LANES], cosine, sine, lane) * SCALE
            ref.queries[at, cols] = query.astype(jnp.bfloat16)
            ref.keys[at, cols] = turn(
                three[:, LANES : 2 * LANES], cosine, sine, lane
            ).astype(jnp.bfloat16)
            ref.values[at, cols] = three[:, 2 * LANES :].astype(jnp.bfloat16)
            ref.values_t[:, at] = three[:, 2 * LANES :].T.astype(jnp.bfloat16)

    def unit_of(pair, head, first):
        return (pair * (LANES // HEAD_DIM) + head) * 2 + (0 if first else 1)

    def attend(pair, first):
        cols = slice(pair * LANES, (pair + 1) * LANES)
        base = 0 if first else half

        for step in range(half // part):
            at = pl.ds(base + step * part, part)
            query_pair = ref.queries[at, cols]
            lane = lax.broadcasted_iota(jnp.int32, (part, LANES), 1)
            parts = []
            for head in range(LANES // HEAD_DIM):
                query = jnp.where(lane // HEAD_DIM == head, query_pair, 0)
                scores = dot_nt(ref.keys[base : base + half, cols], query)
                if not first:
                    scores = scores + ref.bias[:, step * part : (step + 1) * part]
                top = jnp.max(scores, axis=0, keepdims=True)
                terms = jnp.exp(scores - top)
                total = jnp.sum(terms, axis=0, keepdims=True)
                probs = (terms * (1.0 / total)).astype(jnp.bfloat16)
                ref.probs[
                    unit_of(pair, head, first), :, step * part : (step + 1) * part
                ] = probs
                parts.append(
                    dot_nn(
                        ref.values_t[head * HEAD_DIM : (head + 1) * HEAD_DIM, base : base + half],
                        probs,
                    )
                )
            ref.context_rolled[at, cols] = jnp.concatenate(parts, axis=0).T.astype(jnp.bfloat16)

    link.arrive("pair0")
    link.send_two("pair1")
    link.send_z("gate")
    project(0)
    link.send_one("out")
    attend(0, True)
    link.send_two("pair2")
    link.send_z("up")
    attend(0, False)
    link.send_one("mlp")
    project(1)
    link.send_two("out")
    attend(1, True)
    link.send_one("gate")
    attend(1, False)
    link.send_two("mlp")
    project(2)
    link.send_one("up")
    attend(2, True)
    link.send_two("gate")
    attend(2, False)

    @row_loop(rows, part)
    def _(at):
        ref.context[at, :] = dot_nn(ref.perm_back[at, :], ref.context_rolled[...]).astype(jnp.bfloat16)

    link.send_two("up")
    link.arrive("out")

    def pair_sum(product, place, sem, keep):
        @row_loop(half, part)
        def _(at):
            there = pl.ds(pl.multiple_of(other_at + at.start, part), part)
            ref.sent[place, at, :] = product(there).astype(jnp.bfloat16)

        got = link.to_core(ref.sent.at[place], ref.taken.at[place], sem)

        @row_loop(half, part)
        def _(at):
            here = pl.ds(pl.multiple_of(own_at + at.start, part), part)
            keep[at, :] = product(here)

        return got

    got_attended = pair_sum(
        lambda at: dot_nt(ref.context[at, :], weights_at(ref.full, spans["out"])), 0, 2, ref.hidden
    )
    got_attended.wait_recv()

    @row_loop(half, 128)
    def _(at):
        hidden = ref.tok[at, :] + ref.hidden[at, :] + ref.taken[0, at, :].astype(jnp.float32)
        ref.hidden[at, :] = hidden
        unit, scale = norm_parts(hidden)
        ref.unit_two[at, :] = unit
        ref.scale_two[at, :] = jnp.broadcast_to(scale, (128, LANES))
        here = pl.ds(pl.multiple_of(own_at + at.start, 128), 128)
        ref.normed_mlp[here, :] = (unit * ref.gain[1:2, :]).astype(jnp.bfloat16)

    got_mlp = link.to_core(ref.normed_mlp.at[own, :], ref.normed_mlp.at[own, :], 6)
    got_grad.wait_recv()
    link.arrive("mlp")

    @row_loop(rows, part)
    def _(at):
        ref.grad_product[at, :] = dot_nn(ref.grad_rows[at, :], weights_at(ref.full, spans["mlp"]))

    got_mlp.wait_recv()
    link.arrive("gate")
    link.arrive("up")

    def gated(gate, up, grad):
        bell = 0.5 * (1.0 + lax.erf(gate * math.sqrt(0.5)))
        activated = gate * bell
        slope = bell + gate * jnp.exp(-0.5 * gate * gate) * (1.0 / math.sqrt(2 * math.pi))
        return activated * up, grad * up * slope, grad * activated

    @row_loop(rows, part)
    def _(at):
        low = ref.normed_mlp[at, :]
        gate = dot_nn(low, weights_at(ref.full, spans["gate"]))
        up = dot_nn(low, weights_at(ref.full, spans["up"]))
        product, grad_gate, grad_up = gated(gate, up, ref.grad_product[at, :main])
        ref.product[at, :main] = product.astype(jnp.bfloat16)
        ref.grad_gate_up[at, :main] = grad_gate.astype(jnp.bfloat16)
        ref.grad_gate_up[at, main : 2 * main] = grad_up.astype(jnp.bfloat16)
        tail = dot_nn(low, weights_at(ref.full, spans["tail"]))
        product, grad_gate, grad_up = gated(
            tail, pltpu.roll(tail, LANES // 2, axis=1), ref.grad_product[at, main:]
        )
        lane = lax.broadcasted_iota(jnp.int32, (part, LANES), 1)
        lower = lane < LANES // 2
        ref.product[at, main:] = jnp.where(lower, product, 0.0).astype(jnp.bfloat16)
        ref.grad_gate_up[at, 2 * main :] = jnp.where(
            lower, grad_gate, pltpu.roll(grad_up, LANES // 2, axis=1)
        ).astype(jnp.bfloat16)

    inner = (spans["gate"][0], 2 * main + LANES)
    link.finish()

    def weight_grad(left, right, held, first):
        wide = right.shape[1]

        @pl.loop(0, 2)
        def _(step):
            cols = pl.ds(pl.multiple_of(step * (width // 2), LANES), width // 2)
            block = dot_tn(left[:, cols], right[...]).astype(jnp.bfloat16)
            held[pl.ds(2 * step, 2), :, :, :, first : first + wide] = block.reshape(
                2, 2, 2, width // 16, wide
            )

    weight_grad(ref.normed_mlp, ref.grad_gate_up, ref.grad_inner, 0)
    scatter.one("inner")
    got_normed_two = pair_sum(
        lambda at: dot_nt(ref.grad_gate_up[at, :], weights_at(ref.full, inner)), 1, 3, ref.grad_hidden
    )
    got_branch = pair_sum(
        lambda at: dot_nt(ref.product[at, :], weights_at(ref.full, spans["mlp"])), 2, 4, ref.outputs
    )
    got_normed_two.wait_recv()
    ref.gain_rows[...] = jnp.zeros_like(ref.gain_rows)

    @row_loop(half, 128)
    def _(at):
        incoming = ref.grad_hidden[at, :] + ref.taken[1, at, :].astype(jnp.float32)
        unit = ref.unit_two[at, :]
        ref.gain_rows[1:2, :] += jnp.sum(incoming * unit, axis=0, keepdims=True)
        grad = ref.cot[at, :] + norm_backward(
            incoming, ref.gain[1:2, :], unit, ref.scale_two[at, 0:1]
        )
        ref.grad_hidden[at, :] = grad
        here = pl.ds(pl.multiple_of(own_at + at.start, 128), 128)
        ref.grad_low[here, :] = grad.astype(jnp.bfloat16)

    got_low = link.to_core(ref.grad_low.at[own, :], ref.grad_low.at[own, :], 7)
    weight_grad(ref.grad_rows, ref.product, ref.full, spans["mlp"][0])
    scatter.one("mlp")
    got_branch.wait_recv()

    @row_loop(half, 128)
    def _(at):
        ref.outputs[at, :] = (
            ref.outputs[at, :] + ref.hidden[at, :] + ref.taken[2, at, :].astype(jnp.float32)
        )

    got_low.wait_recv()

    @row_loop(rows, part)
    def _(at):
        ref.grad_context[at, :] = dot_nn(
            ref.grad_low[at, :], weights_at(ref.full, spans["out"])
        ).astype(jnp.bfloat16)

    @row_loop(rows, part)
    def _(at):
        ref.grad_rolled[at, :] = dot_nn(ref.perm[at, :], ref.grad_context[...]).astype(jnp.bfloat16)

    weight_grad(ref.grad_low, ref.context, ref.full, spans["out"][0])
    scatter.one("out")
    scatter.two("inner")

    def settle(name):
        total = scatter.four(name)
        hidden_here = ref.grad_mlp_out.shape[1]
        short = hidden_here - main
        if name == "inner":
            ref.grad_in[:, :main] = total[:, :main]
            ref.grad_in[:, main:hidden_here] = total[:, 2 * main : 2 * main + short]
            ref.grad_in[:, hidden_here : hidden_here + main] = total[:, main : 2 * main]
            ref.grad_in[:, hidden_here + main :] = total[:, 2 * main + short :]
        elif name == "mlp":
            ref.grad_mlp_out[...] = total[:, :hidden_here]
        elif name == "out":
            ref.grad_attn_out[...] = total
        elif name == "gains":
            turned = total.T
            ref.gains[...] = turned[0:2, :] + turned[8:10, :]
        else:
            pair = int(name[4:])
            for kind in range(3):
                ref.grad_qkv[kind, :, pair * LANES : (pair + 1) * LANES] = total[
                    :, kind * LANES : (kind + 1) * LANES
                ]

    def pull(pair, first):
        cols = slice(pair * LANES, (pair + 1) * LANES)
        base = 0 if first else half
        span = slice(base, base + half)

        @row_loop(half, part)
        def _(at):
            at = pl.ds(pl.multiple_of(base + at.start, part), part)
            ref.keys_t[:, at] = ref.keys[at, cols].astype(jnp.float32).T.astype(jnp.bfloat16)

        for step in range(half // part):
            at = pl.ds(base + step * part, part)
            lane = lax.broadcasted_iota(jnp.int32, (part, LANES), 1)
            query_pair = ref.queries[at, cols]
            grad_pair = ref.grad_rolled[at, cols]
            product = grad_pair.astype(jnp.float32) * ref.context_rolled[at, cols].astype(jnp.float32)
            product = product.T
            parts, all_probs, all_grads, all_queries, all_pulls = [], [], [], [], []
            for head in range(LANES // HEAD_DIM):
                query = jnp.where(lane // HEAD_DIM == head, query_pair, 0)
                grad = jnp.where(lane // HEAD_DIM == head, grad_pair, 0)
                probs = ref.probs[
                    unit_of(pair, head, first), :, step * part : (step + 1) * part
                ]
                grad_probs = dot_nt(ref.values[span, cols], grad)
                drop = jnp.sum(
                    product[head * HEAD_DIM : (head + 1) * HEAD_DIM], axis=0, keepdims=True
                )
                pulled = (probs.astype(jnp.float32) * (grad_probs - drop)).astype(jnp.bfloat16)
                all_probs.append(probs)
                all_grads.append(grad)
                all_queries.append(query)
                all_pulls.append(pulled)
                parts.append(
                    dot_nn(ref.keys_t[head * HEAD_DIM : (head + 1) * HEAD_DIM, span], pulled)
                )
            grad_values = dot_nn(
                jnp.concatenate(all_probs, axis=1), jnp.concatenate(all_grads, axis=0)
            )
            grad_keys = dot_nn(
                jnp.concatenate(all_pulls, axis=1), jnp.concatenate(all_queries, axis=0)
            )

            if step == 0:
                ref.acc[span, LANES : 2 * LANES] = grad_keys
                ref.acc[span, 2 * LANES :] = grad_values
            else:
                ref.acc[span, LANES : 2 * LANES] += grad_keys
                ref.acc[span, 2 * LANES :] += grad_values

            ref.acc[at, :LANES] = jnp.concatenate(parts, axis=0).T

    def unproject(pair):
        first = 3 * LANES * pair

        @row_loop(rows, part)
        def _(at):
            lane = lax.broadcasted_iota(jnp.int32, (part, LANES), 1)
            cosine, sine = ref.cosine[at, :], -ref.sine[at, :]
            grad_query = turn(ref.acc[at, :LANES], cosine, sine, lane) * SCALE
            grad_key = turn(ref.acc[at, LANES : 2 * LANES], cosine, sine, lane)
            ref.grad_three[at, :LANES] = grad_query.astype(jnp.bfloat16)
            ref.grad_three[at, LANES : 2 * LANES] = grad_key.astype(jnp.bfloat16)
            ref.grad_three[at, 2 * LANES :] = ref.acc[at, 2 * LANES :].astype(jnp.bfloat16)

        weight_grad(ref.rolled, ref.grad_three, ref.full, spans["gate"][0] + first)
        scatter.one("pair%d" % pair)

        @row_loop(rows, part)
        def _(at):
            ref.grad_projected[at, first : first + 3 * LANES] = dot_nn(
                ref.perm_back[at, :], ref.grad_three[...]
            ).astype(jnp.bfloat16)

    pull(0, True)
    scatter.two("mlp")
    pull(0, False)
    unproject(0)
    scatter.three("inner")
    pull(1, True)
    scatter.two("out")
    pull(1, False)
    scatter.three("mlp")
    unproject(1)
    pull(2, True)
    scatter.two("pair0")
    scatter.three("out")
    settle("inner")
    pull(2, False)
    unproject(2)
    scatter.three("pair0")
    scatter.two("pair1")
    settle("mlp")
    qkv_span = (spans["pair0"][0], 3 * pairs * LANES)
    got_one = pair_sum(
        lambda at: dot_nt(ref.grad_projected[at, :], weights_at(ref.full, qkv_span)),
        0, 5, ref.grad_tokens,
    )
    scatter.three("pair1")
    got_one.wait_recv()

    @row_loop(half, 128)
    def _(at):
        incoming = ref.grad_tokens[at, :] + ref.taken[0, at, :].astype(jnp.float32)
        unit = ref.unit_one[at, :]
        ref.gain_rows[0:1, :] += jnp.sum(incoming * unit, axis=0, keepdims=True)
        ref.grad_tokens[at, :] = ref.grad_hidden[at, :] + norm_backward(
            incoming, ref.gain[0:1, :], unit, ref.scale_one[at, 0:1]
        )

    got_gain = link.to_core(ref.gain_rows, ref.gain_other, 8)
    scatter.two("pair2")
    settle("out")
    got_gain.wait_recv()
    gain_rows = ref.gain_rows[...] + ref.gain_other[...]
    high = gain_rows.astype(jnp.bfloat16)
    rest = (gain_rows - high.astype(jnp.float32)).astype(jnp.bfloat16)
    slot = lax.broadcasted_iota(jnp.int32, (16, LANES), 0)
    lane = lax.broadcasted_iota(jnp.int32, (16, LANES), 1)
    pick = jnp.where(slot == lane, 1.0, 0.0).astype(jnp.bfloat16)
    columns = dot_tn(jnp.concatenate([high, rest], axis=0), pick).astype(jnp.bfloat16)
    ref.full[:, :, :, :, 0:LANES] = columns.reshape(4, 2, 2, width // 16, LANES)
    scatter.one("gains")
    settle("pair0")
    scatter.three("pair2")
    scatter.two("gains")
    settle("pair1")
    scatter.three("gains")
    settle("pair2")
    settle("gains")
    link.finish()


def call_layer(shards_here, tokens, cotangent, offsets, spans):
    half, width = tokens.shape
    rows = 2 * half
    height = shards_here["w_attn_out"].shape[0]
    total = spans["total"][1]
    width_here = spans["out"][1]
    hidden_here = shards_here["w_mlp_out"].shape[1]
    pairs = width_here // LANES
    main = spans["gate"][1]
    half_dim = HEAD_DIM // 2
    inverse = np.power(ROPE_BASE, -2.0 * np.arange(half_dim) / HEAD_DIM).astype(np.float32)
    inverse = jnp.asarray(np.tile(inverse, LANES // half_dim)[None, :])
    low, wide = jnp.bfloat16, jnp.float32
    outs = dict(
        outputs=((half, width), wide),
        grad_tokens=((half, width), wide),
        grad_qkv=((3, height, width_here), wide),
        grad_attn_out=((height, width_here), wide),
        grad_in=((height, 2 * hidden_here), wide),
        grad_mlp_out=((height, hidden_here), wide),
        gains=((2, height), wide),
    )
    chunk_count = 1 + pairs + 4
    kept = dict(
        full=((4, 2, 2, height, total), low),
        grad_inner=((4, 2, 2, height, 2 * main + LANES), low),
        low_one=((2, 2, height, total), low),
        high_one=((2, 2, height, total), low),
        low_two=((2, height, total), low),
        high_two=((2, height, total), low),
        far_sum=((3, height, total), low),
        normed=((rows, width), low),
        rolled=((rows, width), low),
        grad_rows=((rows, width), low),
        normed_mlp=((rows, width), low),
        perm=((rows, rows), low),
        perm_back=((rows, rows), low),
        bias=((half, half), wide),
        values_t=((LANES, rows), low),
        keys_t=((LANES, rows), low),
        queries=((rows, width_here), low),
        keys=((rows, width_here), low),
        values=((rows, width_here), low),
        context=((rows, width_here), low),
        context_rolled=((rows, width_here), low),
        probs=((2 * width_here // HEAD_DIM, half, half), low),
        grad_rolled=((rows, width_here), low),
        product=((rows, main + LANES), low),
        grad_gate_up=((rows, 2 * main + LANES), low),
        grad_product=((rows, main + LANES), wide),
        sent=((3, half, width), low),
        taken=((3, half, width), low),
        hidden=((half, width), wide),
        grad_hidden=((half, width), wide),
        unit_one=((half, width), wide),
        unit_two=((half, width), wide),
        scale_one=((half, LANES), wide),
        scale_two=((half, LANES), wide),
        cosine=((rows, LANES), wide),
        sine=((rows, LANES), wide),
        gain=((8, width), wide),
        gain_rows=((8, width), wide),
        gain_other=((8, width), wide),
    )
    kept.update(tok=((half, width), wide), cot=((half, width), wide))
    scratch = {name: pltpu.VMEM(*entry) for name, entry in kept.items()}
    scratch["fetch"] = pltpu.SemaphoreType.DMA((2,))
    for name, count in (
        ("far", 3 * chunk_count), ("near", 4 * chunk_count), ("core", 9), ("sum", 7 * (pairs + 4)),
    ):
        scratch[name + "_out"] = pltpu.SemaphoreType.DMA((count,))
        scratch[name + "_in"] = pltpu.SemaphoreType.DMA((count,))
    names = ["offsets", "tokens", "cotangent", "inverse"] + list(shards_here) + list(outs) + list(scratch)
    vmem = pl.BlockSpec(memory_space=pltpu.VMEM)
    results = pl.pallas_call(
        functools.partial(layer_kernel, names, spans),
        out_shape=[jax.ShapeDtypeStruct(*entry) for entry in outs.values()],
        in_specs=[pl.BlockSpec(memory_space=pltpu.SMEM)] + [pl.BlockSpec(memory_space=pl.ANY)] * 2 + [vmem] * (1 + len(shards_here)),
        out_specs=[vmem] * len(outs),
        scratch_shapes=list(scratch.values()),
        compiler_params=pltpu.CompilerParams(
            collective_id=0, has_side_effects=True, vmem_limit_bytes=63 * 1024 * 1024
        ),
        cost_estimate=pl.CostEstimate(
            flops=12 * 10**9, bytes_accessed=30 * 10**6, transcendentals=10**7
        ),
    )(offsets, tokens, cotangent, inverse, *shards_here.values())
    return types.SimpleNamespace(**dict(zip(outs, results)))


def fast_shards(tokens, offsets, w_qkv, w_attn_out, w_in, w_mlp_out, gain_attn, gain_mlp, cotangent):
    half = tokens.shape[0]
    height, _, width_here = w_qkv.shape
    hidden_here = w_in.shape[2]
    spans = fast_columns(width_here, hidden_here)
    shards_here = dict(
        w_qkv=w_qkv.transpose(1, 0, 2),
        w_attn_out=w_attn_out.T,
        w_in=w_in.reshape(height, -1),
        w_mlp_out=w_mlp_out.T,
        gain_one=gain_attn[None, :],
        gain_two=gain_mlp[None, :],
    )
    f = call_layer(shards_here, tokens, cotangent, offsets, spans)
    return (
        f.outputs,
        f.grad_tokens,
        f.grad_qkv.transpose(1, 0, 2),
        f.grad_attn_out.T,
        f.grad_in.reshape(height, 2, hidden_here),
        f.grad_mlp_out.T,
        f.gains[0],
        f.gains[1],
    )


def solution(mesh):
    in_specs = (
        P(("dp", "tensor"), None),
        P("dp", None),
        P("dp", None, "tensor"),
        P("tensor", "dp"),
        P("dp", None, "tensor"),
        P("tensor", "dp"),
        P("dp"),
        P("dp"),
        P(("dp", "tensor"), None),
    )
    out_specs = (
        P(("dp", "tensor"), None),
        P(("dp", "tensor"), None),
        P("dp", None, "tensor"),
        P("tensor", "dp"),
        P("dp", None, "tensor"),
        P("tensor", "dp"),
        P("dp"),
        P("dp"),
    )
    sizes = dict(mesh.shape)
    body = fast_shards if (sizes["dp"], sizes["tensor"]) == (16, 2) else shards
    return jax.shard_map(body, mesh=mesh, in_specs=in_specs, out_specs=out_specs, check_vma=False)
```

```python
import functools
import math
import types

import jax
import jax.numpy as jnp
import numpy as np
from jax import lax
from jax.experimental import pallas as pl
from jax.experimental.pallas import tpu as pltpu
from jax.sharding import PartitionSpec as P

HEAD_DIM = 64


EPSILON = 1e-05
ROPE_BASE = 160000.0
NEGATIVE = -1e30
LANES = 128
QUERY_BLOCK = 256
SCALE = 1.0 / math.sqrt(HEAD_DIM)
VMEM_LIMIT = 48 * 1024 * 1024


def seq_starts(offset_row, position):
    before = offset_row[None, :] <= position[:, None]
    return jnp.max(jnp.where(before, offset_row[None, :], 0), axis=1)


def rope_tables(position):
    half_dim = HEAD_DIM // 2
    inverse = jnp.power(
        jnp.float32(ROPE_BASE), -2.0 * jnp.arange(half_dim, dtype=jnp.float32) / HEAD_DIM
    )
    angles = position.astype(jnp.float32)[:, None] * inverse[None, :]
    copies = LANES // half_dim
    cosine = jnp.cos(angles)
    sine = jnp.sin(angles)
    return (
        jnp.concatenate([cosine] * copies, axis=1),
        jnp.concatenate([-sine, sine] * (copies // 2), axis=1),
    )


def levels_of(count):
    out = []
    stride = 1
    while stride < count:
        size = min(4, count // stride)
        out.append((stride, size))
        stride *= size
    return out


def swap_pairs(count, mask):
    return [(place, place ^ mask) for place in range(count)]


def send_step(held, stride, size):
    count = lax.axis_size("dp")
    return [held] + [
        lax.ppermute(held, "dp", swap_pairs(count, step * stride)) for step in range(1, size)
    ]


def place_step(taken, stride, size):
    mine = (lax.axis_index("dp") // stride) % size
    outer, height, width = taken[0].shape
    spread = jnp.zeros((outer, size, height, width), taken[0].dtype)
    for step in range(size):
        spread = lax.dynamic_update_slice(spread, taken[step][:, None], (0, mine ^ step, 0, 0))
    return spread.reshape(outer * size, height, width)


def after(later, *earlier):
    return lax.optimization_barrier((later, *earlier))[0]


def gather_both(first, second):
    one, two = first[None], second[None]
    taken = None
    for level in reversed(levels_of(lax.axis_size("dp"))):
        if taken is not None:
            two = place_step(taken, *last)
        one = place_step(send_step(one, *level), *level)
        taken = send_step(after(two, one), *level)
        last = level
    return one.reshape(-1, one.shape[2]), (taken, last)


def gather_rest(pending, *earlier):
    taken, level = pending
    taken = lax.optimization_barrier((taken, *earlier))[0]
    full = place_step(taken, *level)
    return full.reshape(-1, full.shape[2])


def sum_blocks(terms, *earlier):
    count = lax.axis_size("dp")
    me = lax.axis_index("dp")
    height = terms.shape[0] // count
    width = terms.shape[1]
    held = terms
    for stride, size in levels_of(count):
        mine = (me // stride) % size
        parts = held.reshape(-1, size, height, width)
        pick = lambda place: lax.dynamic_index_in_dim(parts, place, 1, keepdims=False)
        got = [
            lax.ppermute(pick(mine ^ step), "dp", swap_pairs(count, step * stride))
            for step in range(1, size)
        ]
        if earlier:
            got = lax.optimization_barrier((got, *earlier))[0]
            earlier = ()
        total = pick(mine).astype(jnp.float32)
        for other in got:
            total = total + other.astype(jnp.float32)
        held = total.astype(jnp.bfloat16)
    return total.reshape(height, width)


def other_half(local_rows):
    return lax.ppermute(local_rows, "tensor", [(0, 1), (1, 0)])


def spread_rows(local_rows):
    return jnp.concatenate([local_rows, other_half(local_rows)], axis=0)


def collect_own(partial_sums, rows_here):
    sent = other_half(partial_sums[rows_here:].astype(jnp.bfloat16))
    return partial_sums[:rows_here] + sent.astype(jnp.float32)


def collect_all(partial_sums, rows_here):
    got = other_half(partial_sums.astype(jnp.bfloat16))
    swapped = jnp.concatenate([got[rows_here:], got[:rows_here]], axis=0)
    return partial_sums + swapped.astype(jnp.float32)


def norm_parts(inputs_v):
    centre = inputs_v - jnp.mean(inputs_v, axis=-1, keepdims=True)
    spread = jnp.mean(centre * centre, axis=-1, keepdims=True)
    scale_v = lax.rsqrt(spread + EPSILON)
    return centre * scale_v, scale_v


def norm_backward(incoming, gain_v, unit, scale_v):
    scaled = incoming * gain_v
    mean_one = jnp.mean(scaled, axis=-1, keepdims=True)
    mean_two = jnp.mean(scaled * unit, axis=-1, keepdims=True)
    return scale_v * (scaled - mean_one - unit * mean_two)


def two_terms(column):
    high = column.astype(jnp.bfloat16)
    rest = (column - lax.reduce_precision(column, 8, 7)).astype(jnp.bfloat16)
    return jnp.stack([high, rest], axis=1)


def padded(pieces):
    width = sum(piece.shape[1] for piece in pieces)
    short = -width % 128
    height = pieces[0].shape[0]
    if short:
        pieces = pieces + [jnp.zeros((height, short), jnp.bfloat16)]
    return jnp.concatenate(pieces, axis=1)


def dot_nn(left, right):
    return jnp.dot(left, right, preferred_element_type=jnp.float32)


def dot_nt(left, right):
    return lax.dot_general(
        left, right, (((1,), (1,)), ((), ())), preferred_element_type=jnp.float32
    )


def dot_tn(left, right):
    return lax.dot_general(
        left, right, (((0,), (0,)), ((), ())), preferred_element_type=jnp.float32
    )


def turn(rows, cosine, sine_signed, lane):
    half_dim = HEAD_DIM // 2
    ahead = pltpu.roll(rows, rows.shape[1] - half_dim, axis=1)
    behind = pltpu.roll(rows, half_dim, axis=1)
    swapped = jnp.where(lane % HEAD_DIM < half_dim, ahead, behind)
    return rows * cosine + swapped * sine_signed


def forward_kernel(
    normed_ref, wq_ref, wk_ref, wv_ref, cos_ref, sin_ref, srow_ref, scol_ref,
    q_ref, k_ref, v_ref, ctx_ref, lse_ref, vt_ref,
):
    rows = normed_ref.shape[0]
    block = min(QUERY_BLOCK, rows)
    normed = normed_ref[...]
    cosine = cos_ref[...]
    sine = sin_ref[...]
    lane = lax.broadcasted_iota(jnp.int32, (rows, LANES), 1)
    dot = functools.partial(jnp.dot, preferred_element_type=jnp.float32)
    q_ref[...] = turn(dot(normed, wq_ref[...]), cosine, sine, lane).astype(jnp.bfloat16)
    k_ref[...] = turn(dot(normed, wk_ref[...]), cosine, sine, lane).astype(jnp.bfloat16)
    values = dot(normed, wv_ref[...])
    v_ref[...] = values.astype(jnp.bfloat16)
    vt_ref[...] = values.T.astype(jnp.bfloat16)

    @pl.loop(0, rows // block)
    def _(step):
        at = pl.ds(pl.multiple_of(step * block, block), block)
        same = scol_ref[...] == srow_ref[:, at]
        parts = []
        for head in range(LANES // HEAD_DIM):
            cols = slice(head * HEAD_DIM, (head + 1) * HEAD_DIM)
            scores = dot_nt(k_ref[:, cols], q_ref[at, cols]) * SCALE
            scores = jnp.where(same, scores, NEGATIVE)
            top = jnp.max(scores, axis=0, keepdims=True)
            terms = jnp.exp(scores - top)
            total = jnp.sum(terms, axis=0, keepdims=True)
            weights = (terms * (1.0 / total)).astype(jnp.bfloat16)
            parts.append(dot(vt_ref[cols, :], weights))
            lse_ref[0, head : head + 1, at] = top + jnp.log(total)
        ctx_ref[at, :] = jnp.concatenate(parts, axis=0).T.astype(jnp.bfloat16)


def backward_kernel(
    grad_ref, wo_ref, q_ref, k_ref, v_ref, cos_ref, sin_ref, srow_ref, scol_ref, lse_ref,
    dq_ref, dk_ref, dv_ref, g_ref, kt_ref, acc_q, acc_k, acc_v,
):
    rows = grad_ref.shape[0]
    block = min(QUERY_BLOCK, rows)
    dot = functools.partial(jnp.dot, preferred_element_type=jnp.float32)
    g_ref[...] = dot(grad_ref[...], wo_ref[...]).astype(jnp.bfloat16)
    kt_ref[...] = k_ref[...].astype(jnp.float32).T.astype(jnp.bfloat16)
    acc_k[...] = jnp.zeros_like(acc_k)
    acc_v[...] = jnp.zeros_like(acc_v)

    @pl.loop(0, rows // block)
    def _(step):
        at = pl.ds(pl.multiple_of(step * block, block), block)
        same = scol_ref[...] == srow_ref[:, at]
        parts = []
        for head in range(LANES // HEAD_DIM):
            cols = slice(head * HEAD_DIM, (head + 1) * HEAD_DIM)
            query = q_ref[at, cols]
            grad = g_ref[at, cols]
            scores = dot_nt(k_ref[:, cols], query) * SCALE
            probs = jnp.exp(jnp.where(same, scores - lse_ref[0, head : head + 1, at], NEGATIVE))
            acc_v[:, cols] += dot(probs.astype(jnp.bfloat16), grad)
            grad_probs = dot_nt(v_ref[:, cols], grad)
            weighted = probs * grad_probs
            drop = jnp.sum(weighted, axis=0, keepdims=True)
            grad_scores = (weighted - probs * drop).astype(jnp.bfloat16)
            acc_k[:, cols] += dot(grad_scores, query)
            parts.append(dot(kt_ref[cols, :], grad_scores))
        acc_q[at, :] = jnp.concatenate(parts, axis=0).T

    cosine = cos_ref[...] * SCALE
    sine = sin_ref[...] * -SCALE
    lane = lax.broadcasted_iota(jnp.int32, (rows, LANES), 1)
    dq_ref[...] = turn(acc_q[...], cosine, sine, lane).astype(jnp.bfloat16)
    dk_ref[...] = turn(acc_k[...], cosine, sine, lane).astype(jnp.bfloat16)
    dv_ref[...] = acc_v[...].astype(jnp.bfloat16)


def whole(shape):
    return pl.BlockSpec(shape, lambda pair: (0,) * len(shape))


def column_block(rows, first):
    return pl.BlockSpec((rows, LANES), lambda pair: (0, first + pair))


def attention_forward(normed_all, attn_pack, cosine, sine, starts, width_here):
    rows, width = normed_all.shape
    pairs = width_here // LANES
    heads_each = LANES // HEAD_DIM
    low = jax.ShapeDtypeStruct((rows, width_here), jnp.bfloat16)
    return pl.pallas_call(
        forward_kernel,
        grid=(pairs,),
        out_shape=(low, low, low, low, jax.ShapeDtypeStruct((pairs, heads_each, rows), jnp.float32)),
        in_specs=[
            whole((rows, width)),
            column_block(width, 0),
            column_block(width, pairs),
            column_block(width, 2 * pairs),
            whole((rows, LANES)),
            whole((rows, LANES)),
            whole((1, rows)),
            whole((rows, 1)),
        ],
        out_specs=[column_block(rows, 0)] * 4
        + [pl.BlockSpec((1, heads_each, rows), lambda pair: (pair, 0, 0))],
        scratch_shapes=[pltpu.VMEM((LANES, rows), jnp.bfloat16)],
        compiler_params=pltpu.CompilerParams(vmem_limit_bytes=VMEM_LIMIT),
        cost_estimate=pl.CostEstimate(
            flops=2 * rows * width * 3 * width_here + 4 * rows * rows * width_here,
            bytes_accessed=2 * (rows * width + 3 * width * width_here + 4 * rows * width_here),
            transcendentals=rows * rows * width_here // HEAD_DIM,
        ),
    )(normed_all, attn_pack, attn_pack, attn_pack, cosine, sine, starts[None, :], starts[:, None])


def attention_backward(grad_rows, attn_pack, queries, key_rows, values, cosine, sine, starts, lse):
    rows, width = grad_rows.shape
    width_here = queries.shape[1]
    pairs = width_here // LANES
    heads_each = LANES // HEAD_DIM
    low = jax.ShapeDtypeStruct((rows, width_here), jnp.bfloat16)
    return pl.pallas_call(
        backward_kernel,
        grid=(pairs,),
        out_shape=(low, low, low),
        in_specs=[
            whole((rows, width)),
            column_block(width, 0),
            column_block(rows, 0),
            column_block(rows, 0),
            column_block(rows, 0),
            whole((rows, LANES)),
            whole((rows, LANES)),
            whole((1, rows)),
            whole((rows, 1)),
            pl.BlockSpec((1, heads_each, rows), lambda pair: (pair, 0, 0)),
        ],
        out_specs=[column_block(rows, 0)] * 3,
        scratch_shapes=[
            pltpu.VMEM((rows, LANES), jnp.bfloat16),
            pltpu.VMEM((LANES, rows), jnp.bfloat16),
            pltpu.VMEM((rows, LANES), jnp.float32),
            pltpu.VMEM((rows, LANES), jnp.float32),
            pltpu.VMEM((rows, LANES), jnp.float32),
        ],
        compiler_params=pltpu.CompilerParams(vmem_limit_bytes=VMEM_LIMIT),
        cost_estimate=pl.CostEstimate(
            flops=2 * rows * width * width_here + 10 * rows * rows * width_here,
            bytes_accessed=2 * (rows * width + width * width_here + 7 * rows * width_here),
            transcendentals=rows * rows * width_here // HEAD_DIM,
        ),
    )(
        grad_rows, attn_pack, queries, key_rows, values, cosine, sine,
        starts[None, :], starts[:, None], lse,
    )


def shards(tokens, offsets, w_qkv, w_attn_out, w_in, w_mlp_out, gain_attn, gain_mlp, cotangent):
    rows_here = tokens.shape[0]
    group_rows = rows_here * lax.axis_size("tensor")
    model_here = w_qkv.shape[0]
    width_here = w_qkv.shape[2]
    hidden_here = w_in.shape[2]
    half_at = lax.axis_index("tensor") * rows_here
    position = (jnp.arange(group_rows, dtype=jnp.int32) + half_at) % group_rows
    starts = seq_starts(offsets[0], position)
    cosine_tab, sine_tab = rope_tables(position - starts)

    attn_pack, pending = gather_both(
        padded([w_qkv.reshape(model_here, 3 * width_here), gain_attn[:, None]]),
        padded(
            [w_attn_out.T, w_in.reshape(model_here, 2 * hidden_here), w_mlp_out.T, gain_mlp[:, None]]
        ),
    )
    gain_one = attn_pack[:, 3 * width_here].astype(jnp.float32)
    qkv_full = attn_pack[:, : 3 * width_here]

    token_rows = spread_rows(tokens)
    cotangent_rows = spread_rows(cotangent)
    grad_rows = cotangent_rows.astype(jnp.bfloat16)
    unit_one, scale_one = norm_parts(token_rows)
    normed_all = (unit_one * gain_one).astype(jnp.bfloat16)
    queries, key_rows, values, context, lse = attention_forward(
        normed_all, attn_pack, cosine_tab, sine_tab, starts, width_here
    )

    rest_pack = gather_rest(pending, lse)
    mlp_at = width_here
    mlp_end = width_here + 2 * hidden_here
    attn_out_full = rest_pack[:, :width_here]
    mlp_in_full = rest_pack[:, mlp_at:mlp_end]
    mlp_out_full = rest_pack[:, mlp_end : mlp_end + hidden_here]
    gain_two = rest_pack[:, mlp_end + hidden_here].astype(jnp.float32)
    attended = collect_all(dot_nt(context, attn_out_full), rows_here)
    hidden = token_rows + attended
    unit_two, scale_two = norm_parts(hidden)
    mlp_rows = (unit_two * gain_two).astype(jnp.bfloat16)
    gate_part = dot_nn(mlp_rows, mlp_in_full[:, :hidden_here])
    up_part = dot_nn(mlp_rows, mlp_in_full[:, hidden_here:])
    grad_product = dot_nn(grad_rows, mlp_out_full)
    bell = 0.5 * (1.0 + lax.erf(gate_part * math.sqrt(0.5)))
    activated = gate_part * bell
    slope = bell + gate_part * jnp.exp(-0.5 * gate_part * gate_part) * (1.0 / math.sqrt(2 * math.pi))
    product_rows = (activated * up_part).astype(jnp.bfloat16)
    grad_gate_up = jnp.concatenate(
        [
            (grad_product * up_part * slope).astype(jnp.bfloat16),
            (grad_product * activated).astype(jnp.bfloat16),
        ],
        axis=1,
    )
    grad_normed_two = collect_all(dot_nt(grad_gate_up, mlp_in_full), rows_here)
    grad_hidden = cotangent_rows + norm_backward(grad_normed_two, gain_two, unit_two, scale_two)
    grad_gain_two = jnp.sum((grad_normed_two * unit_two)[:rows_here], axis=0)
    grad_hidden_rows = grad_hidden.astype(jnp.bfloat16)
    grads_three = attention_backward(
        grad_hidden_rows, rest_pack, queries, key_rows, values,
        cosine_tab, sine_tab, starts, lse,
    )
    mlp_terms = padded(
        [
            dot_tn(mlp_rows, grad_gate_up).astype(jnp.bfloat16),
            dot_tn(grad_rows, product_rows).astype(jnp.bfloat16),
            two_terms(grad_gain_two),
        ]
    )
    mlp_sums = sum_blocks(mlp_terms, grads_three[0])
    branch = collect_own(dot_nt(product_rows, mlp_out_full), rows_here)
    outputs = hidden[:rows_here] + branch

    grad_projected = jnp.concatenate(grads_three, axis=1)
    grad_normed_one = collect_own(dot_nt(grad_projected, qkv_full), rows_here)
    grad_tokens = grad_hidden[:rows_here] + norm_backward(
        grad_normed_one, gain_one, unit_one[:rows_here], scale_one[:rows_here]
    )
    grad_gain_one = jnp.sum(grad_normed_one * unit_one[:rows_here], axis=0)
    attn_terms = padded(
        [
            dot_tn(normed_all, grad_projected).astype(jnp.bfloat16),
            dot_tn(grad_hidden_rows, context).astype(jnp.bfloat16),
            two_terms(grad_gain_one),
        ]
    )
    attn_sums = sum_blocks(attn_terms)

    gain_one_cols = attn_sums[:, 4 * width_here : 4 * width_here + 2].sum(axis=1)
    gain_two_cols = mlp_sums[:, 3 * hidden_here : 3 * hidden_here + 2].sum(axis=1)
    gains = jnp.stack([gain_one_cols, gain_two_cols])
    gains = gains + other_half(gains)
    return (
        outputs,
        grad_tokens,
        attn_sums[:, : 3 * width_here].reshape(model_here, 3, width_here),
        attn_sums[:, 3 * width_here : 4 * width_here].T,
        mlp_sums[:, : 2 * hidden_here].reshape(model_here, 2, hidden_here),
        mlp_sums[:, 2 * hidden_here : 3 * hidden_here].T,
        gains[0],
        gains[1],
    )


def fast_columns(width_here, hidden_here):
    main = hidden_here // LANES * LANES
    pairs = width_here // LANES
    at = {"gains": (0, LANES)}
    place = LANES
    for pair in range(pairs):
        at["pair%d" % pair] = (place, 3 * LANES)
        place += 3 * LANES
    for name, size in (
        ("out", width_here), ("mlp", main + LANES), ("gate", main), ("up", main), ("tail", LANES),
    ):
        at[name] = (place, size)
        place += size
    at["total"] = (0, place)
    return at


def pack_shards(ref, spans):
    height = ref.w_attn_out.shape[0]
    main = spans["gate"][1]
    hidden_here = ref.w_in.shape[1] // 2
    pairs = spans["out"][1] // LANES
    wide = jnp.float32
    down = lax.broadcasted_iota(jnp.int32, (height, height), 0)
    along = lax.broadcasted_iota(jnp.int32, (height, height), 1)
    lane = lax.broadcasted_iota(jnp.int32, (height, LANES), 1)
    gains = jnp.zeros((height, LANES), wide)
    for place, row in enumerate((ref.gain_one, ref.gain_two)):
        column = jnp.sum(jnp.where(down == along, row[...].astype(wide), 0.0), axis=1, keepdims=True)
        gains = jnp.where(lane == place, column, gains)
    pieces = [gains.astype(jnp.bfloat16)]
    for pair in range(pairs):
        for kind in range(3):
            pieces.append(ref.w_qkv[kind, :, pair * LANES : (pair + 1) * LANES])
    tail = jnp.concatenate(
        [ref.w_in[:, main:hidden_here], ref.w_in[:, hidden_here + main :]], axis=1
    )
    mlp = jnp.concatenate(
        [ref.w_mlp_out[...], jnp.zeros((height, main + LANES - hidden_here), jnp.bfloat16)], axis=1
    )
    pieces += [
        ref.w_attn_out[...],
        mlp,
        ref.w_in[:, :main],
        ref.w_in[:, hidden_here : hidden_here + main],
        tail,
    ]
    return pieces


class Links:
    def __init__(self, ref):
        self.ref = ref
        self.dp = lax.axis_index("dp")
        self.core = lax.axis_index("tensor")
        self.x = self.dp % 2
        self.y = (self.dp // 2) % 2
        self.z = self.dp // 4
        plane = self.dp % 4
        self.x_side = self.dp + 1 - 2 * self.x
        self.y_side = self.dp + 2 - 4 * self.y
        self.z_of = [None, self.z + 1 - 2 * (self.z % 2), (self.z + 2) % 4, 3 - self.z]
        self.z_side = [None] + [place * 4 + plane for place in self.z_of[1:]]
        self.started = []

    def enter(self):
        barrier = pltpu.get_barrier_semaphore()
        others = [(self.x_side, self.core), (self.y_side, self.core), (self.dp, 1 - self.core)]
        others += [(place, self.core) for place in self.z_side[1:]]
        for other in others:
            pl.semaphore_signal(
                barrier, inc=1, device_id=other, device_id_type=pl.DeviceIdType.MESH
            )
        pl.semaphore_wait(barrier, len(others))

    def copy(self, source, target, sems, place, device):
        return pltpu.make_async_remote_copy(
            src_ref=source,
            dst_ref=target,
            send_sem=sems[0].at[place],
            recv_sem=sems[1].at[place],
            device_id=device,
            device_id_type=pl.DeviceIdType.MESH,
        )

    def start(self, *copies):
        for copy in copies:
            copy.start()
            self.started.append(copy)

    def to_core(self, source, target, place):
        copy = self.copy(
            source, target, (self.ref.core_out, self.ref.core_in), place, (self.dp, 1 - self.core)
        )
        self.start(copy)
        return copy

    def finish(self):
        for copy in self.started:
            copy.wait_send()
        self.started = []


class Gather(Links):
    def __init__(self, ref, chunks):
        super().__init__(ref)
        self.chunks = chunks
        self.got = {}

    def send_z(self, name):
        chunk = list(self.chunks).index(name)
        cols = pl.ds(*self.chunks[name])
        block = self.ref.full.at[self.z, self.y, self.x, :, cols]
        copies = [
            self.copy(
                block, block, (self.ref.far_out, self.ref.far_in), 3 * chunk + step - 1,
                (self.z_side[step], self.core),
            )
            for step in (1, 2, 3)
        ]
        self.start(*copies)
        self.got[name] = copies

    def arrive(self, name):
        for copy in self.got[name]:
            copy.wait_recv()

    def near(self, name, stage, first, second):
        chunk = list(self.chunks).index(name)
        sems = (self.ref.near_out, self.ref.near_in)
        place = 4 * chunk + 2 * stage
        copies = [
            self.copy(first[0], first[0], sems, place, (first[1], self.core)),
            self.copy(second[0], second[0], sems, place + 1, (second[1], self.core)),
        ]
        self.arrive(name)
        self.start(*copies)
        self.got[name] = copies

    def send_one(self, name):
        cols = pl.ds(*self.chunks[name])
        low, high = pl.ds(0, 2), pl.ds(2, 2)
        full = self.ref.full
        self.near(
            name, 0,
            (full.at[low, self.y, self.x, :, cols], self.x_side),
            (full.at[high, self.y, self.x, :, cols], self.y_side),
        )

    def send_two(self, name):
        cols = pl.ds(*self.chunks[name])
        low, high = pl.ds(0, 2), pl.ds(2, 2)
        both = pl.ds(0, 2)
        full = self.ref.full
        self.near(
            name, 1,
            (full.at[low, self.y, both, :, cols], self.y_side),
            (full.at[high, both, self.x, :, cols], self.x_side),
        )


class Scatter:
    def __init__(self, link, chunks):
        self.link = link
        self.ref = link.ref
        self.chunks = chunks
        self.got = {}

    def send(self, name, stage, moves):
        sems = (self.ref.sum_out, self.ref.sum_in)
        place = 7 * list(self.chunks).index(name) + 2 * stage
        copies = [
            self.link.copy(source, target, sems, place + step, (side, self.link.core))
            for step, (source, target, side) in enumerate(moves)
        ]
        self.link.start(*copies)
        self.got[name] = copies

    def arrive(self, name):
        for copy in self.got[name]:
            copy.wait_recv()

    def parts(self, name):
        held, span, place = self.chunks[name]
        return held, pl.ds(*span), pl.ds(place, span[1])

    def one(self, name):
        link, ref = self.link, self.ref
        held, cols, to = self.parts(name)
        both = pl.ds(0, 2)
        self.send(name, 0, [
            (held.at[pl.ds(0, 2), 1 - link.y, both, :, cols], ref.low_one.at[:, :, :, to], link.y_side),
            (held.at[pl.ds(2, 2), both, 1 - link.x, :, cols], ref.high_one.at[:, :, :, to], link.x_side),
        ])

    def two(self, name):
        link, ref = self.link, self.ref
        held, cols, to = self.parts(name)
        both = pl.ds(0, 2)
        self.arrive(name)
        at = (pl.ds(0, 2), link.y, both, slice(None), cols)
        held[at] = held[at] + ref.low_one[:, :, :, to]
        at = (pl.ds(2, 2), both, link.x, slice(None), cols)
        held[at] = held[at] + ref.high_one[:, :, :, to]
        self.send(name, 1, [
            (held.at[pl.ds(0, 2), link.y, 1 - link.x, :, cols], ref.low_two.at[:, :, to], link.x_side),
            (held.at[pl.ds(2, 2), 1 - link.y, link.x, :, cols], ref.high_two.at[:, :, to], link.y_side),
        ])

    def three(self, name):
        link, ref = self.link, self.ref
        held, cols, to = self.parts(name)
        self.arrive(name)
        at = (pl.ds(0, 2), link.y, link.x, slice(None), cols)
        held[at] = held[at] + ref.low_two[:, :, to]
        at = (pl.ds(2, 2), link.y, link.x, slice(None), cols)
        held[at] = held[at] + ref.high_two[:, :, to]
        self.send(name, 2, [
            (
                held.at[link.z_of[step], link.y, link.x, :, cols],
                ref.far_sum.at[step - 1, :, to],
                link.z_side[step],
            )
            for step in (1, 2, 3)
        ])

    def four(self, name):
        link, ref = self.link, self.ref
        held, cols, to = self.parts(name)
        self.arrive(name)
        total = held[link.z, link.y, link.x, :, cols].astype(jnp.float32)
        for step in range(3):
            total = total + ref.far_sum[step, :, to].astype(jnp.float32)
        return total


def weights_at(full, span):
    block = full[:, :, :, :, span[0] : span[0] + span[1]]
    return block.reshape(-1, span[1])


def row_loop(rows, block):
    def wrap(body):
        @pl.loop(0, rows // block)
        def _(step):
            body(pl.ds(pl.multiple_of(step * block, block), block))

    return wrap


def layer_kernel(names, spans, *refs):
    ref = types.SimpleNamespace(**dict(zip(names, refs)))
    half, width = ref.tok.shape
    rows = 2 * half
    fetch_tok = pltpu.make_async_copy(ref.tokens, ref.tok, ref.fetch.at[0])
    fetch_cot = pltpu.make_async_copy(ref.cotangent, ref.cot, ref.fetch.at[1])
    fetch_tok.start()
    fetch_cot.start()
    pairs = (spans["out"][1]) // LANES
    main = spans["gate"][1]
    chunk_names = ["gains"] + ["pair%d" % pair for pair in range(pairs)] + ["out", "mlp"]
    chunks = {name: spans[name] for name in chunk_names}
    chunks["gate"] = spans["gate"]
    chunks["up"] = (spans["up"][0], main + LANES)
    link = Gather(ref, chunks)
    core = link.core
    own = pl.ds(pl.multiple_of(core * half, half), half)
    own_at = core * half
    other_at = (1 - core) * half
    part = 256

    ref.grad_low = ref.normed
    ref.grad_context = ref.product.at[:, : pairs * LANES]
    ref.grad_three = ref.product.at[:, : 3 * LANES]
    ref.grad_projected = ref.grad_gate_up
    ref.acc = ref.grad_product.at[:, : 3 * LANES]
    scatter = Scatter(
        link,
        {
            "inner": (ref.grad_inner, (0, 2 * main + LANES), spans["gate"][0]),
            "mlp": (ref.full, spans["mlp"], spans["mlp"][0]),
            "out": (ref.full, spans["out"], spans["out"][0]),
            **{
                "pair%d" % pair: (
                    ref.full,
                    (spans["gate"][0] + 3 * LANES * pair, 3 * LANES),
                    spans["pair%d" % pair][0],
                )
                for pair in range(pairs)
            },
            "gains": (ref.full, spans["gains"], spans["gains"][0]),
        },
    )

    place = 0
    for piece in pack_shards(ref, spans):
        wide = piece.shape[1]
        ref.full[link.z, link.y, link.x, :, place : place + wide] = piece
        place += wide
    link.enter()
    link.send_z("gains")
    link.send_z("pair0")
    link.send_z("pair1")

    fetch_tok.wait()

    @row_loop(half, 128)
    def _(at):
        unit, scale = norm_parts(ref.tok[at, :])
        ref.unit_one[at, :] = unit
        ref.scale_one[at, :] = jnp.broadcast_to(scale, (128, LANES))

    link.send_one("gains")

    shift = jnp.int32(0)
    for slot in range(ref.offsets.shape[1]):
        entry = ref.offsets[0, slot]
        shift = jnp.maximum(shift, jnp.where(entry <= half - 1, entry, 0))

    def source_of(place):
        moved = place + shift
        return jnp.where(moved >= rows, moved - rows, moved)

    def start_of(place):
        start = jnp.zeros_like(place)
        for slot in range(ref.offsets.shape[1]):
            entry = ref.offsets[0, slot]
            start = jnp.maximum(start, jnp.where(place >= entry, entry, 0))
        return start

    @row_loop(rows, part)
    def _(at):
        down = source_of(lax.broadcasted_iota(jnp.int32, (part, 1), 0) + at.start)
        along = lax.broadcasted_iota(jnp.int32, (part, rows), 1)
        ref.perm[at, :] = jnp.where(down == along, 1.0, 0.0).astype(jnp.bfloat16)
        down = lax.broadcasted_iota(jnp.int32, (part, rows), 0) + at.start
        along = source_of(lax.broadcasted_iota(jnp.int32, (1, rows), 1))
        ref.perm_back[at, :] = jnp.where(down == along, 1.0, 0.0).astype(jnp.bfloat16)

    link.send_two("gains")
    link.send_one("pair0")
    link.send_z("pair2")

    fetch_cot.wait()

    @row_loop(half, 128)
    def _(at):
        here = pl.ds(pl.multiple_of(own_at + at.start, 128), 128)
        ref.grad_rows[here, :] = ref.cot[at, :].astype(jnp.bfloat16)

    def table(at):
        place = source_of(lax.broadcasted_iota(jnp.int32, (part, LANES), 0) + at.start)
        start = start_of(place)
        angle = (place - start).astype(jnp.float32) * ref.inverse[...]
        lane = lax.broadcasted_iota(jnp.int32, (part, LANES), 1)
        sine = jnp.sin(angle)
        ref.cosine[at, :] = jnp.cos(angle)
        ref.sine[at, :] = jnp.where(lane % HEAD_DIM < HEAD_DIM // 2, -sine, sine)

    row_loop(half, part)(table)
    link.arrive("gains")
    slot = lax.broadcasted_iota(jnp.int32, (8, LANES), 0)
    lane = lax.broadcasted_iota(jnp.int32, (8, LANES), 1)
    pick = jnp.where(slot == lane, 1.0, 0.0).astype(jnp.bfloat16)
    ref.gain[...] = dot_nt(pick, weights_at(ref.full, spans["gains"]))

    @row_loop(half, 128)
    def _(at):
        here = pl.ds(pl.multiple_of(own_at + at.start, 128), 128)
        ref.normed[here, :] = (ref.unit_one[at, :] * ref.gain[0:1, :]).astype(jnp.bfloat16)

    got_normed = link.to_core(ref.normed.at[own, :], ref.normed.at[own, :], 1)
    got_grad = link.to_core(ref.grad_rows.at[own, :], ref.grad_rows.at[own, :], 0)
    link.send_one("pair1")
    link.send_z("out")

    @row_loop(half, part)
    def _(at):
        table(pl.ds(pl.multiple_of(half + at.start, part), part))

    key_start = start_of(source_of(lax.broadcasted_iota(jnp.int32, (half, 1), 0) + half))
    query_start = start_of(source_of(lax.broadcasted_iota(jnp.int32, (1, half), 1) + half))
    ref.bias[...] = jnp.where(key_start == query_start, 0.0, NEGATIVE)
    got_normed.wait_recv()
    link.send_two("pair0")

    @row_loop(rows, part)
    def _(at):
        ref.rolled[at, :] = dot_nn(ref.perm[at, :], ref.normed[...]).astype(jnp.bfloat16)

    link.send_one("pair2")
    link.send_z("mlp")

    def project(pair):
        if pair:
            link.arrive("pair%d" % pair)
        cols = slice(pair * LANES, (pair + 1) * LANES)

        @row_loop(rows, part)
        def _(at):
            three = dot_nn(ref.rolled[at, :], weights_at(ref.full, spans["pair%d" % pair]))
            lane = lax.broadcasted_iota(jnp.int32, (part, LANES), 1)
            cosine, sine = ref.cosine[at, :], ref.sine[at, :]
            query = turn(three[:, :LANES], cosine, sine, lane) * SCALE
            ref.queries[at, cols] = query.astype(jnp.bfloat16)
            ref.keys[at, cols] = turn(
                three[:, LANES : 2 * LANES], cosine, sine, lane
            ).astype(jnp.bfloat16)
            ref.values[at, cols] = three[:, 2 * LANES :].astype(jnp.bfloat16)
            ref.values_t[:, at] = three[:, 2 * LANES :].T.astype(jnp.bfloat16)

    def unit_of(pair, head, first):
        return (pair * (LANES // HEAD_DIM) + head) * 2 + (0 if first else 1)

    def attend(pair, first):
        cols = slice(pair * LANES, (pair + 1) * LANES)
        base = 0 if first else half

        for step in range(half // part):
            at = pl.ds(base + step * part, part)
            query_pair = ref.queries[at, cols]
            lane = lax.broadcasted_iota(jnp.int32, (part, LANES), 1)
            parts = []
            for head in range(LANES // HEAD_DIM):
                query = jnp.where(lane // HEAD_DIM == head, query_pair, 0)
                scores = dot_nt(ref.keys[base : base + half, cols], query)
                if not first:
                    scores = scores + ref.bias[:, step * part : (step + 1) * part]
                top = jnp.max(scores, axis=0, keepdims=True)
                terms = jnp.exp(scores - top)
                total = jnp.sum(terms, axis=0, keepdims=True)
                probs = (terms * (1.0 / total)).astype(jnp.bfloat16)
                ref.probs[
                    unit_of(pair, head, first), :, step * part : (step + 1) * part
                ] = probs
                parts.append(
                    dot_nn(
                        ref.values_t[head * HEAD_DIM : (head + 1) * HEAD_DIM, base : base + half],
                        probs,
                    )
                )
            ref.context_rolled[at, cols] = jnp.concatenate(parts, axis=0).T.astype(jnp.bfloat16)

    link.arrive("pair0")
    link.send_two("pair1")
    link.send_z("gate")
    project(0)
    link.send_one("out")
    attend(0, True)
    link.send_two("pair2")
    link.send_z("up")
    attend(0, False)
    link.send_one("mlp")
    project(1)
    link.send_two("out")
    attend(1, True)
    link.send_one("gate")
    attend(1, False)
    link.send_two("mlp")
    project(2)
    link.send_one("up")
    attend(2, True)
    link.send_two("gate")
    attend(2, False)

    @row_loop(rows, part)
    def _(at):
        ref.context[at, :] = dot_nn(ref.perm_back[at, :], ref.context_rolled[...]).astype(jnp.bfloat16)

    link.send_two("up")
    link.arrive("out")

    def pair_sum(product, place, sem, keep):
        @row_loop(half, part)
        def _(at):
            there = pl.ds(pl.multiple_of(other_at + at.start, part), part)
            ref.sent[place, at, :] = product(there).astype(jnp.bfloat16)

        got = link.to_core(ref.sent.at[place], ref.taken.at[place], sem)

        @row_loop(half, part)
        def _(at):
            here = pl.ds(pl.multiple_of(own_at + at.start, part), part)
            keep[at, :] = product(here)

        return got

    got_attended = pair_sum(
        lambda at: dot_nt(ref.context[at, :], weights_at(ref.full, spans["out"])), 0, 2, ref.hidden
    )
    got_attended.wait_recv()

    @row_loop(half, 128)
    def _(at):
        hidden = ref.tok[at, :] + ref.hidden[at, :] + ref.taken[0, at, :].astype(jnp.float32)
        ref.hidden[at, :] = hidden
        unit, scale = norm_parts(hidden)
        ref.unit_two[at, :] = unit
        ref.scale_two[at, :] = jnp.broadcast_to(scale, (128, LANES))
        here = pl.ds(pl.multiple_of(own_at + at.start, 128), 128)
        ref.normed_mlp[here, :] = (unit * ref.gain[1:2, :]).astype(jnp.bfloat16)

    got_mlp = link.to_core(ref.normed_mlp.at[own, :], ref.normed_mlp.at[own, :], 6)
    got_grad.wait_recv()
    link.arrive("mlp")

    @row_loop(rows, part)
    def _(at):
        ref.grad_product[at, :] = dot_nn(ref.grad_rows[at, :], weights_at(ref.full, spans["mlp"]))

    got_mlp.wait_recv()
    link.arrive("gate")
    link.arrive("up")

    def gated(gate, up, grad):
        bell = 0.5 * (1.0 + lax.erf(gate * math.sqrt(0.5)))
        activated = gate * bell
        slope = bell + gate * jnp.exp(-0.5 * gate * gate) * (1.0 / math.sqrt(2 * math.pi))
        return activated * up, grad * up * slope, grad * activated

    @row_loop(rows, part)
    def _(at):
        low = ref.normed_mlp[at, :]
        gate = dot_nn(low, weights_at(ref.full, spans["gate"]))
        up = dot_nn(low, weights_at(ref.full, spans["up"]))
        product, grad_gate, grad_up = gated(gate, up, ref.grad_product[at, :main])
        ref.product[at, :main] = product.astype(jnp.bfloat16)
        ref.grad_gate_up[at, :main] = grad_gate.astype(jnp.bfloat16)
        ref.grad_gate_up[at, main : 2 * main] = grad_up.astype(jnp.bfloat16)
        tail = dot_nn(low, weights_at(ref.full, spans["tail"]))
        product, grad_gate, grad_up = gated(
            tail, pltpu.roll(tail, LANES // 2, axis=1), ref.grad_product[at, main:]
        )
        lane = lax.broadcasted_iota(jnp.int32, (part, LANES), 1)
        lower = lane < LANES // 2
        ref.product[at, main:] = jnp.where(lower, product, 0.0).astype(jnp.bfloat16)
        ref.grad_gate_up[at, 2 * main :] = jnp.where(
            lower, grad_gate, pltpu.roll(grad_up, LANES // 2, axis=1)
        ).astype(jnp.bfloat16)

    inner = (spans["gate"][0], 2 * main + LANES)
    link.finish()

    def weight_grad(left, right, held, first):
        wide = right.shape[1]

        @pl.loop(0, 2)
        def _(step):
            cols = pl.ds(pl.multiple_of(step * (width // 2), LANES), width // 2)
            block = dot_tn(left[:, cols], right[...]).astype(jnp.bfloat16)
            held[pl.ds(2 * step, 2), :, :, :, first : first + wide] = block.reshape(
                2, 2, 2, width // 16, wide
            )

    weight_grad(ref.normed_mlp, ref.grad_gate_up, ref.grad_inner, 0)
    scatter.one("inner")
    got_normed_two = pair_sum(
        lambda at: dot_nt(ref.grad_gate_up[at, :], weights_at(ref.full, inner)), 1, 3, ref.grad_hidden
    )
    got_branch = pair_sum(
        lambda at: dot_nt(ref.product[at, :], weights_at(ref.full, spans["mlp"])), 2, 4, ref.outputs
    )
    got_normed_two.wait_recv()
    ref.gain_rows[...] = jnp.zeros_like(ref.gain_rows)

    @row_loop(half, 128)
    def _(at):
        incoming = ref.grad_hidden[at, :] + ref.taken[1, at, :].astype(jnp.float32)
        unit = ref.unit_two[at, :]
        ref.gain_rows[1:2, :] += jnp.sum(incoming * unit, axis=0, keepdims=True)
        grad = ref.cot[at, :] + norm_backward(
            incoming, ref.gain[1:2, :], unit, ref.scale_two[at, 0:1]
        )
        ref.grad_hidden[at, :] = grad
        here = pl.ds(pl.multiple_of(own_at + at.start, 128), 128)
        ref.grad_low[here, :] = grad.astype(jnp.bfloat16)

    got_low = link.to_core(ref.grad_low.at[own, :], ref.grad_low.at[own, :], 7)
    weight_grad(ref.grad_rows, ref.product, ref.full, spans["mlp"][0])
    scatter.one("mlp")
    got_branch.wait_recv()

    @row_loop(half, 128)
    def _(at):
        ref.outputs[at, :] = (
            ref.outputs[at, :] + ref.hidden[at, :] + ref.taken[2, at, :].astype(jnp.float32)
        )

    got_low.wait_recv()

    @row_loop(rows, part)
    def _(at):
        ref.grad_context[at, :] = dot_nn(
            ref.grad_low[at, :], weights_at(ref.full, spans["out"])
        ).astype(jnp.bfloat16)

    @row_loop(rows, part)
    def _(at):
        ref.grad_rolled[at, :] = dot_nn(ref.perm[at, :], ref.grad_context[...]).astype(jnp.bfloat16)

    weight_grad(ref.grad_low, ref.context, ref.full, spans["out"][0])
    scatter.one("out")
    scatter.two("inner")

    def settle(name):
        total = scatter.four(name)
        hidden_here = ref.grad_mlp_out.shape[1]
        short = hidden_here - main
        if name == "inner":
            ref.grad_gate[:, :main] = total[:, :main]
            ref.grad_gate[:, main:] = total[:, 2 * main : 2 * main + short]
            ref.grad_up[:, :main] = total[:, main : 2 * main]
            ref.grad_up[:, main:] = total[:, 2 * main + short :]
        elif name == "mlp":
            ref.grad_mlp_out[...] = total[:, :hidden_here]
        elif name == "out":
            ref.grad_attn_out[...] = total
        elif name == "gains":
            turned = total.T
            ref.gains[...] = turned[0:2, :] + turned[8:10, :]
        else:
            pair = int(name[4:])
            for kind in range(3):
                ref.grad_qkv[kind, :, pair * LANES : (pair + 1) * LANES] = total[
                    :, kind * LANES : (kind + 1) * LANES
                ]

    def pull(pair, first):
        cols = slice(pair * LANES, (pair + 1) * LANES)
        base = 0 if first else half
        span = slice(base, base + half)

        @row_loop(half, part)
        def _(at):
            at = pl.ds(pl.multiple_of(base + at.start, part), part)
            ref.keys_t[:, at] = ref.keys[at, cols].astype(jnp.float32).T.astype(jnp.bfloat16)

        for step in range(half // part):
            at = pl.ds(base + step * part, part)
            lane = lax.broadcasted_iota(jnp.int32, (part, LANES), 1)
            query_pair = ref.queries[at, cols]
            grad_pair = ref.grad_rolled[at, cols]
            product = grad_pair.astype(jnp.float32) * ref.context_rolled[at, cols].astype(jnp.float32)
            product = product.T
            parts, all_probs, all_grads, all_queries, all_pulls = [], [], [], [], []
            for head in range(LANES // HEAD_DIM):
                query = jnp.where(lane // HEAD_DIM == head, query_pair, 0)
                grad = jnp.where(lane // HEAD_DIM == head, grad_pair, 0)
                probs = ref.probs[
                    unit_of(pair, head, first), :, step * part : (step + 1) * part
                ]
                grad_probs = dot_nt(ref.values[span, cols], grad)
                drop = jnp.sum(
                    product[head * HEAD_DIM : (head + 1) * HEAD_DIM], axis=0, keepdims=True
                )
                pulled = (probs.astype(jnp.float32) * (grad_probs - drop)).astype(jnp.bfloat16)
                all_probs.append(probs)
                all_grads.append(grad)
                all_queries.append(query)
                all_pulls.append(pulled)
                parts.append(
                    dot_nn(ref.keys_t[head * HEAD_DIM : (head + 1) * HEAD_DIM, span], pulled)
                )
            grad_values = dot_nn(
                jnp.concatenate(all_probs, axis=1), jnp.concatenate(all_grads, axis=0)
            )
            grad_keys = dot_nn(
                jnp.concatenate(all_pulls, axis=1), jnp.concatenate(all_queries, axis=0)
            )

            if step == 0:
                ref.acc[span, LANES : 2 * LANES] = grad_keys
                ref.acc[span, 2 * LANES :] = grad_values
            else:
                ref.acc[span, LANES : 2 * LANES] += grad_keys
                ref.acc[span, 2 * LANES :] += grad_values

            ref.acc[at, :LANES] = jnp.concatenate(parts, axis=0).T

    def unproject(pair):
        first = 3 * LANES * pair

        @row_loop(rows, part)
        def _(at):
            lane = lax.broadcasted_iota(jnp.int32, (part, LANES), 1)
            cosine, sine = ref.cosine[at, :], -ref.sine[at, :]
            grad_query = turn(ref.acc[at, :LANES], cosine, sine, lane) * SCALE
            grad_key = turn(ref.acc[at, LANES : 2 * LANES], cosine, sine, lane)
            ref.grad_three[at, :LANES] = grad_query.astype(jnp.bfloat16)
            ref.grad_three[at, LANES : 2 * LANES] = grad_key.astype(jnp.bfloat16)
            ref.grad_three[at, 2 * LANES :] = ref.acc[at, 2 * LANES :].astype(jnp.bfloat16)

        weight_grad(ref.rolled, ref.grad_three, ref.full, spans["gate"][0] + first)
        scatter.one("pair%d" % pair)

        @row_loop(rows, part)
        def _(at):
            ref.grad_projected[at, first : first + 3 * LANES] = dot_nn(
                ref.perm_back[at, :], ref.grad_three[...]
            ).astype(jnp.bfloat16)

    pull(0, True)
    scatter.two("mlp")
    pull(0, False)
    unproject(0)
    scatter.three("inner")
    pull(1, True)
    scatter.two("out")
    pull(1, False)
    scatter.three("mlp")
    unproject(1)
    pull(2, True)
    scatter.two("pair0")
    scatter.three("out")
    settle("inner")
    pull(2, False)
    unproject(2)
    scatter.three("pair0")
    scatter.two("pair1")
    settle("mlp")
    qkv_span = (spans["pair0"][0], 3 * pairs * LANES)
    got_one = pair_sum(
        lambda at: dot_nt(ref.grad_projected[at, :], weights_at(ref.full, qkv_span)),
        0, 5, ref.grad_tokens,
    )
    scatter.three("pair1")
    got_one.wait_recv()

    @row_loop(half, 128)
    def _(at):
        incoming = ref.grad_tokens[at, :] + ref.taken[0, at, :].astype(jnp.float32)
        unit = ref.unit_one[at, :]
        ref.gain_rows[0:1, :] += jnp.sum(incoming * unit, axis=0, keepdims=True)
        ref.grad_tokens[at, :] = ref.grad_hidden[at, :] + norm_backward(
            incoming, ref.gain[0:1, :], unit, ref.scale_one[at, 0:1]
        )

    got_gain = link.to_core(ref.gain_rows, ref.gain_other, 8)
    scatter.two("pair2")
    settle("out")
    got_gain.wait_recv()
    gain_rows = ref.gain_rows[...] + ref.gain_other[...]
    high = gain_rows.astype(jnp.bfloat16)
    rest = (gain_rows - high.astype(jnp.float32)).astype(jnp.bfloat16)
    slot = lax.broadcasted_iota(jnp.int32, (16, LANES), 0)
    lane = lax.broadcasted_iota(jnp.int32, (16, LANES), 1)
    pick = jnp.where(slot == lane, 1.0, 0.0).astype(jnp.bfloat16)
    columns = dot_tn(jnp.concatenate([high, rest], axis=0), pick).astype(jnp.bfloat16)
    ref.full[:, :, :, :, 0:LANES] = columns.reshape(4, 2, 2, width // 16, LANES)
    scatter.one("gains")
    settle("pair0")
    scatter.three("pair2")
    scatter.two("gains")
    settle("pair1")
    scatter.three("gains")
    settle("pair2")
    settle("gains")
    link.finish()


def call_layer(shards_here, tokens, cotangent, offsets, spans):
    half, width = tokens.shape
    rows = 2 * half
    height = shards_here["w_attn_out"].shape[0]
    total = spans["total"][1]
    width_here = spans["out"][1]
    hidden_here = shards_here["w_mlp_out"].shape[1]
    pairs = width_here // LANES
    main = spans["gate"][1]
    half_dim = HEAD_DIM // 2
    inverse = np.power(ROPE_BASE, -2.0 * np.arange(half_dim) / HEAD_DIM).astype(np.float32)
    inverse = jnp.asarray(np.tile(inverse, LANES // half_dim)[None, :])
    low, wide = jnp.bfloat16, jnp.float32
    outs = dict(
        outputs=((half, width), wide),
        grad_tokens=((half, width), wide),
        grad_qkv=((3, height, width_here), wide),
        grad_attn_out=((height, width_here), wide),
        grad_gate=((height, hidden_here), wide),
        grad_up=((height, hidden_here), wide),
        grad_mlp_out=((height, hidden_here), wide),
        gains=((2, height), wide),
    )
    chunk_count = 1 + pairs + 4
    kept = dict(
        full=((4, 2, 2, height, total), low),
        grad_inner=((4, 2, 2, height, 2 * main + LANES), low),
        low_one=((2, 2, height, total), low),
        high_one=((2, 2, height, total), low),
        low_two=((2, height, total), low),
        high_two=((2, height, total), low),
        far_sum=((3, height, total), low),
        normed=((rows, width), low),
        rolled=((rows, width), low),
        grad_rows=((rows, width), low),
        normed_mlp=((rows, width), low),
        perm=((rows, rows), low),
        perm_back=((rows, rows), low),
        bias=((half, half), wide),
        values_t=((LANES, rows), low),
        keys_t=((LANES, rows), low),
        queries=((rows, width_here), low),
        keys=((rows, width_here), low),
        values=((rows, width_here), low),
        context=((rows, width_here), low),
        context_rolled=((rows, width_here), low),
        probs=((2 * width_here // HEAD_DIM, half, half), low),
        grad_rolled=((rows, width_here), low),
        product=((rows, main + LANES), low),
        grad_gate_up=((rows, 2 * main + LANES), low),
        grad_product=((rows, main + LANES), wide),
        sent=((3, half, width), low),
        taken=((3, half, width), low),
        hidden=((half, width), wide),
        grad_hidden=((half, width), wide),
        unit_one=((half, width), wide),
        unit_two=((half, width), wide),
        scale_one=((half, LANES), wide),
        scale_two=((half, LANES), wide),
        cosine=((rows, LANES), wide),
        sine=((rows, LANES), wide),
        gain=((8, width), wide),
        gain_rows=((8, width), wide),
        gain_other=((8, width), wide),
    )
    kept.update(tok=((half, width), wide), cot=((half, width), wide))
    scratch = {name: pltpu.VMEM(*entry) for name, entry in kept.items()}
    scratch["fetch"] = pltpu.SemaphoreType.DMA((2,))
    for name, count in (
        ("far", 3 * chunk_count), ("near", 4 * chunk_count), ("core", 9), ("sum", 7 * (pairs + 4)),
    ):
        scratch[name + "_out"] = pltpu.SemaphoreType.DMA((count,))
        scratch[name + "_in"] = pltpu.SemaphoreType.DMA((count,))
    names = ["offsets", "tokens", "cotangent", "inverse"] + list(shards_here) + list(outs) + list(scratch)
    vmem = pl.BlockSpec(memory_space=pltpu.VMEM)
    results = pl.pallas_call(
        functools.partial(layer_kernel, names, spans),
        out_shape=[jax.ShapeDtypeStruct(*entry) for entry in outs.values()],
        in_specs=[pl.BlockSpec(memory_space=pltpu.SMEM)] + [pl.BlockSpec(memory_space=pl.ANY)] * 2 + [vmem] * (1 + len(shards_here)),
        out_specs=[vmem] * len(outs),
        scratch_shapes=list(scratch.values()),
        compiler_params=pltpu.CompilerParams(
            collective_id=0, has_side_effects=True, vmem_limit_bytes=63 * 1024 * 1024
        ),
        cost_estimate=pl.CostEstimate(
            flops=12 * 10**9, bytes_accessed=30 * 10**6, transcendentals=10**7
        ),
    )(offsets, tokens, cotangent, inverse, *shards_here.values())
    return types.SimpleNamespace(**dict(zip(outs, results)))


def fast_shards(tokens, offsets, w_qkv, w_attn_out, w_in, w_mlp_out, gain_attn, gain_mlp, cotangent):
    half = tokens.shape[0]
    height, _, width_here = w_qkv.shape
    hidden_here = w_in.shape[2]
    spans = fast_columns(width_here, hidden_here)
    shards_here = dict(
        w_qkv=w_qkv.transpose(1, 0, 2),
        w_attn_out=w_attn_out.T,
        w_in=w_in.reshape(height, -1),
        w_mlp_out=w_mlp_out.T,
        gain_one=gain_attn[None, :],
        gain_two=gain_mlp[None, :],
    )
    f = call_layer(shards_here, tokens, cotangent, offsets, spans)
    return (
        f.outputs,
        f.grad_tokens,
        f.grad_qkv.transpose(1, 0, 2),
        f.grad_attn_out.T,
        jnp.stack([f.grad_gate, f.grad_up], axis=1),
        f.grad_mlp_out.T,
        f.gains[0],
        f.gains[1],
    )


def solution(mesh):
    in_specs = (
        P(("dp", "tensor"), None),
        P("dp", None),
        P("dp", None, "tensor"),
        P("tensor", "dp"),
        P("dp", None, "tensor"),
        P("tensor", "dp"),
        P("dp"),
        P("dp"),
        P(("dp", "tensor"), None),
    )
    out_specs = (
        P(("dp", "tensor"), None),
        P(("dp", "tensor"), None),
        P("dp", None, "tensor"),
        P("tensor", "dp"),
        P("dp", None, "tensor"),
        P("tensor", "dp"),
        P("dp"),
        P("dp"),
    )
    sizes = dict(mesh.shape)
    body = fast_shards if (sizes["dp"], sizes["tensor"]) == (16, 2) else shards
    return jax.shard_map(body, mesh=mesh, in_specs=in_specs, out_specs=out_specs, check_vma=False)
```

```python
import functools
import math
import types

import jax
import jax.numpy as jnp
import numpy as np
from jax import lax
from jax.experimental import pallas as pl
from jax.experimental.pallas import tpu as pltpu
from jax.sharding import PartitionSpec as P

HEAD_DIM = 64


EPSILON = 1e-05
ROPE_BASE = 160000.0
NEGATIVE = -1e30
LANES = 128
QUERY_BLOCK = 256
SCALE = 1.0 / math.sqrt(HEAD_DIM)
VMEM_LIMIT = 48 * 1024 * 1024


def seq_starts(offset_row, position):
    before = offset_row[None, :] <= position[:, None]
    return jnp.max(jnp.where(before, offset_row[None, :], 0), axis=1)


def rope_tables(position):
    half_dim = HEAD_DIM // 2
    inverse = jnp.power(
        jnp.float32(ROPE_BASE), -2.0 * jnp.arange(half_dim, dtype=jnp.float32) / HEAD_DIM
    )
    angles = position.astype(jnp.float32)[:, None] * inverse[None, :]
    copies = LANES // half_dim
    cosine = jnp.cos(angles)
    sine = jnp.sin(angles)
    return (
        jnp.concatenate([cosine] * copies, axis=1),
        jnp.concatenate([-sine, sine] * (copies // 2), axis=1),
    )


def levels_of(count):
    out = []
    stride = 1
    while stride < count:
        size = min(4, count // stride)
        out.append((stride, size))
        stride *= size
    return out


def swap_pairs(count, mask):
    return [(place, place ^ mask) for place in range(count)]


def send_step(held, stride, size):
    count = lax.axis_size("dp")
    return [held] + [
        lax.ppermute(held, "dp", swap_pairs(count, step * stride)) for step in range(1, size)
    ]


def place_step(taken, stride, size):
    mine = (lax.axis_index("dp") // stride) % size
    outer, height, width = taken[0].shape
    spread = jnp.zeros((outer, size, height, width), taken[0].dtype)
    for step in range(size):
        spread = lax.dynamic_update_slice(spread, taken[step][:, None], (0, mine ^ step, 0, 0))
    return spread.reshape(outer * size, height, width)


def after(later, *earlier):
    return lax.optimization_barrier((later, *earlier))[0]


def gather_both(first, second):
    one, two = first[None], second[None]
    taken = None
    for level in reversed(levels_of(lax.axis_size("dp"))):
        if taken is not None:
            two = place_step(taken, *last)
        one = place_step(send_step(one, *level), *level)
        taken = send_step(after(two, one), *level)
        last = level
    return one.reshape(-1, one.shape[2]), (taken, last)


def gather_rest(pending, *earlier):
    taken, level = pending
    taken = lax.optimization_barrier((taken, *earlier))[0]
    full = place_step(taken, *level)
    return full.reshape(-1, full.shape[2])


def sum_blocks(terms, *earlier):
    count = lax.axis_size("dp")
    me = lax.axis_index("dp")
    height = terms.shape[0] // count
    width = terms.shape[1]
    held = terms
    for stride, size in levels_of(count):
        mine = (me // stride) % size
        parts = held.reshape(-1, size, height, width)
        pick = lambda place: lax.dynamic_index_in_dim(parts, place, 1, keepdims=False)
        got = [
            lax.ppermute(pick(mine ^ step), "dp", swap_pairs(count, step * stride))
            for step in range(1, size)
        ]
        if earlier:
            got = lax.optimization_barrier((got, *earlier))[0]
            earlier = ()
        total = pick(mine).astype(jnp.float32)
        for other in got:
            total = total + other.astype(jnp.float32)
        held = total.astype(jnp.bfloat16)
    return total.reshape(height, width)


def other_half(local_rows):
    return lax.ppermute(local_rows, "tensor", [(0, 1), (1, 0)])


def spread_rows(local_rows):
    return jnp.concatenate([local_rows, other_half(local_rows)], axis=0)


def collect_own(partial_sums, rows_here):
    sent = other_half(partial_sums[rows_here:].astype(jnp.bfloat16))
    return partial_sums[:rows_here] + sent.astype(jnp.float32)


def collect_all(partial_sums, rows_here):
    got = other_half(partial_sums.astype(jnp.bfloat16))
    swapped = jnp.concatenate([got[rows_here:], got[:rows_here]], axis=0)
    return partial_sums + swapped.astype(jnp.float32)


def norm_parts(inputs_v):
    centre = inputs_v - jnp.mean(inputs_v, axis=-1, keepdims=True)
    spread = jnp.mean(centre * centre, axis=-1, keepdims=True)
    scale_v = lax.rsqrt(spread + EPSILON)
    return centre * scale_v, scale_v


def norm_backward(incoming, gain_v, unit, scale_v):
    scaled = incoming * gain_v
    mean_one = jnp.mean(scaled, axis=-1, keepdims=True)
    mean_two = jnp.mean(scaled * unit, axis=-1, keepdims=True)
    return scale_v * (scaled - mean_one - unit * mean_two)


def two_terms(column):
    high = column.astype(jnp.bfloat16)
    rest = (column - lax.reduce_precision(column, 8, 7)).astype(jnp.bfloat16)
    return jnp.stack([high, rest], axis=1)


def padded(pieces):
    width = sum(piece.shape[1] for piece in pieces)
    short = -width % 128
    height = pieces[0].shape[0]
    if short:
        pieces = pieces + [jnp.zeros((height, short), jnp.bfloat16)]
    return jnp.concatenate(pieces, axis=1)


def dot_nn(left, right):
    return jnp.dot(left, right, preferred_element_type=jnp.float32)


def dot_nt(left, right):
    return lax.dot_general(
        left, right, (((1,), (1,)), ((), ())), preferred_element_type=jnp.float32
    )


def dot_tn(left, right):
    return lax.dot_general(
        left, right, (((0,), (0,)), ((), ())), preferred_element_type=jnp.float32
    )


def turn(rows, cosine, sine_signed, lane):
    half_dim = HEAD_DIM // 2
    ahead = pltpu.roll(rows, rows.shape[1] - half_dim, axis=1)
    behind = pltpu.roll(rows, half_dim, axis=1)
    swapped = jnp.where(lane % HEAD_DIM < half_dim, ahead, behind)
    return rows * cosine + swapped * sine_signed


def forward_kernel(
    normed_ref, wq_ref, wk_ref, wv_ref, cos_ref, sin_ref, srow_ref, scol_ref,
    q_ref, k_ref, v_ref, ctx_ref, lse_ref, vt_ref,
):
    rows = normed_ref.shape[0]
    block = min(QUERY_BLOCK, rows)
    normed = normed_ref[...]
    cosine = cos_ref[...]
    sine = sin_ref[...]
    lane = lax.broadcasted_iota(jnp.int32, (rows, LANES), 1)
    dot = functools.partial(jnp.dot, preferred_element_type=jnp.float32)
    q_ref[...] = turn(dot(normed, wq_ref[...]), cosine, sine, lane).astype(jnp.bfloat16)
    k_ref[...] = turn(dot(normed, wk_ref[...]), cosine, sine, lane).astype(jnp.bfloat16)
    values = dot(normed, wv_ref[...])
    v_ref[...] = values.astype(jnp.bfloat16)
    vt_ref[...] = values.T.astype(jnp.bfloat16)

    @pl.loop(0, rows // block)
    def _(step):
        at = pl.ds(pl.multiple_of(step * block, block), block)
        same = scol_ref[...] == srow_ref[:, at]
        parts = []
        for head in range(LANES // HEAD_DIM):
            cols = slice(head * HEAD_DIM, (head + 1) * HEAD_DIM)
            scores = dot_nt(k_ref[:, cols], q_ref[at, cols]) * SCALE
            scores = jnp.where(same, scores, NEGATIVE)
            top = jnp.max(scores, axis=0, keepdims=True)
            terms = jnp.exp(scores - top)
            total = jnp.sum(terms, axis=0, keepdims=True)
            weights = (terms * (1.0 / total)).astype(jnp.bfloat16)
            parts.append(dot(vt_ref[cols, :], weights))
            lse_ref[0, head : head + 1, at] = top + jnp.log(total)
        ctx_ref[at, :] = jnp.concatenate(parts, axis=0).T.astype(jnp.bfloat16)


def backward_kernel(
    grad_ref, wo_ref, q_ref, k_ref, v_ref, cos_ref, sin_ref, srow_ref, scol_ref, lse_ref,
    dq_ref, dk_ref, dv_ref, g_ref, kt_ref, acc_q, acc_k, acc_v,
):
    rows = grad_ref.shape[0]
    block = min(QUERY_BLOCK, rows)
    dot = functools.partial(jnp.dot, preferred_element_type=jnp.float32)
    g_ref[...] = dot(grad_ref[...], wo_ref[...]).astype(jnp.bfloat16)
    kt_ref[...] = k_ref[...].astype(jnp.float32).T.astype(jnp.bfloat16)
    acc_k[...] = jnp.zeros_like(acc_k)
    acc_v[...] = jnp.zeros_like(acc_v)

    @pl.loop(0, rows // block)
    def _(step):
        at = pl.ds(pl.multiple_of(step * block, block), block)
        same = scol_ref[...] == srow_ref[:, at]
        parts = []
        for head in range(LANES // HEAD_DIM):
            cols = slice(head * HEAD_DIM, (head + 1) * HEAD_DIM)
            query = q_ref[at, cols]
            grad = g_ref[at, cols]
            scores = dot_nt(k_ref[:, cols], query) * SCALE
            probs = jnp.exp(jnp.where(same, scores - lse_ref[0, head : head + 1, at], NEGATIVE))
            acc_v[:, cols] += dot(probs.astype(jnp.bfloat16), grad)
            grad_probs = dot_nt(v_ref[:, cols], grad)
            weighted = probs * grad_probs
            drop = jnp.sum(weighted, axis=0, keepdims=True)
            grad_scores = (weighted - probs * drop).astype(jnp.bfloat16)
            acc_k[:, cols] += dot(grad_scores, query)
            parts.append(dot(kt_ref[cols, :], grad_scores))
        acc_q[at, :] = jnp.concatenate(parts, axis=0).T

    cosine = cos_ref[...] * SCALE
    sine = sin_ref[...] * -SCALE
    lane = lax.broadcasted_iota(jnp.int32, (rows, LANES), 1)
    dq_ref[...] = turn(acc_q[...], cosine, sine, lane).astype(jnp.bfloat16)
    dk_ref[...] = turn(acc_k[...], cosine, sine, lane).astype(jnp.bfloat16)
    dv_ref[...] = acc_v[...].astype(jnp.bfloat16)


def whole(shape):
    return pl.BlockSpec(shape, lambda pair: (0,) * len(shape))


def column_block(rows, first):
    return pl.BlockSpec((rows, LANES), lambda pair: (0, first + pair))


def attention_forward(normed_all, attn_pack, cosine, sine, starts, width_here):
    rows, width = normed_all.shape
    pairs = width_here // LANES
    heads_each = LANES // HEAD_DIM
    low = jax.ShapeDtypeStruct((rows, width_here), jnp.bfloat16)
    return pl.pallas_call(
        forward_kernel,
        grid=(pairs,),
        out_shape=(low, low, low, low, jax.ShapeDtypeStruct((pairs, heads_each, rows), jnp.float32)),
        in_specs=[
            whole((rows, width)),
            column_block(width, 0),
            column_block(width, pairs),
            column_block(width, 2 * pairs),
            whole((rows, LANES)),
            whole((rows, LANES)),
            whole((1, rows)),
            whole((rows, 1)),
        ],
        out_specs=[column_block(rows, 0)] * 4
        + [pl.BlockSpec((1, heads_each, rows), lambda pair: (pair, 0, 0))],
        scratch_shapes=[pltpu.VMEM((LANES, rows), jnp.bfloat16)],
        compiler_params=pltpu.CompilerParams(vmem_limit_bytes=VMEM_LIMIT),
        cost_estimate=pl.CostEstimate(
            flops=2 * rows * width * 3 * width_here + 4 * rows * rows * width_here,
            bytes_accessed=2 * (rows * width + 3 * width * width_here + 4 * rows * width_here),
            transcendentals=rows * rows * width_here // HEAD_DIM,
        ),
    )(normed_all, attn_pack, attn_pack, attn_pack, cosine, sine, starts[None, :], starts[:, None])


def attention_backward(grad_rows, attn_pack, queries, key_rows, values, cosine, sine, starts, lse):
    rows, width = grad_rows.shape
    width_here = queries.shape[1]
    pairs = width_here // LANES
    heads_each = LANES // HEAD_DIM
    low = jax.ShapeDtypeStruct((rows, width_here), jnp.bfloat16)
    return pl.pallas_call(
        backward_kernel,
        grid=(pairs,),
        out_shape=(low, low, low),
        in_specs=[
            whole((rows, width)),
            column_block(width, 0),
            column_block(rows, 0),
            column_block(rows, 0),
            column_block(rows, 0),
            whole((rows, LANES)),
            whole((rows, LANES)),
            whole((1, rows)),
            whole((rows, 1)),
            pl.BlockSpec((1, heads_each, rows), lambda pair: (pair, 0, 0)),
        ],
        out_specs=[column_block(rows, 0)] * 3,
        scratch_shapes=[
            pltpu.VMEM((rows, LANES), jnp.bfloat16),
            pltpu.VMEM((LANES, rows), jnp.bfloat16),
            pltpu.VMEM((rows, LANES), jnp.float32),
            pltpu.VMEM((rows, LANES), jnp.float32),
            pltpu.VMEM((rows, LANES), jnp.float32),
        ],
        compiler_params=pltpu.CompilerParams(vmem_limit_bytes=VMEM_LIMIT),
        cost_estimate=pl.CostEstimate(
            flops=2 * rows * width * width_here + 10 * rows * rows * width_here,
            bytes_accessed=2 * (rows * width + width * width_here + 7 * rows * width_here),
            transcendentals=rows * rows * width_here // HEAD_DIM,
        ),
    )(
        grad_rows, attn_pack, queries, key_rows, values, cosine, sine,
        starts[None, :], starts[:, None], lse,
    )


def shards(tokens, offsets, w_qkv, w_attn_out, w_in, w_mlp_out, gain_attn, gain_mlp, cotangent):
    rows_here = tokens.shape[0]
    group_rows = rows_here * lax.axis_size("tensor")
    model_here = w_qkv.shape[0]
    width_here = w_qkv.shape[2]
    hidden_here = w_in.shape[2]
    half_at = lax.axis_index("tensor") * rows_here
    position = (jnp.arange(group_rows, dtype=jnp.int32) + half_at) % group_rows
    starts = seq_starts(offsets[0], position)
    cosine_tab, sine_tab = rope_tables(position - starts)

    attn_pack, pending = gather_both(
        padded([w_qkv.reshape(model_here, 3 * width_here), gain_attn[:, None]]),
        padded(
            [w_attn_out.T, w_in.reshape(model_here, 2 * hidden_here), w_mlp_out.T, gain_mlp[:, None]]
        ),
    )
    gain_one = attn_pack[:, 3 * width_here].astype(jnp.float32)
    qkv_full = attn_pack[:, : 3 * width_here]

    token_rows = spread_rows(tokens)
    cotangent_rows = spread_rows(cotangent)
    grad_rows = cotangent_rows.astype(jnp.bfloat16)
    unit_one, scale_one = norm_parts(token_rows)
    normed_all = (unit_one * gain_one).astype(jnp.bfloat16)
    queries, key_rows, values, context, lse = attention_forward(
        normed_all, attn_pack, cosine_tab, sine_tab, starts, width_here
    )

    rest_pack = gather_rest(pending, lse)
    mlp_at = width_here
    mlp_end = width_here + 2 * hidden_here
    attn_out_full = rest_pack[:, :width_here]
    mlp_in_full = rest_pack[:, mlp_at:mlp_end]
    mlp_out_full = rest_pack[:, mlp_end : mlp_end + hidden_here]
    gain_two = rest_pack[:, mlp_end + hidden_here].astype(jnp.float32)
    attended = collect_all(dot_nt(context, attn_out_full), rows_here)
    hidden = token_rows + attended
    unit_two, scale_two = norm_parts(hidden)
    mlp_rows = (unit_two * gain_two).astype(jnp.bfloat16)
    gate_part = dot_nn(mlp_rows, mlp_in_full[:, :hidden_here])
    up_part = dot_nn(mlp_rows, mlp_in_full[:, hidden_here:])
    grad_product = dot_nn(grad_rows, mlp_out_full)
    bell = 0.5 * (1.0 + lax.erf(gate_part * math.sqrt(0.5)))
    activated = gate_part * bell
    slope = bell + gate_part * jnp.exp(-0.5 * gate_part * gate_part) * (1.0 / math.sqrt(2 * math.pi))
    product_rows = (activated * up_part).astype(jnp.bfloat16)
    grad_gate_up = jnp.concatenate(
        [
            (grad_product * up_part * slope).astype(jnp.bfloat16),
            (grad_product * activated).astype(jnp.bfloat16),
        ],
        axis=1,
    )
    grad_normed_two = collect_all(dot_nt(grad_gate_up, mlp_in_full), rows_here)
    grad_hidden = cotangent_rows + norm_backward(grad_normed_two, gain_two, unit_two, scale_two)
    grad_gain_two = jnp.sum((grad_normed_two * unit_two)[:rows_here], axis=0)
    grad_hidden_rows = grad_hidden.astype(jnp.bfloat16)
    grads_three = attention_backward(
        grad_hidden_rows, rest_pack, queries, key_rows, values,
        cosine_tab, sine_tab, starts, lse,
    )
    mlp_terms = padded(
        [
            dot_tn(mlp_rows, grad_gate_up).astype(jnp.bfloat16),
            dot_tn(grad_rows, product_rows).astype(jnp.bfloat16),
            two_terms(grad_gain_two),
        ]
    )
    mlp_sums = sum_blocks(mlp_terms, grads_three[0])
    branch = collect_own(dot_nt(product_rows, mlp_out_full), rows_here)
    outputs = hidden[:rows_here] + branch

    grad_projected = jnp.concatenate(grads_three, axis=1)
    grad_normed_one = collect_own(dot_nt(grad_projected, qkv_full), rows_here)
    grad_tokens = grad_hidden[:rows_here] + norm_backward(
        grad_normed_one, gain_one, unit_one[:rows_here], scale_one[:rows_here]
    )
    grad_gain_one = jnp.sum(grad_normed_one * unit_one[:rows_here], axis=0)
    attn_terms = padded(
        [
            dot_tn(normed_all, grad_projected).astype(jnp.bfloat16),
            dot_tn(grad_hidden_rows, context).astype(jnp.bfloat16),
            two_terms(grad_gain_one),
        ]
    )
    attn_sums = sum_blocks(attn_terms)

    gain_one_cols = attn_sums[:, 4 * width_here : 4 * width_here + 2].sum(axis=1)
    gain_two_cols = mlp_sums[:, 3 * hidden_here : 3 * hidden_here + 2].sum(axis=1)
    gains = jnp.stack([gain_one_cols, gain_two_cols])
    gains = gains + other_half(gains)
    return (
        outputs,
        grad_tokens,
        attn_sums[:, : 3 * width_here].reshape(model_here, 3, width_here),
        attn_sums[:, 3 * width_here : 4 * width_here].T,
        mlp_sums[:, : 2 * hidden_here].reshape(model_here, 2, hidden_here),
        mlp_sums[:, 2 * hidden_here : 3 * hidden_here].T,
        gains[0],
        gains[1],
    )


def fast_columns(width_here, hidden_here):
    main = hidden_here // LANES * LANES
    pairs = width_here // LANES
    at = {"gains": (0, LANES)}
    place = LANES
    for pair in range(pairs):
        at["pair%d" % pair] = (place, 3 * LANES)
        place += 3 * LANES
    for name, size in (
        ("out", width_here), ("mlp", main + LANES), ("gate", main), ("up", main), ("tail", LANES),
    ):
        at[name] = (place, size)
        place += size
    at["total"] = (0, place)
    return at


def pack_shards(ref, spans):
    height = ref.w_attn_out.shape[0]
    main = spans["gate"][1]
    hidden_here = ref.w_in.shape[1] // 2
    pairs = spans["out"][1] // LANES
    wide = jnp.float32
    down = lax.broadcasted_iota(jnp.int32, (height, height), 0)
    along = lax.broadcasted_iota(jnp.int32, (height, height), 1)
    lane = lax.broadcasted_iota(jnp.int32, (height, LANES), 1)
    gains = jnp.zeros((height, LANES), wide)
    for place, row in enumerate((ref.gain_one, ref.gain_two)):
        column = jnp.sum(jnp.where(down == along, row[...].astype(wide), 0.0), axis=1, keepdims=True)
        gains = jnp.where(lane == place, column, gains)
    pieces = [gains.astype(jnp.bfloat16)]
    for pair in range(pairs):
        for kind in range(3):
            pieces.append(ref.w_qkv[kind, :, pair * LANES : (pair + 1) * LANES])
    tail = jnp.concatenate(
        [ref.w_in[:, main:hidden_here], ref.w_in[:, hidden_here + main :]], axis=1
    )
    mlp = jnp.concatenate(
        [ref.w_mlp_out[...], jnp.zeros((height, main + LANES - hidden_here), jnp.bfloat16)], axis=1
    )
    pieces += [
        ref.w_attn_out[...],
        mlp,
        ref.w_in[:, :main],
        ref.w_in[:, hidden_here : hidden_here + main],
        tail,
    ]
    return pieces


class Links:
    def __init__(self, ref):
        self.ref = ref
        self.dp = lax.axis_index("dp")
        self.core = lax.axis_index("tensor")
        self.x = self.dp % 2
        self.y = (self.dp // 2) % 2
        self.z = self.dp // 4
        plane = self.dp % 4
        self.x_side = self.dp + 1 - 2 * self.x
        self.y_side = self.dp + 2 - 4 * self.y
        self.z_of = [None, self.z + 1 - 2 * (self.z % 2), (self.z + 2) % 4, 3 - self.z]
        self.z_side = [None] + [place * 4 + plane for place in self.z_of[1:]]
        self.started = []

    def enter(self):
        barrier = pltpu.get_barrier_semaphore()
        others = [(self.x_side, self.core), (self.y_side, self.core), (self.dp, 1 - self.core)]
        others += [(place, self.core) for place in self.z_side[1:]]
        for other in others:
            pl.semaphore_signal(
                barrier, inc=1, device_id=other, device_id_type=pl.DeviceIdType.MESH
            )
        pl.semaphore_wait(barrier, len(others))

    def copy(self, source, target, sems, place, device):
        return pltpu.make_async_remote_copy(
            src_ref=source,
            dst_ref=target,
            send_sem=sems[0].at[place],
            recv_sem=sems[1].at[place],
            device_id=device,
            device_id_type=pl.DeviceIdType.MESH,
        )

    def start(self, *copies):
        for copy in copies:
            copy.start()
            self.started.append(copy)

    def to_core(self, source, target, place):
        copy = self.copy(
            source, target, (self.ref.core_out, self.ref.core_in), place, (self.dp, 1 - self.core)
        )
        self.start(copy)
        return copy

    def finish(self):
        for copy in self.started:
            copy.wait_send()
        self.started = []


class Gather(Links):
    def __init__(self, ref, chunks):
        super().__init__(ref)
        self.chunks = chunks
        self.got = {}

    def send_z(self, name):
        chunk = list(self.chunks).index(name)
        cols = pl.ds(*self.chunks[name])
        block = self.ref.full.at[self.z, self.y, self.x, :, cols]
        copies = [
            self.copy(
                block, block, (self.ref.far_out, self.ref.far_in), 3 * chunk + step - 1,
                (self.z_side[step], self.core),
            )
            for step in (1, 2, 3)
        ]
        self.start(*copies)
        self.got[name] = copies

    def arrive(self, name):
        for copy in self.got[name]:
            copy.wait_recv()

    def near(self, name, stage, first, second):
        chunk = list(self.chunks).index(name)
        sems = (self.ref.near_out, self.ref.near_in)
        place = 4 * chunk + 2 * stage
        copies = [
            self.copy(first[0], first[0], sems, place, (first[1], self.core)),
            self.copy(second[0], second[0], sems, place + 1, (second[1], self.core)),
        ]
        self.arrive(name)
        self.start(*copies)
        self.got[name] = copies

    def send_one(self, name):
        cols = pl.ds(*self.chunks[name])
        low, high = pl.ds(0, 2), pl.ds(2, 2)
        full = self.ref.full
        self.near(
            name, 0,
            (full.at[low, self.y, self.x, :, cols], self.x_side),
            (full.at[high, self.y, self.x, :, cols], self.y_side),
        )

    def send_two(self, name):
        cols = pl.ds(*self.chunks[name])
        low, high = pl.ds(0, 2), pl.ds(2, 2)
        both = pl.ds(0, 2)
        full = self.ref.full
        self.near(
            name, 1,
            (full.at[low, self.y, both, :, cols], self.y_side),
            (full.at[high, both, self.x, :, cols], self.x_side),
        )


class Scatter:
    def __init__(self, link, chunks):
        self.link = link
        self.ref = link.ref
        self.chunks = chunks
        self.got = {}

    def send(self, name, stage, moves):
        sems = (self.ref.sum_out, self.ref.sum_in)
        place = 7 * list(self.chunks).index(name) + 2 * stage
        copies = [
            self.link.copy(source, target, sems, place + step, (side, self.link.core))
            for step, (source, target, side) in enumerate(moves)
        ]
        self.link.start(*copies)
        self.got[name] = copies

    def arrive(self, name):
        for copy in self.got[name]:
            copy.wait_recv()

    def parts(self, name):
        held, span, place = self.chunks[name]
        return held, pl.ds(*span), pl.ds(place, span[1])

    def one(self, name):
        link, ref = self.link, self.ref
        held, cols, to = self.parts(name)
        both = pl.ds(0, 2)
        self.send(name, 0, [
            (held.at[pl.ds(0, 2), 1 - link.y, both, :, cols], ref.low_one.at[:, :, :, to], link.y_side),
            (held.at[pl.ds(2, 2), both, 1 - link.x, :, cols], ref.high_one.at[:, :, :, to], link.x_side),
        ])

    def two(self, name):
        link, ref = self.link, self.ref
        held, cols, to = self.parts(name)
        both = pl.ds(0, 2)
        self.arrive(name)
        at = (pl.ds(0, 2), link.y, both, slice(None), cols)
        held[at] = held[at] + ref.low_one[:, :, :, to]
        at = (pl.ds(2, 2), both, link.x, slice(None), cols)
        held[at] = held[at] + ref.high_one[:, :, :, to]
        self.send(name, 1, [
            (held.at[pl.ds(0, 2), link.y, 1 - link.x, :, cols], ref.low_two.at[:, :, to], link.x_side),
            (held.at[pl.ds(2, 2), 1 - link.y, link.x, :, cols], ref.high_two.at[:, :, to], link.y_side),
        ])

    def three(self, name):
        link, ref = self.link, self.ref
        held, cols, to = self.parts(name)
        self.arrive(name)
        at = (pl.ds(0, 2), link.y, link.x, slice(None), cols)
        held[at] = held[at] + ref.low_two[:, :, to]
        at = (pl.ds(2, 2), link.y, link.x, slice(None), cols)
        held[at] = held[at] + ref.high_two[:, :, to]
        self.send(name, 2, [
            (
                held.at[link.z_of[step], link.y, link.x, :, cols],
                ref.far_sum.at[step - 1, :, to],
                link.z_side[step],
            )
            for step in (1, 2, 3)
        ])

    def four(self, name):
        link, ref = self.link, self.ref
        held, cols, to = self.parts(name)
        self.arrive(name)
        total = held[link.z, link.y, link.x, :, cols].astype(jnp.float32)
        for step in range(3):
            total = total + ref.far_sum[step, :, to].astype(jnp.float32)
        return total


def weights_at(full, span):
    block = full[:, :, :, :, span[0] : span[0] + span[1]]
    return block.reshape(-1, span[1])


def row_loop(rows, block):
    def wrap(body):
        @pl.loop(0, rows // block)
        def _(step):
            body(pl.ds(pl.multiple_of(step * block, block), block))

    return wrap


def layer_kernel(names, spans, *refs):
    ref = types.SimpleNamespace(**dict(zip(names, refs)))
    half, width = ref.tok.shape
    rows = 2 * half
    fetch_tok = pltpu.make_async_copy(ref.tokens, ref.tok, ref.fetch.at[0])
    fetch_cot = pltpu.make_async_copy(ref.cotangent, ref.cot, ref.fetch.at[1])
    fetch_tok.start()
    fetch_cot.start()
    pairs = (spans["out"][1]) // LANES
    main = spans["gate"][1]
    chunk_names = ["gains"] + ["pair%d" % pair for pair in range(pairs)] + ["out", "mlp"]
    chunks = {name: spans[name] for name in chunk_names}
    chunks["gate"] = spans["gate"]
    chunks["up"] = (spans["up"][0], main + LANES)
    link = Gather(ref, chunks)
    core = link.core
    own = pl.ds(pl.multiple_of(core * half, half), half)
    own_at = core * half
    other_at = (1 - core) * half
    part = 256

    ref.grad_low = ref.normed
    ref.grad_context = ref.product.at[:, : pairs * LANES]
    ref.grad_three = ref.product.at[:, : 3 * LANES]
    ref.grad_projected = ref.grad_gate_up
    ref.acc = ref.grad_product.at[:, : 3 * LANES]
    scatter = Scatter(
        link,
        {
            "inner": (ref.grad_inner, (0, 2 * main + LANES), spans["gate"][0]),
            "mlp": (ref.full, spans["mlp"], spans["mlp"][0]),
            "out": (ref.full, spans["out"], spans["out"][0]),
            **{
                "pair%d" % pair: (
                    ref.full,
                    (spans["gate"][0] + 3 * LANES * pair, 3 * LANES),
                    spans["pair%d" % pair][0],
                )
                for pair in range(pairs)
            },
            "gains": (ref.full, spans["gains"], spans["gains"][0]),
        },
    )

    place = 0
    for piece in pack_shards(ref, spans):
        wide = piece.shape[1]
        ref.full[link.z, link.y, link.x, :, place : place + wide] = piece
        place += wide
    link.enter()
    link.send_z("gains")
    link.send_z("pair0")
    link.send_z("pair1")

    fetch_tok.wait()

    @row_loop(half, 128)
    def _(at):
        unit, scale = norm_parts(ref.tok[at, :])
        ref.unit_one[at, :] = unit
        ref.scale_one[at, :] = jnp.broadcast_to(scale, (128, LANES))

    link.send_one("gains")

    shift = jnp.int32(0)
    for slot in range(ref.offsets.shape[1]):
        entry = ref.offsets[0, slot]
        shift = jnp.maximum(shift, jnp.where(entry <= half - 1, entry, 0))

    def source_of(place):
        moved = place + shift
        return jnp.where(moved >= rows, moved - rows, moved)

    def start_of(place):
        start = jnp.zeros_like(place)
        for slot in range(ref.offsets.shape[1]):
            entry = ref.offsets[0, slot]
            start = jnp.maximum(start, jnp.where(place >= entry, entry, 0))
        return start

    @row_loop(rows, part)
    def _(at):
        down = source_of(lax.broadcasted_iota(jnp.int32, (part, 1), 0) + at.start)
        along = lax.broadcasted_iota(jnp.int32, (part, rows), 1)
        ref.perm[at, :] = jnp.where(down == along, 1.0, 0.0).astype(jnp.bfloat16)
        down = lax.broadcasted_iota(jnp.int32, (part, rows), 0) + at.start
        along = source_of(lax.broadcasted_iota(jnp.int32, (1, rows), 1))
        ref.perm_back[at, :] = jnp.where(down == along, 1.0, 0.0).astype(jnp.bfloat16)

    link.send_two("gains")
    link.send_one("pair0")
    link.send_z("pair2")

    fetch_cot.wait()

    @row_loop(half, 128)
    def _(at):
        here = pl.ds(pl.multiple_of(own_at + at.start, 128), 128)
        ref.grad_rows[here, :] = ref.cot[at, :].astype(jnp.bfloat16)

    def table(at):
        place = source_of(lax.broadcasted_iota(jnp.int32, (part, LANES), 0) + at.start)
        start = start_of(place)
        angle = (place - start).astype(jnp.float32) * ref.inverse[...]
        lane = lax.broadcasted_iota(jnp.int32, (part, LANES), 1)
        sine = jnp.sin(angle)
        ref.cosine[at, :] = jnp.cos(angle)
        ref.sine[at, :] = jnp.where(lane % HEAD_DIM < HEAD_DIM // 2, -sine, sine)

    row_loop(half, part)(table)
    link.arrive("gains")
    slot = lax.broadcasted_iota(jnp.int32, (8, LANES), 0)
    lane = lax.broadcasted_iota(jnp.int32, (8, LANES), 1)
    pick = jnp.where(slot == lane, 1.0, 0.0).astype(jnp.bfloat16)
    ref.gain[...] = dot_nt(pick, weights_at(ref.full, spans["gains"]))

    @row_loop(half, 128)
    def _(at):
        here = pl.ds(pl.multiple_of(own_at + at.start, 128), 128)
        ref.normed[here, :] = (ref.unit_one[at, :] * ref.gain[0:1, :]).astype(jnp.bfloat16)

    got_normed = link.to_core(ref.normed.at[own, :], ref.normed.at[own, :], 1)
    got_grad = link.to_core(ref.grad_rows.at[own, :], ref.grad_rows.at[own, :], 0)
    link.send_one("pair1")
    link.send_z("out")

    @row_loop(half, part)
    def _(at):
        table(pl.ds(pl.multiple_of(half + at.start, part), part))

    key_start = start_of(source_of(lax.broadcasted_iota(jnp.int32, (half, 1), 0) + half))
    query_start = start_of(source_of(lax.broadcasted_iota(jnp.int32, (1, half), 1) + half))
    ref.bias[...] = jnp.where(key_start == query_start, 0.0, NEGATIVE)
    got_normed.wait_recv()
    link.send_two("pair0")

    @row_loop(rows, part)
    def _(at):
        ref.rolled[at, :] = dot_nn(ref.perm[at, :], ref.normed[...]).astype(jnp.bfloat16)

    link.send_one("pair2")
    link.send_z("mlp")

    def project(pair):
        if pair:
            link.arrive("pair%d" % pair)
        cols = slice(pair * LANES, (pair + 1) * LANES)

        @row_loop(rows, part)
        def _(at):
            three = dot_nn(ref.rolled[at, :], weights_at(ref.full, spans["pair%d" % pair]))
            lane = lax.broadcasted_iota(jnp.int32, (part, LANES), 1)
            cosine, sine = ref.cosine[at, :], ref.sine[at, :]
            query = turn(three[:, :LANES], cosine, sine, lane) * SCALE
            ref.queries[at, cols] = query.astype(jnp.bfloat16)
            ref.keys[at, cols] = turn(
                three[:, LANES : 2 * LANES], cosine, sine, lane
            ).astype(jnp.bfloat16)
            ref.values[at, cols] = three[:, 2 * LANES :].astype(jnp.bfloat16)
            ref.values_t[:, at] = three[:, 2 * LANES :].T.astype(jnp.bfloat16)

    def unit_of(pair, head, first):
        return (pair * (LANES // HEAD_DIM) + head) * 2 + (0 if first else 1)

    def attend(pair, first):
        cols = slice(pair * LANES, (pair + 1) * LANES)
        base = 0 if first else half

        for step in range(half // part):
            at = pl.ds(base + step * part, part)
            query_pair = ref.queries[at, cols]
            lane = lax.broadcasted_iota(jnp.int32, (part, LANES), 1)
            parts = []
            for head in range(LANES // HEAD_DIM):
                query = jnp.where(lane // HEAD_DIM == head, query_pair, 0)
                scores = dot_nt(ref.keys[base : base + half, cols], query)
                if not first:
                    scores = scores + ref.bias[:, step * part : (step + 1) * part]
                top = jnp.max(scores, axis=0, keepdims=True)
                terms = jnp.exp(scores - top)
                total = jnp.sum(terms, axis=0, keepdims=True)
                probs = (terms * (1.0 / total)).astype(jnp.bfloat16)
                ref.probs[
                    unit_of(pair, head, first), :, step * part : (step + 1) * part
                ] = probs
                parts.append(
                    dot_nn(
                        ref.values_t[head * HEAD_DIM : (head + 1) * HEAD_DIM, base : base + half],
                        probs,
                    )
                )
            ref.context_rolled[at, cols] = jnp.concatenate(parts, axis=0).T.astype(jnp.bfloat16)

    link.arrive("pair0")
    link.send_two("pair1")
    link.send_z("gate")
    project(0)
    link.send_one("out")
    attend(0, True)
    link.send_two("pair2")
    link.send_z("up")
    attend(0, False)
    link.send_one("mlp")
    project(1)
    link.send_two("out")
    attend(1, True)
    link.send_one("gate")
    attend(1, False)
    link.send_two("mlp")
    project(2)
    link.send_one("up")
    attend(2, True)
    link.send_two("gate")
    attend(2, False)

    @row_loop(rows, part)
    def _(at):
        ref.context[at, :] = dot_nn(ref.perm_back[at, :], ref.context_rolled[...]).astype(jnp.bfloat16)

    link.send_two("up")
    link.arrive("out")

    def pair_sum(product, place, sem, keep):
        @row_loop(half, part)
        def _(at):
            there = pl.ds(pl.multiple_of(other_at + at.start, part), part)
            ref.sent[place, at, :] = product(there).astype(jnp.bfloat16)

        got = link.to_core(ref.sent.at[place], ref.taken.at[place], sem)

        @row_loop(half, part)
        def _(at):
            here = pl.ds(pl.multiple_of(own_at + at.start, part), part)
            keep[at, :] = product(here)

        return got

    got_attended = pair_sum(
        lambda at: dot_nt(ref.context[at, :], weights_at(ref.full, spans["out"])), 0, 2, ref.hidden
    )
    got_attended.wait_recv()

    @row_loop(half, 128)
    def _(at):
        hidden = ref.tok[at, :] + ref.hidden[at, :] + ref.taken[0, at, :].astype(jnp.float32)
        ref.hidden[at, :] = hidden
        unit, scale = norm_parts(hidden)
        ref.unit_two[at, :] = unit
        ref.scale_two[at, :] = jnp.broadcast_to(scale, (128, LANES))
        here = pl.ds(pl.multiple_of(own_at + at.start, 128), 128)
        ref.normed_mlp[here, :] = (unit * ref.gain[1:2, :]).astype(jnp.bfloat16)

    got_mlp = link.to_core(ref.normed_mlp.at[own, :], ref.normed_mlp.at[own, :], 6)
    got_grad.wait_recv()
    link.arrive("mlp")

    @row_loop(rows, part)
    def _(at):
        ref.grad_product[at, :] = dot_nn(ref.grad_rows[at, :], weights_at(ref.full, spans["mlp"]))

    got_mlp.wait_recv()
    link.arrive("gate")
    link.arrive("up")

    def gated(gate, up, grad):
        bell = 0.5 * (1.0 + lax.erf(gate * math.sqrt(0.5)))
        activated = gate * bell
        slope = bell + gate * jnp.exp(-0.5 * gate * gate) * (1.0 / math.sqrt(2 * math.pi))
        return activated * up, grad * up * slope, grad * activated

    @row_loop(rows, part)
    def _(at):
        low = ref.normed_mlp[at, :]
        gate = dot_nn(low, weights_at(ref.full, spans["gate"]))
        up = dot_nn(low, weights_at(ref.full, spans["up"]))
        product, grad_gate, grad_up = gated(gate, up, ref.grad_product[at, :main])
        ref.product[at, :main] = product.astype(jnp.bfloat16)
        ref.grad_gate_up[at, :main] = grad_gate.astype(jnp.bfloat16)
        ref.grad_gate_up[at, main : 2 * main] = grad_up.astype(jnp.bfloat16)
        tail = dot_nn(low, weights_at(ref.full, spans["tail"]))
        product, grad_gate, grad_up = gated(
            tail, pltpu.roll(tail, LANES // 2, axis=1), ref.grad_product[at, main:]
        )
        lane = lax.broadcasted_iota(jnp.int32, (part, LANES), 1)
        lower = lane < LANES // 2
        ref.product[at, main:] = jnp.where(lower, product, 0.0).astype(jnp.bfloat16)
        ref.grad_gate_up[at, 2 * main :] = jnp.where(
            lower, grad_gate, pltpu.roll(grad_up, LANES // 2, axis=1)
        ).astype(jnp.bfloat16)

    inner = (spans["gate"][0], 2 * main + LANES)
    link.finish()

    def weight_grad(left, right, held, first):
        wide = right.shape[1]

        @pl.loop(0, 2)
        def _(step):
            cols = pl.ds(pl.multiple_of(step * (width // 2), LANES), width // 2)
            block = dot_tn(left[:, cols], right[...]).astype(jnp.bfloat16)
            held[pl.ds(2 * step, 2), :, :, :, first : first + wide] = block.reshape(
                2, 2, 2, width // 16, wide
            )

    weight_grad(ref.normed_mlp, ref.grad_gate_up, ref.grad_inner, 0)
    scatter.one("inner")
    got_normed_two = pair_sum(
        lambda at: dot_nt(ref.grad_gate_up[at, :], weights_at(ref.full, inner)), 1, 3, ref.grad_hidden
    )
    got_branch = pair_sum(
        lambda at: dot_nt(ref.product[at, :], weights_at(ref.full, spans["mlp"])), 2, 4, ref.outputs
    )
    got_normed_two.wait_recv()
    ref.gain_rows[...] = jnp.zeros_like(ref.gain_rows)

    @row_loop(half, 128)
    def _(at):
        incoming = ref.grad_hidden[at, :] + ref.taken[1, at, :].astype(jnp.float32)
        unit = ref.unit_two[at, :]
        ref.gain_rows[1:2, :] += jnp.sum(incoming * unit, axis=0, keepdims=True)
        grad = ref.cot[at, :] + norm_backward(
            incoming, ref.gain[1:2, :], unit, ref.scale_two[at, 0:1]
        )
        ref.grad_hidden[at, :] = grad
        here = pl.ds(pl.multiple_of(own_at + at.start, 128), 128)
        ref.grad_low[here, :] = grad.astype(jnp.bfloat16)

    got_low = link.to_core(ref.grad_low.at[own, :], ref.grad_low.at[own, :], 7)
    weight_grad(ref.grad_rows, ref.product, ref.full, spans["mlp"][0])
    scatter.one("mlp")
    got_branch.wait_recv()

    @row_loop(half, 128)
    def _(at):
        ref.outputs[at, :] = (
            ref.outputs[at, :] + ref.hidden[at, :] + ref.taken[2, at, :].astype(jnp.float32)
        )

    got_low.wait_recv()

    @row_loop(rows, part)
    def _(at):
        ref.grad_context[at, :] = dot_nn(
            ref.grad_low[at, :], weights_at(ref.full, spans["out"])
        ).astype(jnp.bfloat16)

    @row_loop(rows, part)
    def _(at):
        ref.grad_rolled[at, :] = dot_nn(ref.perm[at, :], ref.grad_context[...]).astype(jnp.bfloat16)

    weight_grad(ref.grad_low, ref.context, ref.full, spans["out"][0])
    scatter.one("out")
    scatter.two("inner")

    def settle(name):
        total = scatter.four(name)
        hidden_here = ref.grad_mlp_out.shape[1]
        short = hidden_here - main
        if name == "inner":
            ref.grad_gate[:, :main] = total[:, :main]
            ref.grad_gate[:, main:] = total[:, 2 * main : 2 * main + short]
            ref.grad_up[:, :main] = total[:, main : 2 * main]
            ref.grad_up[:, main:] = total[:, 2 * main + short :]
        elif name == "mlp":
            ref.grad_mlp_out[...] = total[:, :hidden_here]
        elif name == "out":
            ref.grad_attn_out[...] = total
        elif name == "gains":
            turned = total.T
            ref.gains[...] = turned[0:2, :] + turned[8:10, :]
        else:
            pair = int(name[4:])
            for kind in range(3):
                ref.grad_qkv[kind, :, pair * LANES : (pair + 1) * LANES] = total[
                    :, kind * LANES : (kind + 1) * LANES
                ]

    def pull(pair, first):
        cols = slice(pair * LANES, (pair + 1) * LANES)
        base = 0 if first else half
        span = slice(base, base + half)

        @row_loop(half, part)
        def _(at):
            at = pl.ds(pl.multiple_of(base + at.start, part), part)
            ref.keys_t[:, at] = ref.keys[at, cols].astype(jnp.float32).T.astype(jnp.bfloat16)

        for step in range(half // part):
            at = pl.ds(base + step * part, part)
            lane = lax.broadcasted_iota(jnp.int32, (part, LANES), 1)
            query_pair = ref.queries[at, cols]
            grad_pair = ref.grad_rolled[at, cols]
            product = grad_pair.astype(jnp.float32) * ref.context_rolled[at, cols].astype(jnp.float32)
            product = product.T
            parts, all_probs, all_grads, all_queries, all_pulls = [], [], [], [], []
            for head in range(LANES // HEAD_DIM):
                query = jnp.where(lane // HEAD_DIM == head, query_pair, 0)
                grad = jnp.where(lane // HEAD_DIM == head, grad_pair, 0)
                probs = ref.probs[
                    unit_of(pair, head, first), :, step * part : (step + 1) * part
                ]
                grad_probs = dot_nt(ref.values[span, cols], grad)
                drop = jnp.sum(
                    product[head * HEAD_DIM : (head + 1) * HEAD_DIM], axis=0, keepdims=True
                )
                pulled = (probs.astype(jnp.float32) * (grad_probs - drop)).astype(jnp.bfloat16)
                all_probs.append(probs)
                all_grads.append(grad)
                all_queries.append(query)
                all_pulls.append(pulled)
                parts.append(
                    dot_nn(ref.keys_t[head * HEAD_DIM : (head + 1) * HEAD_DIM, span], pulled)
                )
            grad_values = dot_nn(
                jnp.concatenate(all_probs, axis=1), jnp.concatenate(all_grads, axis=0)
            )
            grad_keys = dot_nn(
                jnp.concatenate(all_pulls, axis=1), jnp.concatenate(all_queries, axis=0)
            )

            if step == 0:
                ref.acc[span, LANES : 2 * LANES] = grad_keys
                ref.acc[span, 2 * LANES :] = grad_values
            else:
                ref.acc[span, LANES : 2 * LANES] += grad_keys
                ref.acc[span, 2 * LANES :] += grad_values

            ref.acc[at, :LANES] = jnp.concatenate(parts, axis=0).T

    def unproject(pair):
        first = 3 * LANES * pair

        @row_loop(rows, part)
        def _(at):
            lane = lax.broadcasted_iota(jnp.int32, (part, LANES), 1)
            cosine, sine = ref.cosine[at, :], -ref.sine[at, :]
            grad_query = turn(ref.acc[at, :LANES], cosine, sine, lane) * SCALE
            grad_key = turn(ref.acc[at, LANES : 2 * LANES], cosine, sine, lane)
            ref.grad_three[at, :LANES] = grad_query.astype(jnp.bfloat16)
            ref.grad_three[at, LANES : 2 * LANES] = grad_key.astype(jnp.bfloat16)
            ref.grad_three[at, 2 * LANES :] = ref.acc[at, 2 * LANES :].astype(jnp.bfloat16)

        weight_grad(ref.rolled, ref.grad_three, ref.full, spans["gate"][0] + first)
        scatter.one("pair%d" % pair)

        @row_loop(rows, part)
        def _(at):
            ref.grad_projected[at, first : first + 3 * LANES] = dot_nn(
                ref.perm_back[at, :], ref.grad_three[...]
            ).astype(jnp.bfloat16)

    pull(0, True)
    scatter.two("mlp")
    pull(0, False)
    unproject(0)
    scatter.three("inner")
    pull(1, True)
    scatter.two("out")
    pull(1, False)
    scatter.three("mlp")
    unproject(1)
    pull(2, True)
    scatter.two("pair0")
    scatter.three("out")
    settle("inner")
    pull(2, False)
    unproject(2)
    scatter.three("pair0")
    scatter.two("pair1")
    qkv_span = (spans["pair0"][0], 3 * pairs * LANES)
    got_one = pair_sum(
        lambda at: dot_nt(ref.grad_projected[at, :], weights_at(ref.full, qkv_span)),
        0, 5, ref.grad_tokens,
    )
    scatter.three("pair1")
    got_one.wait_recv()

    @row_loop(half, 128)
    def _(at):
        incoming = ref.grad_tokens[at, :] + ref.taken[0, at, :].astype(jnp.float32)
        ref.grad_tokens[at, :] = incoming
        ref.gain_rows[0:1, :] += jnp.sum(incoming * ref.unit_one[at, :], axis=0, keepdims=True)

    got_gain = link.to_core(ref.gain_rows, ref.gain_other, 8)
    scatter.two("pair2")

    @row_loop(half, 128)
    def _(at):
        ref.grad_tokens[at, :] = ref.grad_hidden[at, :] + norm_backward(
            ref.grad_tokens[at, :], ref.gain[0:1, :], ref.unit_one[at, :], ref.scale_one[at, 0:1]
        )

    got_gain.wait_recv()
    gain_rows = ref.gain_rows[...] + ref.gain_other[...]
    high = gain_rows.astype(jnp.bfloat16)
    rest = (gain_rows - high.astype(jnp.float32)).astype(jnp.bfloat16)
    slot = lax.broadcasted_iota(jnp.int32, (16, LANES), 0)
    lane = lax.broadcasted_iota(jnp.int32, (16, LANES), 1)
    pick = jnp.where(slot == lane, 1.0, 0.0).astype(jnp.bfloat16)
    columns = dot_tn(jnp.concatenate([high, rest], axis=0), pick).astype(jnp.bfloat16)
    ref.full[:, :, :, :, 0:LANES] = columns.reshape(4, 2, 2, width // 16, LANES)
    scatter.one("gains")
    scatter.three("pair2")
    settle("out")
    settle("mlp")
    scatter.two("gains")
    settle("pair0")
    scatter.three("gains")
    settle("pair1")
    settle("pair2")
    settle("gains")
    link.finish()


def call_layer(shards_here, tokens, cotangent, offsets, spans):
    half, width = tokens.shape
    rows = 2 * half
    height = shards_here["w_attn_out"].shape[0]
    total = spans["total"][1]
    width_here = spans["out"][1]
    hidden_here = shards_here["w_mlp_out"].shape[1]
    pairs = width_here // LANES
    main = spans["gate"][1]
    half_dim = HEAD_DIM // 2
    inverse = np.power(ROPE_BASE, -2.0 * np.arange(half_dim) / HEAD_DIM).astype(np.float32)
    inverse = jnp.asarray(np.tile(inverse, LANES // half_dim)[None, :])
    low, wide = jnp.bfloat16, jnp.float32
    outs = dict(
        outputs=((half, width), wide),
        grad_tokens=((half, width), wide),
        grad_qkv=((3, height, width_here), wide),
        grad_attn_out=((height, width_here), wide),
        grad_gate=((height, hidden_here), wide),
        grad_up=((height, hidden_here), wide),
        grad_mlp_out=((height, hidden_here), wide),
        gains=((2, height), wide),
    )
    chunk_count = 1 + pairs + 4
    kept = dict(
        full=((4, 2, 2, height, total), low),
        grad_inner=((4, 2, 2, height, 2 * main + LANES), low),
        low_one=((2, 2, height, total), low),
        high_one=((2, 2, height, total), low),
        low_two=((2, height, total), low),
        high_two=((2, height, total), low),
        far_sum=((3, height, total), low),
        normed=((rows, width), low),
        rolled=((rows, width), low),
        grad_rows=((rows, width), low),
        normed_mlp=((rows, width), low),
        perm=((rows, rows), low),
        perm_back=((rows, rows), low),
        bias=((half, half), wide),
        values_t=((LANES, rows), low),
        keys_t=((LANES, rows), low),
        queries=((rows, width_here), low),
        keys=((rows, width_here), low),
        values=((rows, width_here), low),
        context=((rows, width_here), low),
        context_rolled=((rows, width_here), low),
        probs=((2 * width_here // HEAD_DIM, half, half), low),
        grad_rolled=((rows, width_here), low),
        product=((rows, main + LANES), low),
        grad_gate_up=((rows, 2 * main + LANES), low),
        grad_product=((rows, main + LANES), wide),
        sent=((3, half, width), low),
        taken=((3, half, width), low),
        hidden=((half, width), wide),
        grad_hidden=((half, width), wide),
        unit_one=((half, width), wide),
        unit_two=((half, width), wide),
        scale_one=((half, LANES), wide),
        scale_two=((half, LANES), wide),
        cosine=((rows, LANES), wide),
        sine=((rows, LANES), wide),
        gain=((8, width), wide),
        gain_rows=((8, width), wide),
        gain_other=((8, width), wide),
    )
    kept.update(tok=((half, width), wide), cot=((half, width), wide))
    scratch = {name: pltpu.VMEM(*entry) for name, entry in kept.items()}
    scratch["fetch"] = pltpu.SemaphoreType.DMA((2,))
    for name, count in (
        ("far", 3 * chunk_count), ("near", 4 * chunk_count), ("core", 9), ("sum", 7 * (pairs + 4)),
    ):
        scratch[name + "_out"] = pltpu.SemaphoreType.DMA((count,))
        scratch[name + "_in"] = pltpu.SemaphoreType.DMA((count,))
    names = ["offsets", "tokens", "cotangent", "inverse"] + list(shards_here) + list(outs) + list(scratch)
    vmem = pl.BlockSpec(memory_space=pltpu.VMEM)
    results = pl.pallas_call(
        functools.partial(layer_kernel, names, spans),
        out_shape=[jax.ShapeDtypeStruct(*entry) for entry in outs.values()],
        in_specs=[pl.BlockSpec(memory_space=pltpu.SMEM)] + [pl.BlockSpec(memory_space=pl.ANY)] * 2 + [vmem] * (1 + len(shards_here)),
        out_specs=[vmem] * len(outs),
        scratch_shapes=list(scratch.values()),
        compiler_params=pltpu.CompilerParams(
            collective_id=0, has_side_effects=True, vmem_limit_bytes=63 * 1024 * 1024
        ),
        cost_estimate=pl.CostEstimate(
            flops=12 * 10**9, bytes_accessed=30 * 10**6, transcendentals=10**7
        ),
    )(offsets, tokens, cotangent, inverse, *shards_here.values())
    return types.SimpleNamespace(**dict(zip(outs, results)))


def fast_shards(tokens, offsets, w_qkv, w_attn_out, w_in, w_mlp_out, gain_attn, gain_mlp, cotangent):
    half = tokens.shape[0]
    height, _, width_here = w_qkv.shape
    hidden_here = w_in.shape[2]
    spans = fast_columns(width_here, hidden_here)
    shards_here = dict(
        w_qkv=w_qkv.transpose(1, 0, 2),
        w_attn_out=w_attn_out.T,
        w_in=w_in.reshape(height, -1),
        w_mlp_out=w_mlp_out.T,
        gain_one=gain_attn[None, :],
        gain_two=gain_mlp[None, :],
    )
    f = call_layer(shards_here, tokens, cotangent, offsets, spans)
    return (
        f.outputs,
        f.grad_tokens,
        f.grad_qkv.transpose(1, 0, 2),
        f.grad_attn_out.T,
        jnp.stack([f.grad_gate, f.grad_up], axis=1),
        f.grad_mlp_out.T,
        f.gains[0],
        f.gains[1],
    )


def solution(mesh):
    in_specs = (
        P(("dp", "tensor"), None),
        P("dp", None),
        P("dp", None, "tensor"),
        P("tensor", "dp"),
        P("dp", None, "tensor"),
        P("tensor", "dp"),
        P("dp"),
        P("dp"),
        P(("dp", "tensor"), None),
    )
    out_specs = (
        P(("dp", "tensor"), None),
        P(("dp", "tensor"), None),
        P("dp", None, "tensor"),
        P("tensor", "dp"),
        P("dp", None, "tensor"),
        P("tensor", "dp"),
        P("dp"),
        P("dp"),
    )
    sizes = dict(mesh.shape)
    body = fast_shards if (sizes["dp"], sizes["tensor"]) == (16, 2) else shards
    return jax.shard_map(body, mesh=mesh, in_specs=in_specs, out_specs=out_specs, check_vma=False)
```
